32 devices in a mesh: blk: 16 (over z, y, core), rows: 2 (over x).
Axes of the slice: x: 2, y: 2, z: 4, core: 2. Of those that a mesh axis runs over, the one named last changes fastest.
Arguments:
- matrix: bfloat16 [12288, 6144], P('rows', 'blk'), may hold values from -128 to 128
- plan: int32 [32], replicated, may hold values from 0 to 31, as said below
Outputs:
- next_matrix: bfloat16 [12288, 6144], P('rows', 'blk')
- off_ratio: float32 [], replicated
The draws below stay inside these ranges and needn't reach their ends.
Inputs may be any that keep to these rules, and one draw needn't show every extreme that they name: `plan`: A permutation of the block numbers. Blocks 2 i and 2 i + 1 form pair i; of these two, one moves into a block of pair i + 1 and the other into a block of pair i - 1, counted around the closed cycle of pairs.
All inputs are finite; a program needn't handle non-finite values.
Results may differ from the reference program's by a relative error of at most 0.0027.
The reference program's roundings to bfloat16 on the way count: a program that leaves them out, or rounds other values in their place, can miss the bound.
Values may be sent and summed in bfloat16 or wider, within the bound.
No kernel may reach another device: no remote copies, remote signals or barrier semaphores. Data moves between devices by JAX's collectives and lax.ppermute only.
A program may use at most 64 MiB of HBM per device.

```python
import math
import jax
import jax.numpy as jnp
import numpy as np
from jax import lax

BW = 192
ROUNDS = 24
ROWS_ALL = 12288
COLS = 6144
N_BLK = 16


def draw_matrix(key, part):
    key = jax.random.fold_in(key, 11)
    key_base, key_rows, key_cols = jax.random.split(key, 3)
    base = jnp.clip(jax.random.normal(key_base, (ROWS_ALL, COLS), jnp.float32), -4.0, 4.0)
    mixed = base + 0.7 * jnp.roll(base, -1, axis=1)
    row_scale = jnp.exp(jax.random.uniform(key_rows, (ROWS_ALL, 1), jnp.float32, 0.0, math.log(10.0)))
    rising = jnp.exp(0.25 * math.log(3.0) * jnp.arange(COLS, dtype=jnp.float32) / COLS)
    col_scale = jnp.exp(jax.random.uniform(key_cols, (1, COLS), jnp.float32, 0.0, math.log(10.0))) * rising[None, :]
    return (0.1 * mixed * row_scale * col_scale).astype(jnp.bfloat16)


def draw_plan(key, part):
    key = jax.random.fold_in(key, 23)
    key_side, key_slot = jax.random.split(key, 2)
    cycle_size = N_BLK
    sides = jax.random.randint(key_side, (cycle_size,), 0, 2, dtype=jnp.int32)
    slots = jax.random.randint(key_slot, (cycle_size,), 0, 2, dtype=jnp.int32)
    devices = jnp.arange(cycle_size, dtype=jnp.int32)
    next_dev = (devices + 1) % cycle_size
    prev_dev = (devices + cycle_size - 1) % cycle_size
    going_right = 2 * next_dev + slots[next_dev]
    going_left = 2 * prev_dev + 1 - slots[prev_dev]
    result = jnp.zeros((2 * cycle_size,), jnp.int32)
    result = result.at[2 * devices + sides].set(going_right)
    result = result.at[2 * devices + 1 - sides].set(going_left)
    return result


def setup_inputs(seed: int = 0) -> dict:
    key_of = jax.random.split(jax.random.key(seed), 3)
    matrix = draw_matrix(jax.random.fold_in(key_of[2], 71), 0)
    plan = draw_plan(jax.random.fold_in(key_of[2], 71), 0)
    return dict(matrix=matrix, plan=plan)


def pair_tables(size, rounds):
    others = np.arange(1, size)
    leads = []
    tails = []
    restores = []
    for turn_index in range(rounds):
        arranged = np.concatenate([np.zeros(1, np.int64), np.roll(others, turn_index % (size - 1))])
        lead_idx = arranged[:size // 2]
        tail_idx = arranged[::-1][:size // 2]
        ordering = np.concatenate([lead_idx, tail_idx])
        leads.append(lead_idx)
        tails.append(tail_idx)
        restores.append(np.argsort(ordering))
    return (jnp.asarray(np.stack(leads), dtype=jnp.int32), jnp.asarray(np.stack(tails), dtype=jnp.int32), jnp.asarray(np.stack(restores), dtype=jnp.int32))

def rotate_columns(values, lead_idx, tail_idx, restore, cosine, sine_val):
    lead_cols = values[:, lead_idx]
    tail_cols = values[:, tail_idx]
    joined = jnp.concatenate([lead_cols * cosine + tail_cols * sine_val, tail_cols * cosine - lead_cols * sine_val], axis=1)
    return joined[:, restore]

def jacobi(gram_sum):
    size = gram_sum.shape[0]
    leads, tails, restores = pair_tables(size, ROUNDS)

    def rotate_once(turn_index, carry):
        gram_now, basis = carry
        lead_idx = leads[turn_index]
        tail_idx = tails[turn_index]
        restore = restores[turn_index]
        diagonal = jnp.diagonal(gram_now)
        head_diag = diagonal[lead_idx]
        tail_diag = diagonal[tail_idx]
        coupling = gram_now[lead_idx, tail_idx]
        difference = head_diag - tail_diag
        sign_val = jnp.where(difference >= 0.0, 1.0, -1.0).astype(gram_now.dtype)
        angle = 0.5 * jnp.arctan2(2.0 * coupling * sign_val, jnp.abs(difference))
        cosine = jnp.cos(angle)
        sine_val = jnp.sin(angle)
        gram_now = rotate_columns(gram_now, lead_idx, tail_idx, restore, cosine, sine_val)
        gram_now = rotate_columns(gram_now.T, lead_idx, tail_idx, restore, cosine, sine_val).T
        basis = rotate_columns(basis, lead_idx, tail_idx, restore, cosine, sine_val)
        return (gram_now, basis)
    start = (gram_sum, jnp.eye(size, dtype=jnp.float32))
    return lax.fori_loop(0, ROUNDS, rotate_once, start)[1]

def reference(matrix, plan):
    block_width = BW
    pair_count = matrix.shape[1] // (2 * block_width)
    row_count = matrix.shape[0]

    def one_pair(pair_index):
        pair_cols = lax.dynamic_slice_in_dim(matrix, pair_index * 2 * block_width, 2 * block_width, 1)
        gram_sum = lax.dot_general(pair_cols, pair_cols, (((0,), (0,)), ((), ())), preferred_element_type=jnp.float32)
        diag_sq = jnp.sum(jnp.diagonal(gram_sum) ** 2)
        off_sq = jnp.sum(gram_sum * gram_sum) - diag_sq
        rotation = jacobi(gram_sum).astype(jnp.bfloat16)
        rotated = jnp.dot(pair_cols, rotation, preferred_element_type=jnp.float32).astype(jnp.bfloat16)
        return (rotated, off_sq, diag_sq)
    rotated, off_terms, diag_terms = lax.map(one_pair, jnp.arange(pair_count, dtype=jnp.int32))
    blocks = rotated.reshape(pair_count, row_count, 2, block_width).transpose(0, 2, 1, 3)
    blocks = blocks.reshape(2 * pair_count, row_count, block_width)
    placed = jnp.zeros_like(blocks).at[plan].set(blocks)
    next_matrix = placed.transpose(1, 0, 2).reshape(row_count, 2 * pair_count * block_width)
    off_ratio = jnp.sqrt(jnp.sum(off_terms) / jnp.sum(diag_terms))
    return (next_matrix, off_ratio)
```

```python
import jax
import jax.numpy as jnp
from jax import lax
from jax.experimental import pallas as pl
from jax.experimental.pallas import tpu as pltpu
from jax.sharding import PartitionSpec as P

ROUNDS = 24
LANES = 128
SUBS = 8


def split_three(values):
    high = values.astype(jnp.bfloat16)
    rest = values - high.astype(jnp.float32)
    middle = rest.astype(jnp.bfloat16)
    low = (rest - middle.astype(jnp.float32)).astype(jnp.bfloat16)
    return high, middle, low


def dot32(left, right, dims=((1,), (0,))):
    return lax.dot_general(left, right, (dims, ((), ())), preferred_element_type=jnp.float32)


def slot_of_row(rows, groups, half):
    part = rows // half
    inside = rows % half
    index = (inside % SUBS) * groups + inside // SUBS
    return jnp.where(part == 0, index, 2 * half - 1 - index)


def slot_of_lane(lanes, half):
    part = lanes // (2 * LANES)
    odd = (lanes // LANES) % 2
    inside = lanes % LANES
    index = 2 * inside + odd
    slot = jnp.where(part == 0, index, 2 * half - 1 - index)
    return jnp.where(inside < half // 2, slot, -1)


def onehot(left, right):
    return jnp.where(left == right, 1.0, 0.0).astype(jnp.bfloat16)


def angles(head, tail, coupling):
    difference = head - tail
    sign_val = jnp.where(difference >= 0.0, 1.0, -1.0)
    across = 2.0 * coupling * sign_val
    along = jnp.abs(difference)
    scale = jnp.maximum(along, jnp.abs(across))
    empty = scale == 0.0
    inverse = 1.0 / jnp.where(empty, 1.0, scale)
    along = jnp.where(empty, 1.0, along * inverse)
    across = across * inverse
    square = along * along + across * across
    root = lax.rsqrt(square)
    root = root * (1.5 - 0.5 * square * root * root)
    cos_sq = 0.5 + 0.5 * (along * root)
    half_root = lax.rsqrt(cos_sq)
    half_root = half_root * (1.5 - 0.5 * cos_sq * half_root * half_root)
    return cos_sq * half_root, 0.5 * (across * root) * half_root


def jacobi_kernel(gram_ref, out_ref, gram_buf, basis_buf):
    size = gram_ref.shape[0]
    half = size // 2
    groups = half // SUBS
    last = groups - 1
    edge = half // 2 - 1
    lane_row = lax.broadcasted_iota(jnp.int32, (1, LANES), 1)
    lane = lax.broadcasted_iota(jnp.int32, (SUBS, LANES), 1)
    sub = lax.broadcasted_iota(jnp.int32, (SUBS, LANES), 0)
    spot = lane - sub * (groups // 2)

    def on_diag(group):
        return spot == group // 2

    row_slot = slot_of_row(lax.broadcasted_iota(jnp.int32, (size, 1), 0), groups, half)
    take_rows = onehot(row_slot, lax.broadcasted_iota(jnp.int32, (size, size), 1))
    lane_slot = slot_of_lane(lax.broadcasted_iota(jnp.int32, (1, 4 * LANES), 1), half)
    take_cols = onehot(lax.broadcasted_iota(jnp.int32, (size, 4 * LANES), 0), lane_slot)
    arranged = jnp.zeros((size, 4 * LANES), jnp.float32)
    for piece in split_three(gram_ref[...]):
        moved = dot32(take_rows, piece).astype(jnp.bfloat16)
        arranged = arranged + dot32(moved, take_cols)
    gram_buf[0] = arranged.reshape(2, groups, SUBS, 4 * LANES)
    basis_buf[0] = take_rows.astype(jnp.float32).reshape(2, groups, SUBS, size)

    zero = jnp.zeros((SUBS, LANES), jnp.float32)
    heads, tails, couplings = [zero, zero], [zero, zero], [zero, zero]
    for group in range(groups):
        odd = group % 2
        mask = on_diag(group)
        lead_cols = slice(odd * LANES, (odd + 1) * LANES)
        tail_cols = slice((2 + odd) * LANES, (3 + odd) * LANES)
        heads[odd] += jnp.where(mask, gram_buf[0, 0, group, :, lead_cols], 0.0)
        tails[odd] += jnp.where(mask, gram_buf[0, 1, group, :, tail_cols], 0.0)
        couplings[odd] += jnp.where(mask, gram_buf[0, 0, group, :, tail_cols], 0.0)

    def flat(values):
        return jnp.sum(values, axis=0, keepdims=True)

    def shift_lanes(lead, tail):
        lead0, lead1 = lead[:, :LANES], lead[:, LANES:]
        tail0, tail1 = tail[:, :LANES], tail[:, LANES:]
        here = lane[: lead.shape[0]]
        new_lead1 = jnp.where(here == 0, tail0, lead0)
        new_lead0 = jnp.where(here == 0, lead0, pltpu.roll(lead1, 1, 1))
        new_tail1 = jnp.where(here == edge, lead1, pltpu.roll(tail0, LANES - 1, 1))
        return new_lead0, new_lead1, tail1, new_tail1

    def turn(turn_index, carry):
        heads, tails, couplings = carry
        source = turn_index % 2
        target = 1 - source
        cosines, sines, new_heads, new_tails = [], [], [], []
        for odd in range(2):
            head, tail = heads[odd], tails[odd]
            coupling = flat(couplings[odd])
            cosine, sine_val = angles(head, tail, coupling)
            cosines.append(cosine)
            sines.append(sine_val)
            first = cosine * head + sine_val * coupling
            second = cosine * coupling + sine_val * tail
            new_heads.append(cosine * first + sine_val * second)
            first = cosine * coupling - sine_val * head
            second = cosine * tail - sine_val * coupling
            new_tails.append(cosine * second - sine_val * first)
        shifted_diag = shift_lanes(
            jnp.concatenate([jnp.broadcast_to(x, (SUBS, LANES)) for x in new_heads], axis=1),
            jnp.concatenate([jnp.broadcast_to(x, (SUBS, LANES)) for x in new_tails], axis=1),
        )
        shifted_diag = [x[:1] for x in shifted_diag]
        cos_lanes = [jnp.broadcast_to(x, (SUBS, LANES)) for x in cosines]
        sin_lanes = [jnp.broadcast_to(x, (SUBS, LANES)) for x in sines]
        cos_wide = jnp.concatenate(cos_lanes, axis=1)
        sin_wide = jnp.concatenate(sin_lanes, axis=1)

        def work(group):
            mask = on_diag(group)
            odd = group % 2
            cos_row = jnp.sum(jnp.where(mask, cos_lanes[odd], 0.0), axis=1, keepdims=True)
            sin_row = jnp.sum(jnp.where(mask, sin_lanes[odd], 0.0), axis=1, keepdims=True)

            def turned(part):
                values = gram_buf[source, part, group]
                lead, tail = values[:, : 2 * LANES], values[:, 2 * LANES :]
                return cos_wide * lead + sin_wide * tail, cos_wide * tail - sin_wide * lead

            top_lead, top_tail = turned(0)
            low_lead, low_tail = turned(1)
            top = shift_lanes(
                cos_row * top_lead + sin_row * low_lead, cos_row * top_tail + sin_row * low_tail
            )
            low = shift_lanes(
                cos_row * low_lead - sin_row * top_lead, cos_row * low_tail - sin_row * top_tail
            )
            lead = basis_buf[source, 0, group]
            tail = basis_buf[source, 1, group]
            base_top = cos_row * lead + sin_row * tail
            base_low = cos_row * tail - sin_row * lead
            return (
                list(top) + [base_top[:, i : i + LANES] for i in range(0, size, LANES)],
                list(low) + [base_low[:, i : i + LANES] for i in range(0, size, LANES)],
            )

        sums = [zero, zero]

        def store(part, group, values):
            for index, value in enumerate(values[:4]):
                gram_buf[target, part, group, :, index * LANES : (index + 1) * LANES] = value
            for index, value in enumerate(values[4:]):
                basis_buf[target, part, group, :, index * LANES : (index + 1) * LANES] = value
            if part == 0:
                odd = group % 2
                sums[odd] += jnp.where(on_diag(group), values[2 + odd], 0.0)

        first_top, first_low = work(0)
        last_top, last_low = work(last)
        store(0, 1, [jnp.where(sub == 0, y, x) for x, y in zip(first_top, first_low)])
        store(0, 0, [jnp.where(sub == 0, x, pltpu.roll(y, 1, 0)) for x, y in zip(first_top, last_top)])
        store(1, last, [
            jnp.where(sub == SUBS - 1, y, pltpu.roll(x, SUBS - 1, 0))
            for x, y in zip(first_low, last_top)
        ])
        store(1, last - 1, last_low)
        for group in range(1, last):
            top, low = work(group)
            store(0, group + 1, top)
            store(1, group - 1, low)
        return (
            (shifted_diag[0], shifted_diag[1]), (shifted_diag[2], shifted_diag[3]), tuple(sums)
        )

    start = (
        tuple(flat(x) for x in heads), tuple(flat(x) for x in tails), tuple(couplings)
    )
    lax.fori_loop(0, ROUNDS, turn, start)

    held = jnp.where(row_slot == 0, 0, 1 + (row_slot + (size - 2 - ROUNDS % (size - 1))) % (size - 1))
    place = onehot(held, lax.broadcasted_iota(jnp.int32, (size, size), 1))
    basis = basis_buf[ROUNDS % 2].reshape(size, size).astype(jnp.bfloat16)
    out_ref[...] = dot32(basis, place, ((0,), (0,))).astype(jnp.bfloat16)


def jacobi(gram_sum):
    size = gram_sum.shape[0]
    groups = size // 2 // SUBS
    return pl.pallas_call(
        jacobi_kernel,
        out_shape=jax.ShapeDtypeStruct((size, size), jnp.bfloat16),
        in_specs=[pl.BlockSpec(memory_space=pltpu.VMEM)],
        out_specs=pl.BlockSpec(memory_space=pltpu.VMEM),
        scratch_shapes=[
            pltpu.VMEM((2, 2, groups, SUBS, 4 * LANES), jnp.float32),
            pltpu.VMEM((2, 2, groups, SUBS, size), jnp.float32),
        ],
        compiler_params=pltpu.CompilerParams(vmem_limit_bytes=32 * 1024 * 1024),
        name="jacobi_turns",
    )(gram_sum)


def shifted(value, axis, steps):
    count = lax.axis_size(axis)
    pairs = [(source, (source + steps) % count) for source in range(count)]
    return lax.ppermute(value, axis, pairs)


def inner_cols(left_side, right_side):
    return lax.dot_general(
        left_side, right_side, (((0,), (0,)), ((), ())), preferred_element_type=jnp.float32
    )


def on_device(matrix, plan):
    cycle_size = lax.axis_size("blk")
    position = lax.axis_index("blk")
    block_width = matrix.shape[1] // 2
    gram_sum = lax.psum(inner_cols(matrix, matrix), "rows")
    diag_sq = jnp.sum(jnp.diagonal(gram_sum) ** 2)
    off_sq = jnp.sum(gram_sum * gram_sum) - diag_sq
    off_total, diag_total = lax.psum((off_sq, diag_sq), "blk")
    off_ratio = jnp.sqrt(off_total / diag_total)
    rotation = jacobi(gram_sum)
    my_dest = lax.dynamic_slice_in_dim(plan, 2 * position, 2)
    next_dev = (position + 1) % cycle_size
    right_first = my_dest[0] // 2 == next_dev
    rotated = jnp.dot(matrix, rotation, preferred_element_type=jnp.float32).astype(jnp.bfloat16)
    going_right = jnp.where(right_first, rotated[:, :block_width], rotated[:, block_width:])
    going_left = jnp.where(right_first, rotated[:, block_width:], rotated[:, :block_width])
    from_left = shifted(going_right, "blk", 1)
    from_right = shifted(going_left, "blk", -1)
    prev_dev = (position + cycle_size - 1) % cycle_size
    their_dest = lax.dynamic_slice_in_dim(plan, 2 * prev_dev, 2)
    in_slot = jnp.where(their_dest[0] // 2 == position, their_dest[0], their_dest[1]) % 2
    slot_zero = jnp.where(in_slot == 0, from_left, from_right)
    slot_one = jnp.where(in_slot == 0, from_right, from_left)
    return (jnp.concatenate([slot_zero, slot_one], axis=1), off_ratio)


def solution(mesh):
    in_specs = (P("rows", "blk"), P())
    out_specs = (P("rows", "blk"), P())
    return jax.shard_map(
        on_device, mesh=mesh, in_specs=in_specs, out_specs=out_specs, check_vma=False
    )
```

```python
import jax
import jax.numpy as jnp
from jax import lax
from jax.experimental import pallas as pl
from jax.experimental.pallas import tpu as pltpu
from jax.sharding import PartitionSpec as P

ROUNDS = 24
LANES = 128
SUBS = 8


def split_three(values):
    high = values.astype(jnp.bfloat16)
    rest = values - high.astype(jnp.float32)
    middle = rest.astype(jnp.bfloat16)
    low = (rest - middle.astype(jnp.float32)).astype(jnp.bfloat16)
    return high, middle, low


def dot32(left, right, dims=((1,), (0,))):
    return lax.dot_general(left, right, (dims, ((), ())), preferred_element_type=jnp.float32)


def slot_of_row(rows, groups, half):
    part = rows // half
    inside = rows % half
    index = (inside % SUBS) * groups + inside // SUBS
    return jnp.where(part == 0, index, 2 * half - 1 - index)


def slot_of_lane(lanes, half):
    part = lanes // (2 * LANES)
    odd = (lanes // LANES) % 2
    inside = lanes % LANES
    index = 2 * inside + odd
    slot = jnp.where(part == 0, index, 2 * half - 1 - index)
    return jnp.where(inside < half // 2, slot, -1)


def onehot(left, right):
    return jnp.where(left == right, 1.0, 0.0).astype(jnp.bfloat16)


def angles(head, tail, coupling):
    difference = head - tail
    sign_val = jnp.where(difference >= 0.0, 1.0, -1.0)
    across = 2.0 * coupling * sign_val
    along = jnp.abs(difference)
    scale = jnp.maximum(along, jnp.abs(across))
    empty = scale == 0.0
    inverse = 1.0 / jnp.where(empty, 1.0, scale)
    along = jnp.where(empty, 1.0, along * inverse)
    across = across * inverse
    square = along * along + across * across
    root = lax.rsqrt(square)
    root = root * (1.5 - 0.5 * square * root * root)
    cos_sq = 0.5 + 0.5 * (along * root)
    half_root = lax.rsqrt(cos_sq)
    half_root = half_root * (1.5 - 0.5 * cos_sq * half_root * half_root)
    return cos_sq * half_root, 0.5 * (across * root) * half_root


def jacobi_kernel(gram_ref, out_ref, gram_a, gram_b, basis_a, basis_b, cos_buf, sin_buf):
    size = gram_ref.shape[0]
    half = size // 2
    groups = half // SUBS
    last = groups - 1
    edge = half // 2 - 1
    lane_row = lax.broadcasted_iota(jnp.int32, (1, LANES), 1)
    lane = lax.broadcasted_iota(jnp.int32, (SUBS, LANES), 1)
    sub = lax.broadcasted_iota(jnp.int32, (SUBS, LANES), 0)
    spot = lane - sub * (groups // 2)

    def on_diag(group):
        return spot == group // 2

    row_slot = slot_of_row(lax.broadcasted_iota(jnp.int32, (size, 1), 0), groups, half)
    take_rows = onehot(row_slot, lax.broadcasted_iota(jnp.int32, (size, size), 1))
    lane_slot = slot_of_lane(lax.broadcasted_iota(jnp.int32, (1, 4 * LANES), 1), half)
    take_cols = onehot(lax.broadcasted_iota(jnp.int32, (size, 4 * LANES), 0), lane_slot)
    arranged = jnp.zeros((size, 4 * LANES), jnp.float32)
    for piece in split_three(gram_ref[...]):
        moved = dot32(take_rows, piece).astype(jnp.bfloat16)
        arranged = arranged + dot32(moved, take_cols)
    gram_a[...] = arranged.reshape(2, groups, SUBS, 4 * LANES)
    basis_a[...] = take_rows.astype(jnp.float32).reshape(2, groups, SUBS, size)

    zero = jnp.zeros((SUBS, LANES), jnp.float32)
    heads, tails, couplings = [zero, zero], [zero, zero], [zero, zero]
    for group in range(groups):
        odd = group % 2
        mask = on_diag(group)
        lead_cols = slice(odd * LANES, (odd + 1) * LANES)
        tail_cols = slice((2 + odd) * LANES, (3 + odd) * LANES)
        heads[odd] += jnp.where(mask, gram_a[0, group, :, lead_cols], 0.0)
        tails[odd] += jnp.where(mask, gram_a[1, group, :, tail_cols], 0.0)
        couplings[odd] += jnp.where(mask, gram_a[0, group, :, tail_cols], 0.0)

    def flat(values):
        return jnp.sum(values, axis=0, keepdims=True)

    def shift_lanes(lead, tail):
        lead0, lead1 = lead[:, :LANES], lead[:, LANES:]
        tail0, tail1 = tail[:, :LANES], tail[:, LANES:]
        here = lane[: lead.shape[0]]
        new_lead1 = jnp.where(here == 0, tail0, lead0)
        new_lead0 = jnp.where(here == 0, lead0, pltpu.roll(lead1, 1, 1))
        new_tail1 = jnp.where(here == edge, lead1, pltpu.roll(tail0, LANES - 1, 1))
        return new_lead0, new_lead1, tail1, new_tail1

    def turn(gram_from, gram_to, basis_from, basis_to, carry):
        heads, tails, couplings = carry
        cosines, sines, new_heads, new_tails = [], [], [], []
        for odd in range(2):
            head, tail = heads[odd], tails[odd]
            coupling = flat(couplings[odd])
            cosine, sine_val = angles(head, tail, coupling)
            cosines.append(cosine)
            sines.append(sine_val)
            first = cosine * head + sine_val * coupling
            second = cosine * coupling + sine_val * tail
            new_heads.append(cosine * first + sine_val * second)
            first = cosine * coupling - sine_val * head
            second = cosine * tail - sine_val * coupling
            new_tails.append(cosine * second - sine_val * first)
        shifted_diag = shift_lanes(
            jnp.concatenate([jnp.broadcast_to(x, (SUBS, LANES)) for x in new_heads], axis=1),
            jnp.concatenate([jnp.broadcast_to(x, (SUBS, LANES)) for x in new_tails], axis=1),
        )
        shifted_diag = [x[:1] for x in shifted_diag]
        cos_lanes = [jnp.broadcast_to(x, (SUBS, LANES)) for x in cosines]
        sin_lanes = [jnp.broadcast_to(x, (SUBS, LANES)) for x in sines]
        cos_wide = jnp.concatenate(cos_lanes, axis=1)
        sin_wide = jnp.concatenate(sin_lanes, axis=1)

        for group in range(groups):
            mask = on_diag(group)
            odd = group % 2
            for buf, lanes in ((cos_buf, cos_lanes[odd]), (sin_buf, sin_lanes[odd])):
                picked = jnp.sum(jnp.where(mask, lanes, 0.0), axis=1, keepdims=True)
                buf[group] = jnp.broadcast_to(picked, (SUBS, LANES))

        def work(group):
            cos_row = jnp.concatenate([cos_buf[group]] * 2, axis=1)
            sin_row = jnp.concatenate([sin_buf[group]] * 2, axis=1)
            cos_base = jnp.concatenate([cos_buf[group]] * (size // LANES), axis=1)
            sin_base = jnp.concatenate([sin_buf[group]] * (size // LANES), axis=1)

            def turned(part):
                values = gram_from[part, group]
                lead, tail = values[:, : 2 * LANES], values[:, 2 * LANES :]
                return cos_wide * lead + sin_wide * tail, cos_wide * tail - sin_wide * lead

            top_lead, top_tail = turned(0)
            low_lead, low_tail = turned(1)
            top = shift_lanes(
                cos_row * top_lead + sin_row * low_lead, cos_row * top_tail + sin_row * low_tail
            )
            low = shift_lanes(
                cos_row * low_lead - sin_row * top_lead, cos_row * low_tail - sin_row * top_tail
            )
            lead = basis_from[0, group]
            tail = basis_from[1, group]
            base_top = cos_base * lead + sin_base * tail
            base_low = cos_base * tail - sin_base * lead
            return (
                list(top) + [base_top[:, i : i + LANES] for i in range(0, size, LANES)],
                list(low) + [base_low[:, i : i + LANES] for i in range(0, size, LANES)],
            )

        sums = [zero, zero]

        def store(part, group, values):
            for index, value in enumerate(values[:4]):
                gram_to[part, group, :, index * LANES : (index + 1) * LANES] = value
            for index, value in enumerate(values[4:]):
                basis_to[part, group, :, index * LANES : (index + 1) * LANES] = value
            if part == 0:
                odd = group % 2
                sums[odd] += jnp.where(on_diag(group), values[2 + odd], 0.0)

        first_top, first_low = work(0)
        last_top, last_low = work(last)
        store(0, 1, [jnp.where(sub == 0, y, x) for x, y in zip(first_top, first_low)])
        store(0, 0, [jnp.where(sub == 0, x, pltpu.roll(y, 1, 0)) for x, y in zip(first_top, last_top)])
        store(1, last, [
            jnp.where(sub == SUBS - 1, y, pltpu.roll(x, SUBS - 1, 0))
            for x, y in zip(first_low, last_top)
        ])
        store(1, last - 1, last_low)
        for group in range(1, last):
            top, low = work(group)
            store(0, group + 1, top)
            store(1, group - 1, low)
        return (
            (shifted_diag[0], shifted_diag[1]), (shifted_diag[2], shifted_diag[3]), tuple(sums)
        )

    start = (
        tuple(flat(x) for x in heads), tuple(flat(x) for x in tails), tuple(couplings)
    )

    def two_turns(_, carry):
        carry = turn(gram_a, gram_b, basis_a, basis_b, carry)
        return turn(gram_b, gram_a, basis_b, basis_a, carry)

    lax.fori_loop(0, ROUNDS // 2, two_turns, start)

    held = jnp.where(row_slot == 0, 0, 1 + (row_slot + (size - 2 - ROUNDS % (size - 1))) % (size - 1))
    place = onehot(held, lax.broadcasted_iota(jnp.int32, (size, size), 1))
    basis = basis_a[...].reshape(size, size).astype(jnp.bfloat16)
    out_ref[...] = dot32(basis, place, ((0,), (0,))).astype(jnp.bfloat16)


def jacobi(gram_sum):
    size = gram_sum.shape[0]
    groups = size // 2 // SUBS
    return pl.pallas_call(
        jacobi_kernel,
        out_shape=jax.ShapeDtypeStruct((size, size), jnp.bfloat16),
        in_specs=[pl.BlockSpec(memory_space=pltpu.VMEM)],
        out_specs=pl.BlockSpec(memory_space=pltpu.VMEM),
        scratch_shapes=[
            pltpu.VMEM((2, groups, SUBS, 4 * LANES), jnp.float32),
            pltpu.VMEM((2, groups, SUBS, 4 * LANES), jnp.float32),
            pltpu.VMEM((2, groups, SUBS, size), jnp.float32),
            pltpu.VMEM((2, groups, SUBS, size), jnp.float32),
            pltpu.VMEM((groups, SUBS, LANES), jnp.float32),
            pltpu.VMEM((groups, SUBS, LANES), jnp.float32),
        ],
        compiler_params=pltpu.CompilerParams(vmem_limit_bytes=32 * 1024 * 1024),
        name="jacobi_turns",
    )(gram_sum)


def shifted(value, axis, steps):
    count = lax.axis_size(axis)
    pairs = [(source, (source + steps) % count) for source in range(count)]
    return lax.ppermute(value, axis, pairs)


def inner_cols(left_side, right_side):
    return lax.dot_general(
        left_side, right_side, (((0,), (0,)), ((), ())), preferred_element_type=jnp.float32
    )


def on_device(matrix, plan):
    cycle_size = lax.axis_size("blk")
    position = lax.axis_index("blk")
    block_width = matrix.shape[1] // 2
    gram_sum = lax.psum(inner_cols(matrix, matrix), "rows")
    diag_sq = jnp.sum(jnp.diagonal(gram_sum) ** 2)
    off_sq = jnp.sum(gram_sum * gram_sum) - diag_sq
    off_total, diag_total = lax.psum((off_sq, diag_sq), "blk")
    off_ratio = jnp.sqrt(off_total / diag_total)
    rotation = jacobi(gram_sum)
    my_dest = lax.dynamic_slice_in_dim(plan, 2 * position, 2)
    next_dev = (position + 1) % cycle_size
    right_first = my_dest[0] // 2 == next_dev
    rotated = jnp.dot(matrix, rotation, preferred_element_type=jnp.float32).astype(jnp.bfloat16)
    going_right = jnp.where(right_first, rotated[:, :block_width], rotated[:, block_width:])
    going_left = jnp.where(right_first, rotated[:, block_width:], rotated[:, :block_width])
    from_left = shifted(going_right, "blk", 1)
    from_right = shifted(going_left, "blk", -1)
    prev_dev = (position + cycle_size - 1) % cycle_size
    their_dest = lax.dynamic_slice_in_dim(plan, 2 * prev_dev, 2)
    in_slot = jnp.where(their_dest[0] // 2 == position, their_dest[0], their_dest[1]) % 2
    slot_zero = jnp.where(in_slot == 0, from_left, from_right)
    slot_one = jnp.where(in_slot == 0, from_right, from_left)
    return (jnp.concatenate([slot_zero, slot_one], axis=1), off_ratio)


def solution(mesh):
    in_specs = (P("rows", "blk"), P())
    out_specs = (P("rows", "blk"), P())
    return jax.shard_map(
        on_device, mesh=mesh, in_specs=in_specs, out_specs=out_specs, check_vma=False
    )
```

```python
import jax
import jax.numpy as jnp
from jax import lax
from jax.experimental import pallas as pl
from jax.experimental.pallas import tpu as pltpu
from jax.sharding import PartitionSpec as P

ROUNDS = 24
LANES = 128
SUBS = 8
TILE = 512
GRAM_TILE = 1024
RAW_ROWS = 1024
FIRST_ROWS = 3072
VMEM_LIMIT = 32 * 1024 * 1024


def split_three(values):
    high = values.astype(jnp.bfloat16)
    rest = values - high.astype(jnp.float32)
    middle = rest.astype(jnp.bfloat16)
    low = (rest - middle.astype(jnp.float32)).astype(jnp.bfloat16)
    return high, middle, low


def dot32(left, right, dims=((1,), (0,))):
    return lax.dot_general(left, right, (dims, ((), ())), preferred_element_type=jnp.float32)


def slot_of_row(rows, groups, half):
    part = rows // half
    inside = rows % half
    index = (inside % SUBS) * groups + inside // SUBS
    return jnp.where(part == 0, index, 2 * half - 1 - index)


def slot_of_lane(lanes, half):
    part = lanes // (2 * LANES)
    odd = (lanes // LANES) % 2
    inside = lanes % LANES
    index = 2 * inside + odd
    slot = jnp.where(part == 0, index, 2 * half - 1 - index)
    return jnp.where(inside < half // 2, slot, -1)


def onehot(left, right):
    return jnp.where(left == right, 1.0, 0.0).astype(jnp.bfloat16)


def angles(head, tail, coupling):
    difference = head - tail
    sign_val = jnp.where(difference >= 0.0, 1.0, -1.0)
    across = 2.0 * coupling * sign_val
    along = jnp.abs(difference)
    scale = jnp.maximum(along, jnp.abs(across))
    empty = scale == 0.0
    inverse = 1.0 / jnp.where(empty, 1.0, scale)
    along = jnp.where(empty, 1.0, along * inverse)
    across = across * inverse
    square = along * along + across * across
    root = lax.rsqrt(square)
    root = root * (1.5 - 0.5 * square * root * root)
    cos_sq = 0.5 + 0.5 * (along * root)
    half_root = lax.rsqrt(cos_sq)
    half_root = half_root * (1.5 - 0.5 * cos_sq * half_root * half_root)
    return cos_sq * half_root, 0.5 * (across * root) * half_root


def full_gram(packed):
    first = packed[:LANES]
    block01, block02 = first[:, LANES : 2 * LANES], first[:, 2 * LANES :]
    block12 = packed[LANES:, LANES : 2 * LANES]
    second = jnp.concatenate([block01.T, packed[LANES:, : 2 * LANES]], axis=1)
    third = jnp.concatenate([block02.T, block12.T, packed[LANES:, 2 * LANES :]], axis=1)
    return jnp.concatenate([first, second, third], axis=0)


def send_columns(lanes, base, slot, width):
    section = lanes // LANES
    lane = lanes % LANES
    rest = width - LANES
    main_start = base + jnp.where(slot == 0, 0, rest)
    rest_start = base + jnp.where(slot == 0, LANES, 0)
    high = (section // 2 + slot) % 2
    inside = lane - high * (LANES - rest)
    mixed = jnp.where((inside >= 0) & (inside < rest), rest_start + inside, -1)
    return jnp.where(section == 1, main_start + lane, mixed)


def jacobi_kernel(side_ref, *refs):
    gram_refs, outs, scratch = refs[:-9], refs[-9:-6], refs[-6:]
    jacobi_body(side_ref, gram_refs, *outs, *scratch)


def jacobi_body(
    side_ref, gram_refs, slow_ref, fast_ref, sums_ref, gram_a, gram_b, basis_a, basis_b, cos_buf, sin_buf
):
    size = gram_refs[0].shape[1]
    half = size // 2
    groups = half // SUBS
    last = groups - 1
    edge = half // 2 - 1
    lane_row = lax.broadcasted_iota(jnp.int32, (1, LANES), 1)
    lane = lax.broadcasted_iota(jnp.int32, (SUBS, LANES), 1)
    sub = lax.broadcasted_iota(jnp.int32, (SUBS, LANES), 0)
    spot = lane - sub * (groups // 2)

    def on_diag(group):
        return spot == group // 2

    row_slot = slot_of_row(lax.broadcasted_iota(jnp.int32, (size, 1), 0), groups, half)
    take_rows = onehot(row_slot, lax.broadcasted_iota(jnp.int32, (size, size), 1))
    lane_slot = slot_of_lane(lax.broadcasted_iota(jnp.int32, (1, 4 * LANES), 1), half)
    take_cols = onehot(lax.broadcasted_iota(jnp.int32, (size, 4 * LANES), 0), lane_slot)
    arranged = jnp.zeros((size, 4 * LANES), jnp.float32)
    packed = gram_refs[0][...]
    for other in gram_refs[1:]:
        packed = packed + other[...]
    gram_sum = full_gram(packed)
    squares = gram_sum * gram_sum
    rows = lax.broadcasted_iota(jnp.int32, (size, size), 0)
    cols = lax.broadcasted_iota(jnp.int32, (size, size), 1)
    diag_sq = jnp.sum(jnp.where(rows == cols, squares, 0.0), keepdims=True)
    off_sq = jnp.sum(squares, keepdims=True) - diag_sq
    sums_ref[...] = jnp.where(sub == 0, off_sq, diag_sq)
    for piece in split_three(gram_sum):
        moved = dot32(take_rows, piece).astype(jnp.bfloat16)
        arranged = arranged + dot32(moved, take_cols)
    gram_a[...] = arranged.reshape(2, groups, SUBS, 4 * LANES)
    basis_a[...] = take_rows.astype(jnp.float32).reshape(2, groups, SUBS, size)

    zero = jnp.zeros((SUBS, LANES), jnp.float32)
    heads, tails, couplings = [zero, zero], [zero, zero], [zero, zero]
    for group in range(groups):
        odd = group % 2
        mask = on_diag(group)
        lead_cols = slice(odd * LANES, (odd + 1) * LANES)
        tail_cols = slice((2 + odd) * LANES, (3 + odd) * LANES)
        heads[odd] += jnp.where(mask, gram_a[0, group, :, lead_cols], 0.0)
        tails[odd] += jnp.where(mask, gram_a[1, group, :, tail_cols], 0.0)
        couplings[odd] += jnp.where(mask, gram_a[0, group, :, tail_cols], 0.0)

    def flat(values):
        return jnp.sum(values, axis=0, keepdims=True)

    def shift_lanes(lead, tail):
        lead0, lead1 = lead[:, :LANES], lead[:, LANES:]
        tail0, tail1 = tail[:, :LANES], tail[:, LANES:]
        here = lane[: lead.shape[0]]
        new_lead1 = jnp.where(here == 0, tail0, lead0)
        new_lead0 = jnp.where(here == 0, lead0, pltpu.roll(lead1, 1, 1))
        new_tail1 = jnp.where(here == edge, lead1, pltpu.roll(tail0, LANES - 1, 1))
        return new_lead0, new_lead1, tail1, new_tail1

    def turn(gram_from, gram_to, basis_from, basis_to, carry):
        heads, tails, couplings = carry
        cosines, sines, new_heads, new_tails = [], [], [], []
        for odd in range(2):
            head, tail = heads[odd], tails[odd]
            coupling = flat(couplings[odd])
            cosine, sine_val = angles(head, tail, coupling)
            cosines.append(cosine)
            sines.append(sine_val)
            first = cosine * head + sine_val * coupling
            second = cosine * coupling + sine_val * tail
            new_heads.append(cosine * first + sine_val * second)
            first = cosine * coupling - sine_val * head
            second = cosine * tail - sine_val * coupling
            new_tails.append(cosine * second - sine_val * first)
        shifted_diag = shift_lanes(
            jnp.concatenate([jnp.broadcast_to(x, (SUBS, LANES)) for x in new_heads], axis=1),
            jnp.concatenate([jnp.broadcast_to(x, (SUBS, LANES)) for x in new_tails], axis=1),
        )
        shifted_diag = [x[:1] for x in shifted_diag]
        cos_lanes = [jnp.broadcast_to(x, (SUBS, LANES)) for x in cosines]
        sin_lanes = [jnp.broadcast_to(x, (SUBS, LANES)) for x in sines]
        cos_wide = jnp.concatenate(cos_lanes, axis=1)
        sin_wide = jnp.concatenate(sin_lanes, axis=1)

        for group in range(groups):
            mask = on_diag(group)
            odd = group % 2
            for buf, lanes in ((cos_buf, cos_lanes[odd]), (sin_buf, sin_lanes[odd])):
                picked = jnp.sum(jnp.where(mask, lanes, 0.0), axis=1, keepdims=True)
                buf[group] = jnp.broadcast_to(picked, (SUBS, LANES))

        def work(group):
            cos_row = jnp.concatenate([cos_buf[group]] * 2, axis=1)
            sin_row = jnp.concatenate([sin_buf[group]] * 2, axis=1)
            cos_base = jnp.concatenate([cos_buf[group]] * (size // LANES), axis=1)
            sin_base = jnp.concatenate([sin_buf[group]] * (size // LANES), axis=1)

            def turned(part):
                values = gram_from[part, group]
                lead, tail = values[:, : 2 * LANES], values[:, 2 * LANES :]
                return cos_wide * lead + sin_wide * tail, cos_wide * tail - sin_wide * lead

            top_lead, top_tail = turned(0)
            low_lead, low_tail = turned(1)
            top = shift_lanes(
                cos_row * top_lead + sin_row * low_lead, cos_row * top_tail + sin_row * low_tail
            )
            low = shift_lanes(
                cos_row * low_lead - sin_row * top_lead, cos_row * low_tail - sin_row * top_tail
            )
            lead = basis_from[0, group]
            tail = basis_from[1, group]
            base_top = cos_base * lead + sin_base * tail
            base_low = cos_base * tail - sin_base * lead
            return (
                list(top) + [base_top[:, i : i + LANES] for i in range(0, size, LANES)],
                list(low) + [base_low[:, i : i + LANES] for i in range(0, size, LANES)],
            )

        sums = [zero, zero]

        def store(part, group, values):
            for index, value in enumerate(values[:4]):
                gram_to[part, group, :, index * LANES : (index + 1) * LANES] = value
            for index, value in enumerate(values[4:]):
                basis_to[part, group, :, index * LANES : (index + 1) * LANES] = value
            if part == 0:
                odd = group % 2
                sums[odd] += jnp.where(on_diag(group), values[2 + odd], 0.0)

        first_top, first_low = work(0)
        last_top, last_low = work(last)
        store(0, 1, [jnp.where(sub == 0, y, x) for x, y in zip(first_top, first_low)])
        store(0, 0, [jnp.where(sub == 0, x, pltpu.roll(y, 1, 0)) for x, y in zip(first_top, last_top)])
        store(1, last, [
            jnp.where(sub == SUBS - 1, y, pltpu.roll(x, SUBS - 1, 0))
            for x, y in zip(first_low, last_top)
        ])
        store(1, last - 1, last_low)
        for group in range(1, last):
            top, low = work(group)
            store(0, group + 1, top)
            store(1, group - 1, low)
        return (
            (shifted_diag[0], shifted_diag[1]), (shifted_diag[2], shifted_diag[3]), tuple(sums)
        )

    start = (
        tuple(flat(x) for x in heads), tuple(flat(x) for x in tails), tuple(couplings)
    )

    def two_turns(_, carry):
        carry = turn(gram_a, gram_b, basis_a, basis_b, carry)
        return turn(gram_b, gram_a, basis_b, basis_a, carry)

    lax.fori_loop(0, ROUNDS // 2, two_turns, start)

    held = jnp.where(row_slot == 0, 0, 1 + (row_slot + (size - 2 - ROUNDS % (size - 1))) % (size - 1))
    basis = basis_a[...].reshape(size, size).astype(jnp.bfloat16)
    lanes = lax.broadcasted_iota(jnp.int32, (1, size), 1)
    for index, ref in enumerate((slow_ref, fast_ref)):
        wanted = send_columns(lanes, side_ref[2 * index], side_ref[2 * index + 1], half)
        ref[...] = dot32(basis, onehot(held, wanted), ((0,), (0,))).astype(jnp.bfloat16)


def jacobi(side, grams):
    size = grams[0].shape[1]
    groups = size // 2 // SUBS
    return pl.pallas_call(
        jacobi_kernel,
        out_shape=(
            jax.ShapeDtypeStruct((size, size), jnp.bfloat16),
            jax.ShapeDtypeStruct((size, size), jnp.bfloat16),
            jax.ShapeDtypeStruct((SUBS, LANES), jnp.float32),
        ),
        in_specs=[pl.BlockSpec(memory_space=pltpu.SMEM)]
        + [pl.BlockSpec(memory_space=pltpu.VMEM)] * len(grams),
        out_specs=[pl.BlockSpec(memory_space=pltpu.VMEM)] * 3,
        scratch_shapes=[
            pltpu.VMEM((2, groups, SUBS, 4 * LANES), jnp.float32),
            pltpu.VMEM((2, groups, SUBS, 4 * LANES), jnp.float32),
            pltpu.VMEM((2, groups, SUBS, size), jnp.float32),
            pltpu.VMEM((2, groups, SUBS, size), jnp.float32),
            pltpu.VMEM((groups, SUBS, LANES), jnp.float32),
            pltpu.VMEM((groups, SUBS, LANES), jnp.float32),
        ],
        compiler_params=pltpu.CompilerParams(vmem_limit_bytes=VMEM_LIMIT),
        cost_estimate=pl.CostEstimate(
            flops=ROUNDS * 20 * size * size * 30, bytes_accessed=8 * size * size, transcendentals=0
        ),
        name="jacobi_turns",
    )(side, *grams)


def gram_kernel(matrix_ref, packed_ref, upper_ref, corner_ref):
    step = pl.program_id(0)
    values = matrix_ref[...]
    right = values[:, 2 * LANES :]
    upper = dot32(values[:, : 2 * LANES], values, ((0,), (0,)))
    corner = dot32(right, right, ((0,), (0,)))

    @pl.when(step == 0)
    def _():
        upper_ref[...] = upper
        corner_ref[...] = corner

    @pl.when(step > 0)
    def _():
        upper_ref[...] += upper
        corner_ref[...] += corner

    @pl.when(step == pl.num_programs(0) - 1)
    def _():
        packed_ref[:LANES] = upper_ref[:LANES]
        packed_ref[LANES:, : 2 * LANES] = upper_ref[LANES:, LANES:]
        packed_ref[LANES:, 2 * LANES :] = corner_ref[...]


def gram_blocks(matrix):
    rows, size = matrix.shape
    return pl.pallas_call(
        gram_kernel,
        grid=(rows // GRAM_TILE,),
        in_specs=[pl.BlockSpec((GRAM_TILE, size), lambda i: (i, 0))],
        out_specs=pl.BlockSpec((2 * LANES, size), lambda i: (0, 0)),
        out_shape=jax.ShapeDtypeStruct((2 * LANES, size), jnp.float32),
        scratch_shapes=[
            pltpu.VMEM((2 * LANES, size), jnp.float32),
            pltpu.VMEM((LANES, LANES), jnp.float32),
        ],
        compiler_params=pltpu.CompilerParams(vmem_limit_bytes=VMEM_LIMIT),
        cost_estimate=pl.CostEstimate(
            flops=2 * rows * size * size, bytes_accessed=2 * rows * size, transcendentals=0
        ),
        name="gram_blocks",
    )(matrix)


def rotate_kernel(matrix_ref, turn_ref, packed_ref):
    rows = matrix_ref.shape[0]
    half = rows // 2
    top = dot32(matrix_ref[:half], turn_ref[:, : 2 * LANES])
    low = dot32(matrix_ref[half:], turn_ref[:, LANES:])
    packed_ref[:half] = top[:, LANES:].astype(jnp.bfloat16)
    packed_ref[half:rows] = low[:, :LANES].astype(jnp.bfloat16)
    packed_ref[rows:] = (top[:, :LANES] + low[:, LANES:]).astype(jnp.bfloat16)


def rotate_rows(matrix, turn, start, count):
    size = matrix.shape[1]
    first = start // TILE
    pack = TILE + TILE // 2
    return pl.pallas_call(
        rotate_kernel,
        grid=(count // TILE,),
        in_specs=[
            pl.BlockSpec((TILE, size), lambda i: (first + i, 0)),
            pl.BlockSpec((size, size), lambda i: (0, 0)),
        ],
        out_specs=pl.BlockSpec((pack, LANES), lambda i: (i, 0)),
        out_shape=jax.ShapeDtypeStruct((count // TILE * pack, LANES), jnp.bfloat16),
        compiler_params=pltpu.CompilerParams(vmem_limit_bytes=VMEM_LIMIT),
        cost_estimate=pl.CostEstimate(
            flops=4 * count * size * LANES, bytes_accessed=3 * count * size, transcendentals=0
        ),
        name="rotate_rows",
    )(matrix, turn)


def low_lanes(slot, rows):
    lane = lax.broadcasted_iota(jnp.int32, (rows, LANES), 1)
    return (lane // (LANES // 2)) == slot


def place_main(slot, out_ref, slow_main, fast_main):
    @pl.when(slot == 0)
    def _():
        out_ref[:, :LANES] = slow_main
        out_ref[:, 2 * LANES :] = fast_main

    @pl.when(slot != 0)
    def _():
        out_ref[:, :LANES] = fast_main
        out_ref[:, 2 * LANES :] = slow_main


def place_kernel(slot_ref, slow_ref, fast_ref, *refs):
    out_ref = refs[-1]
    rows = out_ref.shape[0]
    half = rows // 2
    slot = slot_ref[0]
    place_main(slot, out_ref, slow_ref[:rows], fast_ref[:rows])
    slow = slow_ref[rows:].astype(jnp.float32)
    fast = fast_ref[rows:].astype(jnp.float32)
    mask = low_lanes(slot, half)
    middle = slice(LANES, 2 * LANES)
    out_ref[:half, middle] = jnp.where(mask, slow, fast).astype(jnp.bfloat16)
    swapped = pltpu.roll(jnp.where(mask, fast, slow), LANES // 2, 1)
    out_ref[half:, middle] = swapped.astype(jnp.bfloat16)


def raw_kernel(slot_ref, raw_ref, turn_ref, fast_ref, *refs):
    out_ref = refs[-1]
    rows = out_ref.shape[0]
    half = rows // 2
    slot = slot_ref[0]
    turned = dot32(raw_ref[...], turn_ref[...])
    place_main(slot, out_ref, turned[:, LANES:].astype(jnp.bfloat16), fast_ref[:rows])
    fast = fast_ref[rows:].astype(jnp.float32)
    mask = low_lanes(slot, half)
    middle = slice(LANES, 2 * LANES)
    out_ref[:half, middle] = jnp.where(mask, turned[:half, :LANES], fast).astype(jnp.bfloat16)
    swapped = pltpu.roll(fast, LANES // 2, 1)
    out_ref[half:, middle] = jnp.where(mask, turned[half:, :LANES], swapped).astype(jnp.bfloat16)


def fill_rows(kernel, slot, sources, specs, fast, held, shape, start, count):
    first = start // TILE
    pack = TILE + TILE // 2
    operands = [slot, *sources, fast]
    in_specs = [
        pl.BlockSpec(memory_space=pltpu.SMEM),
        *specs,
        pl.BlockSpec((pack, LANES), lambda i: (first + i, 0)),
    ]
    aliases = {}
    if held is not None:
        aliases = {len(operands): 0}
        operands.append(held)
        in_specs.append(pl.BlockSpec(memory_space=pl.ANY))
    return pl.pallas_call(
        kernel,
        grid=(count // TILE,),
        in_specs=in_specs,
        out_specs=pl.BlockSpec((TILE, shape[1]), lambda i: (first + i, 0)),
        out_shape=jax.ShapeDtypeStruct(shape, jnp.bfloat16),
        input_output_aliases=aliases,
        compiler_params=pltpu.CompilerParams(vmem_limit_bytes=VMEM_LIMIT),
        cost_estimate=pl.CostEstimate(
            flops=count * shape[1], bytes_accessed=4 * count * shape[1], transcendentals=0
        ),
        name="fill_rows",
    )(*operands)


def swapped_with(value, axis, partner):
    count = lax.axis_size(axis)
    return lax.ppermute(value, axis, [(source, partner(source, count)) for source in range(count)])


def slow_partner(source, count):
    return (source + 1) % count if source % 2 else (source + count - 1) % count


def fast_partner(source, count):
    return source ^ 1


def sends_and_slot(plan):
    count = lax.axis_size("blk")
    position = lax.axis_index("blk")
    step = 2 * (position % 2) - 1
    slow_dev = (position + step + count) % count
    mine = lax.dynamic_slice_in_dim(plan, 2 * position, 2)
    theirs = lax.dynamic_slice_in_dim(plan, 2 * slow_dev, 2)
    first_slow = mine[0] // 2 == slow_dev
    slow_to = jnp.where(first_slow, mine[0], mine[1])
    fast_to = jnp.where(first_slow, mine[1], mine[0])
    in_slot = jnp.where(theirs[0] // 2 == position, theirs[0], theirs[1]) % 2
    return first_slow, slow_to % 2, fast_to % 2, in_slot


def on_device(matrix, plan):
    rows, size = matrix.shape
    width = size // 2
    first_slow, slow_slot, fast_slot, in_slot = sends_and_slot(plan)
    zero = jnp.zeros((), jnp.int32)
    side = jnp.stack([
        jnp.where(first_slow, zero, width), slow_slot, jnp.where(first_slow, width, zero), fast_slot
    ]).astype(jnp.int32)
    slot = in_slot.astype(jnp.int32)[None]

    raw = swapped_with(matrix[:RAW_ROWS], "blk", slow_partner)
    own = gram_blocks(matrix)
    if lax.axis_size("rows") == 2:
        grams = [own, swapped_with(own, "rows", fast_partner)]
    else:
        grams = [lax.psum(own, "rows")]
    slow_turn, fast_turn, sums = jacobi(side, grams)
    totals = jnp.sum(lax.all_gather(sums, "blk"), axis=0)
    off_ratio = jnp.sqrt(totals[0, 0] / totals[1, 0])

    their_turn = swapped_with(slow_turn[:, : 2 * LANES], "blk", slow_partner)
    spans = [(RAW_ROWS, FIRST_ROWS), (RAW_ROWS + FIRST_ROWS, rows - RAW_ROWS - FIRST_ROWS)]
    arrived = [
        swapped_with(rotate_rows(matrix, slow_turn, start, count), "blk", slow_partner)
        for start, count in spans
    ]
    fast = swapped_with(rotate_rows(matrix, fast_turn, 0, rows), "blk", fast_partner)
    shape = (rows, size)
    pack = TILE + TILE // 2
    result = fill_rows(
        raw_kernel,
        slot,
        [raw, their_turn],
        [
            pl.BlockSpec((TILE, size), lambda i: (i, 0)),
            pl.BlockSpec((size, 2 * LANES), lambda i: (0, 0)),
        ],
        fast, None, shape, 0, RAW_ROWS,
    )
    for (start, count), slow in zip(spans, arrived):
        result = fill_rows(
            place_kernel,
            slot,
            [slow],
            [pl.BlockSpec((pack, LANES), lambda i: (i, 0))],
            fast, result, shape, start, count,
        )
    return result, off_ratio


def solution(mesh):
    in_specs = (P("rows", "blk"), P())
    out_specs = (P("rows", "blk"), P())
    return jax.shard_map(
        on_device, mesh=mesh, in_specs=in_specs, out_specs=out_specs, check_vma=False
    )
```

```python
import jax
import jax.numpy as jnp
from jax import lax
from jax.experimental import pallas as pl
from jax.experimental.pallas import tpu as pltpu
from jax.sharding import PartitionSpec as P

ROUNDS = 24
LANES = 128
SUBS = 8
UNIT = 512
PACK = UNIT + UNIT // 2
GRAM_TILE = 1024
RAW_ROWS = 1024
FIRST_ROWS = 3072
VMEM_LIMIT = 32 * 1024 * 1024
GRAM_VMEM_LIMIT = 60 * 1024 * 1024


def split_three(values):
    high = values.astype(jnp.bfloat16)
    rest = values - high.astype(jnp.float32)
    middle = rest.astype(jnp.bfloat16)
    low = (rest - middle.astype(jnp.float32)).astype(jnp.bfloat16)
    return high, middle, low


def dot32(left, right, dims=((1,), (0,))):
    return lax.dot_general(left, right, (dims, ((), ())), preferred_element_type=jnp.float32)


def slot_of_row(rows, groups, half):
    part = rows // half
    inside = rows % half
    index = (inside % SUBS) * groups + inside // SUBS
    return jnp.where(part == 0, index, 2 * half - 1 - index)


def slot_of_lane(lanes, half):
    part = lanes // (2 * LANES)
    odd = (lanes // LANES) % 2
    inside = lanes % LANES
    index = 2 * inside + odd
    slot = jnp.where(part == 0, index, 2 * half - 1 - index)
    return jnp.where(inside < half // 2, slot, -1)


def onehot(left, right):
    return jnp.where(left == right, 1.0, 0.0).astype(jnp.bfloat16)


def angles(head, tail, coupling):
    difference = head - tail
    sign_val = jnp.where(difference >= 0.0, 1.0, -1.0)
    across = 2.0 * coupling * sign_val
    along = jnp.abs(difference)
    scale = jnp.maximum(along, jnp.abs(across))
    empty = scale == 0.0
    inverse = 1.0 / jnp.where(empty, 1.0, scale)
    along = jnp.where(empty, 1.0, along * inverse)
    across = across * inverse
    square = along * along + across * across
    root = lax.rsqrt(square)
    root = root * (1.5 - 0.5 * square * root * root)
    cos_sq = 0.5 + 0.5 * (along * root)
    half_root = lax.rsqrt(cos_sq)
    half_root = half_root * (1.5 - 0.5 * cos_sq * half_root * half_root)
    return cos_sq * half_root, 0.5 * (across * root) * half_root


def full_gram(packed):
    first = packed[:LANES]
    block01, block02 = first[:, LANES : 2 * LANES], first[:, 2 * LANES :]
    block12 = packed[LANES:, LANES : 2 * LANES]
    second = jnp.concatenate([block01.T, packed[LANES:, : 2 * LANES]], axis=1)
    third = jnp.concatenate([block02.T, block12.T, packed[LANES:, 2 * LANES :]], axis=1)
    return jnp.concatenate([first, second, third], axis=0)


def send_columns(lanes, base, slot, width):
    section = lanes // LANES
    lane = lanes % LANES
    rest = width - LANES
    main_start = base + jnp.where(slot == 0, 0, rest)
    rest_start = base + jnp.where(slot == 0, LANES, 0)
    high = (section // 2 + slot) % 2
    inside = lane - high * (LANES - rest)
    mixed = jnp.where((inside >= 0) & (inside < rest), rest_start + inside, -1)
    return jnp.where(section == 1, main_start + lane, mixed)


def moves(plan_ref):
    count = plan_ref.shape[0] // 2
    position = lax.axis_index("blk")
    slow_dev = lax.rem(position + 2 * lax.rem(position, 2) - 1 + count, count)
    mine = plan_ref[2 * position], plan_ref[2 * position + 1]
    theirs = plan_ref[2 * slow_dev], plan_ref[2 * slow_dev + 1]
    first_slow = mine[0] // 2 == slow_dev
    slow_slot = lax.rem(jnp.where(first_slow, mine[0], mine[1]), 2)
    fast_slot = lax.rem(jnp.where(first_slow, mine[1], mine[0]), 2)
    in_slot = lax.rem(jnp.where(theirs[0] // 2 == position, theirs[0], theirs[1]), 2)
    return first_slow, slow_slot, fast_slot, in_slot


def jacobi_kernel(plan_ref, *refs):
    jacobi_body(plan_ref, refs[:-10], *refs[-10:])


def jacobi_body(
    plan_ref, gram_refs, slow_ref, fast_ref, send_ref, sums_ref,
    gram_a, gram_b, basis_a, basis_b, cos_buf, sin_buf,
):
    size = gram_refs[0].shape[1]
    half = size // 2
    groups = half // SUBS
    last = groups - 1
    edge = half // 2 - 1
    lane_row = lax.broadcasted_iota(jnp.int32, (1, LANES), 1)
    lane = lax.broadcasted_iota(jnp.int32, (SUBS, LANES), 1)
    sub = lax.broadcasted_iota(jnp.int32, (SUBS, LANES), 0)
    spot = lane - sub * (groups // 2)

    def on_diag(group):
        return spot == group // 2

    row_slot = slot_of_row(lax.broadcasted_iota(jnp.int32, (size, 1), 0), groups, half)
    take_rows = onehot(row_slot, lax.broadcasted_iota(jnp.int32, (size, size), 1))
    lane_slot = slot_of_lane(lax.broadcasted_iota(jnp.int32, (1, 4 * LANES), 1), half)
    take_cols = onehot(lax.broadcasted_iota(jnp.int32, (size, 4 * LANES), 0), lane_slot)
    arranged = jnp.zeros((size, 4 * LANES), jnp.float32)
    packed = gram_refs[0][...]
    for other in gram_refs[1:]:
        packed = packed + other[...]
    gram_sum = full_gram(packed)
    squares = gram_sum * gram_sum
    rows = lax.broadcasted_iota(jnp.int32, (size, size), 0)
    cols = lax.broadcasted_iota(jnp.int32, (size, size), 1)
    diag_sq = jnp.sum(jnp.where(rows == cols, squares, 0.0), keepdims=True)
    off_sq = jnp.sum(squares, keepdims=True) - diag_sq
    sums_ref[...] = jnp.where(sub == 0, off_sq, diag_sq)
    for piece in split_three(gram_sum):
        moved = dot32(take_rows, piece).astype(jnp.bfloat16)
        arranged = arranged + dot32(moved, take_cols)
    gram_a[...] = arranged.reshape(2, groups, SUBS, 4 * LANES)
    basis_a[...] = take_rows.astype(jnp.float32).reshape(2, groups, SUBS, size)

    zero = jnp.zeros((SUBS, LANES), jnp.float32)
    heads, tails, couplings = [zero, zero], [zero, zero], [zero, zero]
    for group in range(groups):
        odd = group % 2
        mask = on_diag(group)
        lead_cols = slice(odd * LANES, (odd + 1) * LANES)
        tail_cols = slice((2 + odd) * LANES, (3 + odd) * LANES)
        heads[odd] += jnp.where(mask, gram_a[0, group, :, lead_cols], 0.0)
        tails[odd] += jnp.where(mask, gram_a[1, group, :, tail_cols], 0.0)
        couplings[odd] += jnp.where(mask, gram_a[0, group, :, tail_cols], 0.0)

    def flat(values):
        return jnp.sum(values, axis=0, keepdims=True)

    def shift_lanes(lead, tail):
        lead0, lead1 = lead[:, :LANES], lead[:, LANES:]
        tail0, tail1 = tail[:, :LANES], tail[:, LANES:]
        here = lane[: lead.shape[0]]
        new_lead1 = jnp.where(here == 0, tail0, lead0)
        new_lead0 = jnp.where(here == 0, lead0, pltpu.roll(lead1, 1, 1))
        new_tail1 = jnp.where(here == edge, lead1, pltpu.roll(tail0, LANES - 1, 1))
        return new_lead0, new_lead1, tail1, new_tail1

    def turn(gram_from, gram_to, basis_from, basis_to, carry):
        heads, tails, couplings = carry
        cosines, sines, new_heads, new_tails = [], [], [], []
        for odd in range(2):
            head, tail = heads[odd], tails[odd]
            coupling = flat(couplings[odd])
            cosine, sine_val = angles(head, tail, coupling)
            cosines.append(cosine)
            sines.append(sine_val)
            first = cosine * head + sine_val * coupling
            second = cosine * coupling + sine_val * tail
            new_heads.append(cosine * first + sine_val * second)
            first = cosine * coupling - sine_val * head
            second = cosine * tail - sine_val * coupling
            new_tails.append(cosine * second - sine_val * first)
        shifted_diag = shift_lanes(
            jnp.concatenate([jnp.broadcast_to(x, (SUBS, LANES)) for x in new_heads], axis=1),
            jnp.concatenate([jnp.broadcast_to(x, (SUBS, LANES)) for x in new_tails], axis=1),
        )
        shifted_diag = [x[:1] for x in shifted_diag]
        cos_lanes = [jnp.broadcast_to(x, (SUBS, LANES)) for x in cosines]
        sin_lanes = [jnp.broadcast_to(x, (SUBS, LANES)) for x in sines]
        cos_wide = jnp.concatenate(cos_lanes, axis=1)
        sin_wide = jnp.concatenate(sin_lanes, axis=1)

        for group in range(groups):
            mask = on_diag(group)
            odd = group % 2
            for buf, lanes in ((cos_buf, cos_lanes[odd]), (sin_buf, sin_lanes[odd])):
                picked = jnp.sum(jnp.where(mask, lanes, 0.0), axis=1, keepdims=True)
                buf[group] = jnp.broadcast_to(picked, (SUBS, LANES))

        def work(group):
            cos_row = jnp.concatenate([cos_buf[group]] * 2, axis=1)
            sin_row = jnp.concatenate([sin_buf[group]] * 2, axis=1)
            cos_base = jnp.concatenate([cos_buf[group]] * (size // LANES), axis=1)
            sin_base = jnp.concatenate([sin_buf[group]] * (size // LANES), axis=1)

            def turned(part):
                values = gram_from[part, group]
                lead, tail = values[:, : 2 * LANES], values[:, 2 * LANES :]
                return cos_wide * lead + sin_wide * tail, cos_wide * tail - sin_wide * lead

            top_lead, top_tail = turned(0)
            low_lead, low_tail = turned(1)
            top = shift_lanes(
                cos_row * top_lead + sin_row * low_lead, cos_row * top_tail + sin_row * low_tail
            )
            low = shift_lanes(
                cos_row * low_lead - sin_row * top_lead, cos_row * low_tail - sin_row * top_tail
            )
            lead = basis_from[0, group]
            tail = basis_from[1, group]
            base_top = cos_base * lead + sin_base * tail
            base_low = cos_base * tail - sin_base * lead
            return (
                list(top) + [base_top[:, i : i + LANES] for i in range(0, size, LANES)],
                list(low) + [base_low[:, i : i + LANES] for i in range(0, size, LANES)],
            )

        sums = [zero, zero]

        def store(part, group, values):
            for index, value in enumerate(values[:4]):
                gram_to[part, group, :, index * LANES : (index + 1) * LANES] = value
            for index, value in enumerate(values[4:]):
                basis_to[part, group, :, index * LANES : (index + 1) * LANES] = value
            if part == 0:
                odd = group % 2
                sums[odd] += jnp.where(on_diag(group), values[2 + odd], 0.0)

        first_top, first_low = work(0)
        last_top, last_low = work(last)
        store(0, 1, [jnp.where(sub == 0, y, x) for x, y in zip(first_top, first_low)])
        store(0, 0, [jnp.where(sub == 0, x, pltpu.roll(y, 1, 0)) for x, y in zip(first_top, last_top)])
        store(1, last, [
            jnp.where(sub == SUBS - 1, y, pltpu.roll(x, SUBS - 1, 0))
            for x, y in zip(first_low, last_top)
        ])
        store(1, last - 1, last_low)
        for group in range(1, last):
            top, low = work(group)
            store(0, group + 1, top)
            store(1, group - 1, low)
        return (
            (shifted_diag[0], shifted_diag[1]), (shifted_diag[2], shifted_diag[3]), tuple(sums)
        )

    start = (
        tuple(flat(x) for x in heads), tuple(flat(x) for x in tails), tuple(couplings)
    )

    def two_turns(_, carry):
        carry = turn(gram_a, gram_b, basis_a, basis_b, carry)
        return turn(gram_b, gram_a, basis_b, basis_a, carry)

    lax.fori_loop(0, ROUNDS // 2, two_turns, start)

    held = jnp.where(row_slot == 0, 0, 1 + (row_slot + (size - 2 - ROUNDS % (size - 1))) % (size - 1))
    basis = basis_a[...].reshape(size, size).astype(jnp.bfloat16)
    lanes = lax.broadcasted_iota(jnp.int32, (1, size), 1)
    first_slow, slow_slot, fast_slot, _ = moves(plan_ref)
    slow_base = jnp.where(first_slow, 0, half)
    for ref, base, slot in ((slow_ref, slow_base, slow_slot), (fast_ref, half - slow_base, fast_slot)):
        wanted = send_columns(lanes, base, slot, half)
        ref[...] = dot32(basis, onehot(held, wanted), ((0,), (0,))).astype(jnp.bfloat16)
    send_ref[...] = slow_ref[:, : 2 * LANES]


def jacobi(plan, grams):
    size = grams[0].shape[1]
    groups = size // 2 // SUBS
    return pl.pallas_call(
        jacobi_kernel,
        out_shape=(
            jax.ShapeDtypeStruct((size, size), jnp.bfloat16),
            jax.ShapeDtypeStruct((size, size), jnp.bfloat16),
            jax.ShapeDtypeStruct((size, 2 * LANES), jnp.bfloat16),
            jax.ShapeDtypeStruct((SUBS, LANES), jnp.float32),
        ),
        in_specs=[pl.BlockSpec(memory_space=pltpu.SMEM)]
        + [pl.BlockSpec(memory_space=pltpu.VMEM)] * len(grams),
        out_specs=[pl.BlockSpec(memory_space=pltpu.VMEM)] * 4,
        scratch_shapes=[
            pltpu.VMEM((2, groups, SUBS, 4 * LANES), jnp.float32),
            pltpu.VMEM((2, groups, SUBS, 4 * LANES), jnp.float32),
            pltpu.VMEM((2, groups, SUBS, size), jnp.float32),
            pltpu.VMEM((2, groups, SUBS, size), jnp.float32),
            pltpu.VMEM((groups, SUBS, LANES), jnp.float32),
            pltpu.VMEM((groups, SUBS, LANES), jnp.float32),
        ],
        compiler_params=pltpu.CompilerParams(vmem_limit_bytes=VMEM_LIMIT),
        cost_estimate=pl.CostEstimate(
            flops=size * size, bytes_accessed=8 * size * size, transcendentals=0
        ),
        name="jacobi_turns",
    )(plan, *grams)


def gram_kernel(matrix_ref, packed_ref, upper_ref, corner_ref):
    step = pl.program_id(0)
    values = matrix_ref[...]
    right = values[:, 2 * LANES :]
    upper = dot32(values[:, : 2 * LANES], values, ((0,), (0,)))
    corner = dot32(right, right, ((0,), (0,)))

    @pl.when(step == 0)
    def _():
        upper_ref[...] = upper
        corner_ref[...] = corner

    @pl.when(step > 0)
    def _():
        upper_ref[...] += upper
        corner_ref[...] += corner

    @pl.when(step == pl.num_programs(0) - 1)
    def _():
        packed_ref[:LANES] = upper_ref[:LANES]
        packed_ref[LANES:, : 2 * LANES] = upper_ref[LANES:, LANES:]
        packed_ref[LANES:, 2 * LANES :] = corner_ref[...]


def gram_blocks(matrix):
    rows, size = matrix.shape
    return pl.pallas_call(
        gram_kernel,
        grid=(rows // GRAM_TILE,),
        in_specs=[pl.BlockSpec((GRAM_TILE, size), lambda i: (i, 0))],
        out_specs=pl.BlockSpec((2 * LANES, size), lambda i: (0, 0)),
        out_shape=jax.ShapeDtypeStruct((2 * LANES, size), jnp.float32),
        scratch_shapes=[
            pltpu.VMEM((2 * LANES, size), jnp.float32),
            pltpu.VMEM((LANES, LANES), jnp.float32),
        ],
        compiler_params=pltpu.CompilerParams(vmem_limit_bytes=GRAM_VMEM_LIMIT),
        cost_estimate=pl.CostEstimate(
            flops=2 * rows * size * size, bytes_accessed=2 * rows * size, transcendentals=0
        ),
        name="gram_blocks",
    )(matrix)


def rotate_kernel(matrix_ref, turn_ref, packed_ref):
    half = UNIT // 2
    for unit in range(matrix_ref.shape[0] // UNIT):
        start, at = unit * UNIT, unit * PACK
        top = dot32(matrix_ref[start : start + half], turn_ref[:, : 2 * LANES])
        low = dot32(matrix_ref[start + half : start + UNIT], turn_ref[:, LANES:])
        packed_ref[at : at + half] = top[:, LANES:].astype(jnp.bfloat16)
        packed_ref[at + half : at + UNIT] = low[:, :LANES].astype(jnp.bfloat16)
        packed_ref[at + UNIT : at + PACK] = (top[:, :LANES] + low[:, LANES:]).astype(jnp.bfloat16)


def rotate_rows(matrix, turn, start, count, tile):
    size = matrix.shape[1]
    first = start // tile
    pack = tile // UNIT * PACK
    return pl.pallas_call(
        rotate_kernel,
        grid=(count // tile,),
        in_specs=[
            pl.BlockSpec((tile, size), lambda i: (first + i, 0)),
            pl.BlockSpec((size, size), lambda i: (0, 0)),
        ],
        out_specs=pl.BlockSpec((pack, LANES), lambda i: (i, 0)),
        out_shape=jax.ShapeDtypeStruct((count // UNIT * PACK, LANES), jnp.bfloat16),
        compiler_params=pltpu.CompilerParams(vmem_limit_bytes=VMEM_LIMIT),
        cost_estimate=pl.CostEstimate(
            flops=4 * count * size * LANES, bytes_accessed=3 * count * size, transcendentals=0
        ),
        name="rotate_rows",
    )(matrix, turn)


def place_main(slot, out_ref, rows, slow_main, fast_main):
    @pl.when(slot == 0)
    def _():
        out_ref[rows, :LANES] = slow_main
        out_ref[rows, 2 * LANES :] = fast_main

    @pl.when(slot != 0)
    def _():
        out_ref[rows, :LANES] = fast_main
        out_ref[rows, 2 * LANES :] = slow_main


def slot_lanes(slot):
    lane = lax.broadcasted_iota(jnp.int32, (UNIT // 2, LANES), 1)
    return (lane // (LANES // 2)) == slot


def place_kernel(plan_ref, slow_ref, fast_ref, *refs):
    out_ref = refs[-1]
    half = UNIT // 2
    slot = moves(plan_ref)[3]
    mask = slot_lanes(slot)
    middle = slice(LANES, 2 * LANES)
    for unit in range(out_ref.shape[0] // UNIT):
        start, at = unit * UNIT, unit * PACK
        main, rest = slice(at, at + UNIT), slice(at + UNIT, at + PACK)
        place_main(slot, out_ref, slice(start, start + UNIT), slow_ref[main], fast_ref[main])
        slow = slow_ref[rest].astype(jnp.float32)
        fast = fast_ref[rest].astype(jnp.float32)
        out_ref[start : start + half, middle] = jnp.where(mask, slow, fast).astype(jnp.bfloat16)
        swapped = pltpu.roll(jnp.where(mask, fast, slow), LANES // 2, 1)
        out_ref[start + half : start + UNIT, middle] = swapped.astype(jnp.bfloat16)


def raw_kernel(plan_ref, raw_ref, turn_ref, fast_ref, *refs):
    out_ref = refs[-1]
    half = UNIT // 2
    slot = moves(plan_ref)[3]
    mask = slot_lanes(slot)
    middle = slice(LANES, 2 * LANES)
    for unit in range(out_ref.shape[0] // UNIT):
        start, at = unit * UNIT, unit * PACK
        rows = slice(start, start + UNIT)
        turned = dot32(raw_ref[rows], turn_ref[...])
        main = turned[:, LANES:].astype(jnp.bfloat16)
        place_main(slot, out_ref, rows, main, fast_ref[at : at + UNIT])
        fast = fast_ref[at + UNIT : at + PACK].astype(jnp.float32)
        top = jnp.where(mask, turned[:half, :LANES], fast)
        out_ref[start : start + half, middle] = top.astype(jnp.bfloat16)
        low = jnp.where(mask, turned[half:, :LANES], pltpu.roll(fast, LANES // 2, 1))
        out_ref[start + half : start + UNIT, middle] = low.astype(jnp.bfloat16)


def fill_rows(kernel, plan, sources, specs, fast, held, shape, start, count, tile):
    first = start // tile
    pack = tile // UNIT * PACK
    operands = [plan, *sources, fast]
    in_specs = [
        pl.BlockSpec(memory_space=pltpu.SMEM),
        *specs,
        pl.BlockSpec((pack, LANES), lambda i: (first + i, 0)),
    ]
    aliases = {}
    if held is not None:
        aliases = {len(operands): 0}
        operands.append(held)
        in_specs.append(pl.BlockSpec(memory_space=pl.ANY))
    return pl.pallas_call(
        kernel,
        grid=(count // tile,),
        in_specs=in_specs,
        out_specs=pl.BlockSpec((tile, shape[1]), lambda i: (first + i, 0)),
        out_shape=jax.ShapeDtypeStruct(shape, jnp.bfloat16),
        input_output_aliases=aliases,
        compiler_params=pltpu.CompilerParams(vmem_limit_bytes=VMEM_LIMIT),
        cost_estimate=pl.CostEstimate(
            flops=count * shape[1], bytes_accessed=4 * count * shape[1], transcendentals=0
        ),
        name="fill_rows",
    )(*operands)


def swapped_with(value, axis, partner):
    count = lax.axis_size(axis)
    return lax.ppermute(value, axis, [(source, partner(source, count)) for source in range(count)])


def slow_partner(source, count):
    return (source + 1) % count if source % 2 else (source + count - 1) % count


def fast_partner(source, count):
    return source ^ 1


def sum_over(values, axis):
    count = lax.axis_size(axis)
    step = 1
    while step < count:
        values = values + swapped_with(values, axis, lambda source, _, step=step: source ^ step)
        step *= 2
    return values


def on_device(matrix, plan):
    rows, size = matrix.shape
    raw = swapped_with(matrix[:RAW_ROWS], "blk", slow_partner)
    own = gram_blocks(matrix)
    if lax.axis_size("rows") == 2:
        grams = [own, swapped_with(own, "rows", fast_partner)]
    else:
        grams = [lax.psum(own, "rows")]
    slow_turn, fast_turn, send_turn, sums = jacobi(plan, grams)

    their_turn = swapped_with(send_turn, "blk", slow_partner)
    spans = [
        (RAW_ROWS, FIRST_ROWS, FIRST_ROWS // 3),
        (RAW_ROWS + FIRST_ROWS, rows - RAW_ROWS - FIRST_ROWS, RAW_ROWS),
    ]
    packs = [rotate_rows(matrix, slow_turn, *span) for span in spans]
    arrived = [swapped_with(pack, "blk", slow_partner) for pack in packs]
    fast_turn, raw, _ = lax.optimization_barrier((fast_turn, raw, packs))
    fast_pack = rotate_rows(matrix, fast_turn, 0, rows, rows // 4)
    fast = swapped_with(fast_pack, "blk", fast_partner)
    sums, _ = lax.optimization_barrier((sums, fast_pack))
    totals = sum_over(sums, "blk")
    off_ratio = jnp.sqrt(totals[0, 0] / totals[1, 0])

    shape = (rows, size)
    raw_specs = [
        pl.BlockSpec((UNIT, size), lambda i: (i, 0)),
        pl.BlockSpec((size, 2 * LANES), lambda i: (0, 0)),
    ]
    result = fill_rows(
        raw_kernel, plan, [raw, their_turn], raw_specs, fast, None, shape, 0, RAW_ROWS, UNIT
    )
    for span, slow in zip(spans, arrived):
        pack = span[2] // UNIT * PACK
        specs = [pl.BlockSpec((pack, LANES), lambda i: (i, 0))]
        result = fill_rows(place_kernel, plan, [slow], specs, fast, result, shape, *span)
    return result, off_ratio


def solution(mesh):
    in_specs = (P("rows", "blk"), P())
    out_specs = (P("rows", "blk"), P())
    return jax.shard_map(
        on_device, mesh=mesh, in_specs=in_specs, out_specs=out_specs, check_vma=False
    )
```

```python
import functools

import jax
import jax.numpy as jnp
from jax import lax
from jax.experimental import pallas as pl
from jax.experimental.pallas import tpu as pltpu
from jax.sharding import PartitionSpec as P

ROUNDS = 24
LANES = 128
SUBS = 8
UNIT = 512
PACK = UNIT + UNIT // 2
GRAM_TILE = 512
RAW_ROWS = 1536
FIRST_ROWS = 3072
ROTATE_TILE = 1536
FILL_TILE = 512
VMEM_LIMIT = 32 * 1024 * 1024
GRAM_VMEM_LIMIT = 58 * 1024 * 1024


def split_three(values):
    high = values.astype(jnp.bfloat16)
    rest = values - high.astype(jnp.float32)
    middle = rest.astype(jnp.bfloat16)
    low = (rest - middle.astype(jnp.float32)).astype(jnp.bfloat16)
    return high, middle, low


def dot32(left, right, dims=((1,), (0,))):
    return lax.dot_general(left, right, (dims, ((), ())), preferred_element_type=jnp.float32)


def slot_of_row(rows, groups, half):
    part = rows // half
    inside = rows % half
    index = (inside % SUBS) * groups + inside // SUBS
    return jnp.where(part == 0, index, 2 * half - 1 - index)


def slot_of_lane(lanes, half):
    part = lanes // (2 * LANES)
    odd = (lanes // LANES) % 2
    inside = lanes % LANES
    index = 2 * inside + odd
    slot = jnp.where(part == 0, index, 2 * half - 1 - index)
    return jnp.where(inside < half // 2, slot, -1)


def onehot(left, right):
    return jnp.where(left == right, 1.0, 0.0).astype(jnp.bfloat16)


def angles(head, tail, coupling):
    difference = head - tail
    sign_val = jnp.where(difference >= 0.0, 1.0, -1.0)
    across = 2.0 * coupling * sign_val
    along = jnp.abs(difference)
    scale = jnp.maximum(along, jnp.abs(across))
    empty = scale == 0.0
    inverse = 1.0 / jnp.where(empty, 1.0, scale)
    along = jnp.where(empty, 1.0, along * inverse)
    across = across * inverse
    square = along * along + across * across
    root = lax.rsqrt(square)
    root = root * (1.5 - 0.5 * square * root * root)
    cos_sq = 0.5 + 0.5 * (along * root)
    half_root = lax.rsqrt(cos_sq)
    half_root = half_root * (1.5 - 0.5 * cos_sq * half_root * half_root)
    return cos_sq * half_root, 0.5 * (across * root) * half_root


def full_gram(packed):
    first = packed[:LANES]
    block01, block02 = first[:, LANES : 2 * LANES], first[:, 2 * LANES :]
    block12 = packed[LANES:, LANES : 2 * LANES]
    second = jnp.concatenate([block01.T, packed[LANES:, : 2 * LANES]], axis=1)
    third = jnp.concatenate([block02.T, block12.T, packed[LANES:, 2 * LANES :]], axis=1)
    return jnp.concatenate([first, second, third], axis=0)


def send_columns(lanes, base, slot, width):
    section = lanes // LANES
    lane = lanes % LANES
    rest = width - LANES
    main_start = base + jnp.where(slot == 0, 0, rest)
    rest_start = base + jnp.where(slot == 0, LANES, 0)
    high = (section // 2 + slot) % 2
    inside = lane - high * (LANES - rest)
    mixed = jnp.where((inside >= 0) & (inside < rest), rest_start + inside, -1)
    return jnp.where(section == 1, main_start + lane, mixed)


def moves(plan_ref):
    count = plan_ref.shape[0] // 2
    position = lax.axis_index("blk")
    slow_dev = lax.rem(position + 2 * lax.rem(position, 2) - 1 + count, count)
    mine = plan_ref[2 * position], plan_ref[2 * position + 1]
    theirs = plan_ref[2 * slow_dev], plan_ref[2 * slow_dev + 1]
    first_slow = mine[0] // 2 == slow_dev
    slow_slot = lax.rem(jnp.where(first_slow, mine[0], mine[1]), 2)
    fast_slot = lax.rem(jnp.where(first_slow, mine[1], mine[0]), 2)
    in_slot = lax.rem(jnp.where(theirs[0] // 2 == position, theirs[0], theirs[1]), 2)
    return first_slow, slow_slot, fast_slot, in_slot


def jacobi_kernel(plan_ref, *refs):
    jacobi_body(plan_ref, refs[:-9], *refs[-9:])


def jacobi_body(
    plan_ref, gram_refs, slow_ref, fast_ref, send_ref,
    gram_a, gram_b, basis_a, basis_b, cos_buf, sin_buf,
):
    size = gram_refs[0].shape[1]
    half = size // 2
    groups = half // SUBS
    last = groups - 1
    edge = half // 2 - 1
    lane_row = lax.broadcasted_iota(jnp.int32, (1, LANES), 1)
    lane = lax.broadcasted_iota(jnp.int32, (SUBS, LANES), 1)
    sub = lax.broadcasted_iota(jnp.int32, (SUBS, LANES), 0)
    spot = lane - sub * (groups // 2)

    def on_diag(group):
        return spot == group // 2

    row_slot = slot_of_row(lax.broadcasted_iota(jnp.int32, (size, 1), 0), groups, half)
    take_rows = onehot(row_slot, lax.broadcasted_iota(jnp.int32, (size, size), 1))
    lane_slot = slot_of_lane(lax.broadcasted_iota(jnp.int32, (1, 4 * LANES), 1), half)
    take_cols = onehot(lax.broadcasted_iota(jnp.int32, (size, 4 * LANES), 0), lane_slot)
    arranged = jnp.zeros((size, 4 * LANES), jnp.float32)
    packed = gram_refs[0][...]
    for other in gram_refs[1:]:
        packed = packed + other[...]
    gram_sum = full_gram(packed)
    for piece in split_three(gram_sum):
        moved = dot32(take_rows, piece).astype(jnp.bfloat16)
        arranged = arranged + dot32(moved, take_cols)
    gram_a[...] = arranged.reshape(2, groups, SUBS, 4 * LANES)
    basis_a[...] = take_rows.astype(jnp.float32).reshape(2, groups, SUBS, size)

    zero = jnp.zeros((SUBS, LANES), jnp.float32)
    heads, tails, couplings = [zero, zero], [zero, zero], [zero, zero]
    for group in range(groups):
        odd = group % 2
        mask = on_diag(group)
        lead_cols = slice(odd * LANES, (odd + 1) * LANES)
        tail_cols = slice((2 + odd) * LANES, (3 + odd) * LANES)
        heads[odd] += jnp.where(mask, gram_a[0, group, :, lead_cols], 0.0)
        tails[odd] += jnp.where(mask, gram_a[1, group, :, tail_cols], 0.0)
        couplings[odd] += jnp.where(mask, gram_a[0, group, :, tail_cols], 0.0)

    def flat(values):
        return jnp.sum(values, axis=0, keepdims=True)

    def shift_lanes(lead, tail):
        lead0, lead1 = lead[:, :LANES], lead[:, LANES:]
        tail0, tail1 = tail[:, :LANES], tail[:, LANES:]
        here = lane[: lead.shape[0]]
        new_lead1 = jnp.where(here == 0, tail0, lead0)
        new_lead0 = jnp.where(here == 0, lead0, pltpu.roll(lead1, 1, 1))
        new_tail1 = jnp.where(here == edge, lead1, pltpu.roll(tail0, LANES - 1, 1))
        return new_lead0, new_lead1, tail1, new_tail1

    def turn(gram_from, gram_to, basis_from, basis_to, carry):
        heads, tails, couplings = carry
        cosines, sines, new_heads, new_tails = [], [], [], []
        for odd in range(2):
            head, tail = heads[odd], tails[odd]
            coupling = flat(couplings[odd])
            cosine, sine_val = angles(head, tail, coupling)
            cosines.append(cosine)
            sines.append(sine_val)
            first = cosine * head + sine_val * coupling
            second = cosine * coupling + sine_val * tail
            new_heads.append(cosine * first + sine_val * second)
            first = cosine * coupling - sine_val * head
            second = cosine * tail - sine_val * coupling
            new_tails.append(cosine * second - sine_val * first)
        shifted_diag = shift_lanes(
            jnp.concatenate([jnp.broadcast_to(x, (SUBS, LANES)) for x in new_heads], axis=1),
            jnp.concatenate([jnp.broadcast_to(x, (SUBS, LANES)) for x in new_tails], axis=1),
        )
        shifted_diag = [x[:1] for x in shifted_diag]
        cos_lanes = [jnp.broadcast_to(x, (SUBS, LANES)) for x in cosines]
        sin_lanes = [jnp.broadcast_to(x, (SUBS, LANES)) for x in sines]
        cos_wide = jnp.concatenate(cos_lanes, axis=1)
        sin_wide = jnp.concatenate(sin_lanes, axis=1)

        for group in range(groups):
            mask = on_diag(group)
            odd = group % 2
            for buf, lanes in ((cos_buf, cos_lanes[odd]), (sin_buf, sin_lanes[odd])):
                picked = jnp.sum(jnp.where(mask, lanes, 0.0), axis=1, keepdims=True)
                buf[group] = jnp.broadcast_to(picked, (SUBS, LANES))

        def work(group):
            cos_row = jnp.concatenate([cos_buf[group]] * 2, axis=1)
            sin_row = jnp.concatenate([sin_buf[group]] * 2, axis=1)
            cos_base = jnp.concatenate([cos_buf[group]] * (size // LANES), axis=1)
            sin_base = jnp.concatenate([sin_buf[group]] * (size // LANES), axis=1)

            def turned(part):
                values = gram_from[part, group]
                lead, tail = values[:, : 2 * LANES], values[:, 2 * LANES :]
                return cos_wide * lead + sin_wide * tail, cos_wide * tail - sin_wide * lead

            top_lead, top_tail = turned(0)
            low_lead, low_tail = turned(1)
            top = shift_lanes(
                cos_row * top_lead + sin_row * low_lead, cos_row * top_tail + sin_row * low_tail
            )
            low = shift_lanes(
                cos_row * low_lead - sin_row * top_lead, cos_row * low_tail - sin_row * top_tail
            )
            lead = basis_from[0, group]
            tail = basis_from[1, group]
            base_top = cos_base * lead + sin_base * tail
            base_low = cos_base * tail - sin_base * lead
            return (
                list(top) + [base_top[:, i : i + LANES] for i in range(0, size, LANES)],
                list(low) + [base_low[:, i : i + LANES] for i in range(0, size, LANES)],
            )

        sums = [zero, zero]

        def store(part, group, values):
            for index, value in enumerate(values[:4]):
                gram_to[part, group, :, index * LANES : (index + 1) * LANES] = value
            for index, value in enumerate(values[4:]):
                basis_to[part, group, :, index * LANES : (index + 1) * LANES] = value
            if part == 0:
                odd = group % 2
                sums[odd] += jnp.where(on_diag(group), values[2 + odd], 0.0)

        first_top, first_low = work(0)
        last_top, last_low = work(last)
        store(0, 1, [jnp.where(sub == 0, y, x) for x, y in zip(first_top, first_low)])
        store(0, 0, [jnp.where(sub == 0, x, pltpu.roll(y, 1, 0)) for x, y in zip(first_top, last_top)])
        store(1, last, [
            jnp.where(sub == SUBS - 1, y, pltpu.roll(x, SUBS - 1, 0))
            for x, y in zip(first_low, last_top)
        ])
        store(1, last - 1, last_low)
        for group in range(1, last):
            top, low = work(group)
            store(0, group + 1, top)
            store(1, group - 1, low)
        return (
            (shifted_diag[0], shifted_diag[1]), (shifted_diag[2], shifted_diag[3]), tuple(sums)
        )

    start = (
        tuple(flat(x) for x in heads), tuple(flat(x) for x in tails), tuple(couplings)
    )

    def two_turns(_, carry):
        carry = turn(gram_a, gram_b, basis_a, basis_b, carry)
        return turn(gram_b, gram_a, basis_b, basis_a, carry)

    lax.fori_loop(0, ROUNDS // 2, two_turns, start)

    held = jnp.where(row_slot == 0, 0, 1 + (row_slot + (size - 2 - ROUNDS % (size - 1))) % (size - 1))
    basis = basis_a[...].reshape(size, size).astype(jnp.bfloat16)
    lanes = lax.broadcasted_iota(jnp.int32, (1, size), 1)
    first_slow, slow_slot, fast_slot, _ = moves(plan_ref)
    slow_base = jnp.where(first_slow, 0, half)
    for ref, base, slot in ((slow_ref, slow_base, slow_slot), (fast_ref, half - slow_base, fast_slot)):
        wanted = send_columns(lanes, base, slot, half)
        ref[...] = dot32(basis, onehot(held, wanted), ((0,), (0,))).astype(jnp.bfloat16)
    send_ref[...] = slow_ref[:, : 2 * LANES]


def jacobi(plan, grams):
    size = grams[0].shape[1]
    groups = size // 2 // SUBS
    return pl.pallas_call(
        jacobi_kernel,
        out_shape=(
            jax.ShapeDtypeStruct((size, size), jnp.bfloat16),
            jax.ShapeDtypeStruct((size, size), jnp.bfloat16),
            jax.ShapeDtypeStruct((size, 2 * LANES), jnp.bfloat16),
        ),
        in_specs=[pl.BlockSpec(memory_space=pltpu.SMEM)]
        + [pl.BlockSpec(memory_space=pltpu.VMEM)] * len(grams),
        out_specs=[pl.BlockSpec(memory_space=pltpu.VMEM)] * 3,
        scratch_shapes=[
            pltpu.VMEM((2, groups, SUBS, 4 * LANES), jnp.float32),
            pltpu.VMEM((2, groups, SUBS, 4 * LANES), jnp.float32),
            pltpu.VMEM((2, groups, SUBS, size), jnp.float32),
            pltpu.VMEM((2, groups, SUBS, size), jnp.float32),
            pltpu.VMEM((groups, SUBS, LANES), jnp.float32),
            pltpu.VMEM((groups, SUBS, LANES), jnp.float32),
        ],
        compiler_params=pltpu.CompilerParams(vmem_limit_bytes=VMEM_LIMIT),
        cost_estimate=pl.CostEstimate(
            flops=ROUNDS * 600 * size * size, bytes_accessed=8 * size * size, transcendentals=0
        ),
        name="jacobi_turns",
    )(plan, *grams)


def sums_kernel(*refs):
    sums_ref = refs[-1]
    packed = refs[0][...]
    for other in refs[1:-1]:
        packed = packed + other[...]
    squares = packed * packed
    total = jnp.zeros((1, 1), jnp.float32)
    diag_sq = jnp.zeros((1, 1), jnp.float32)
    rows = lax.broadcasted_iota(jnp.int32, (LANES, LANES), 0)
    cols = lax.broadcasted_iota(jnp.int32, (LANES, LANES), 1)
    for row, col, weight in (
        (0, 0, 1.0), (0, 1, 2.0), (0, 2, 2.0), (1, 0, 1.0), (1, 1, 2.0), (1, 2, 1.0)
    ):
        block = squares[row * LANES : (row + 1) * LANES, col * LANES : (col + 1) * LANES]
        total = total + weight * jnp.sum(block, keepdims=True)
        if weight == 1.0:
            diag_sq = diag_sq + jnp.sum(jnp.where(rows == cols, block, 0.0), keepdims=True)
    sub = lax.broadcasted_iota(jnp.int32, (SUBS, LANES), 0)
    sums_ref[...] = jnp.where(sub == 0, total - diag_sq, diag_sq)


def gram_sums(grams):
    return pl.pallas_call(
        sums_kernel,
        out_shape=jax.ShapeDtypeStruct((SUBS, LANES), jnp.float32),
        in_specs=[pl.BlockSpec(memory_space=pltpu.VMEM)] * len(grams),
        out_specs=pl.BlockSpec(memory_space=pltpu.VMEM),
        name="gram_sums",
    )(*grams)


def gram_kernel(matrix_ref, packed_ref, raw_ref, held, upper_ref, corner_ref, sems, raw_sem):
    rows = held.shape[0]
    copies = []
    for index in range(rows // GRAM_TILE):
        part = pl.ds(index * GRAM_TILE, GRAM_TILE)
        copies.append(pltpu.make_async_copy(matrix_ref.at[part], held.at[part], sems.at[index]))
        copies[-1].start()
    early = pl.ds(0, RAW_ROWS)
    leave = pltpu.make_async_copy(held.at[early], raw_ref, raw_sem)
    for index, copy in enumerate(copies):
        copy.wait()
        if (index + 1) * GRAM_TILE == RAW_ROWS:
            leave.start()
        values = held[index * GRAM_TILE : (index + 1) * GRAM_TILE]
        right = values[:, 2 * LANES :]
        upper = dot32(values[:, : 2 * LANES], values, ((0,), (0,)))
        corner = dot32(right, right, ((0,), (0,)))
        if index == 0:
            upper_ref[...] = upper
            corner_ref[...] = corner
        else:
            upper_ref[...] += upper
            corner_ref[...] += corner
    packed_ref[:LANES] = upper_ref[:LANES]
    packed_ref[LANES:, : 2 * LANES] = upper_ref[LANES:, LANES:]
    packed_ref[LANES:, 2 * LANES :] = corner_ref[...]
    leave.wait()


def gram_blocks(matrix):
    rows, size = matrix.shape
    return pl.pallas_call(
        gram_kernel,
        in_specs=[pl.BlockSpec(memory_space=pl.ANY)],
        out_specs=[pl.BlockSpec(memory_space=pltpu.VMEM), pl.BlockSpec(memory_space=pl.ANY)],
        out_shape=(
            jax.ShapeDtypeStruct((2 * LANES, size), jnp.float32),
            jax.ShapeDtypeStruct((RAW_ROWS, size), jnp.bfloat16),
        ),
        scratch_shapes=[
            pltpu.VMEM((rows, size), jnp.bfloat16),
            pltpu.VMEM((2 * LANES, size), jnp.float32),
            pltpu.VMEM((LANES, LANES), jnp.float32),
            pltpu.SemaphoreType.DMA((rows // GRAM_TILE,)),
            pltpu.SemaphoreType.DMA,
        ],
        compiler_params=pltpu.CompilerParams(vmem_limit_bytes=GRAM_VMEM_LIMIT),
        cost_estimate=pl.CostEstimate(
            flops=2 * rows * size * size, bytes_accessed=2 * rows * size, transcendentals=0
        ),
        name="gram_blocks",
    )(matrix)


def pack_unit(values, turn, packed_ref, at):
    half = UNIT // 2
    top = dot32(values[:half], turn[:, : 2 * LANES])
    low = dot32(values[half:], turn[:, LANES:])
    packed_ref[at : at + half] = top[:, LANES:].astype(jnp.bfloat16)
    packed_ref[at + half : at + UNIT] = low[:, :LANES].astype(jnp.bfloat16)
    packed_ref[at + UNIT : at + PACK] = (top[:, :LANES] + low[:, LANES:]).astype(jnp.bfloat16)


def rotate_kernel(ranges, matrix_ref, slow_ref, fast_ref, fast_pack_ref, *slow_packs):
    step = pl.program_id(0)
    units = matrix_ref.shape[0] // UNIT
    for unit in range(units):
        values = matrix_ref[unit * UNIT : (unit + 1) * UNIT]
        pack_unit(values, fast_ref[...], fast_pack_ref, unit * PACK)
    for (first, count), pack_ref in zip(ranges, slow_packs):
        @pl.when((step >= first) & (step < first + count))
        def _(pack_ref=pack_ref):
            for unit in range(units):
                values = matrix_ref[unit * UNIT : (unit + 1) * UNIT]
                pack_unit(values, slow_ref[...], pack_ref, unit * PACK)


def rotate_all(matrix, slow_turn, fast_turn, spans):
    rows, size = matrix.shape
    pack = ROTATE_TILE // UNIT * PACK
    ranges = [(start // ROTATE_TILE, count // ROTATE_TILE) for start, count, _ in spans]
    packs = [rows] + [count for _, count, _ in spans]
    turn_spec = pl.BlockSpec((size, size), lambda i: (0, 0))

    def slow_spec(first, count):
        return pl.BlockSpec((pack, LANES), lambda i: (jnp.clip(i - first, 0, count - 1), 0))

    return pl.pallas_call(
        functools.partial(rotate_kernel, ranges),
        grid=(rows // ROTATE_TILE,),
        in_specs=[pl.BlockSpec((ROTATE_TILE, size), lambda i: (i, 0)), turn_spec, turn_spec],
        out_specs=[pl.BlockSpec((pack, LANES), lambda i: (i, 0))]
        + [slow_spec(*part) for part in ranges],
        out_shape=[
            jax.ShapeDtypeStruct((count // UNIT * PACK, LANES), jnp.bfloat16) for count in packs
        ],
        compiler_params=pltpu.CompilerParams(vmem_limit_bytes=VMEM_LIMIT),
        cost_estimate=pl.CostEstimate(
            flops=8 * rows * size * LANES, bytes_accessed=6 * rows * size, transcendentals=0
        ),
        name="rotate_rows",
    )(matrix, slow_turn, fast_turn)


def place_main(slot, out_ref, rows, slow_main, fast_main):
    @pl.when(slot == 0)
    def _():
        out_ref[rows, :LANES] = slow_main
        out_ref[rows, 2 * LANES :] = fast_main

    @pl.when(slot != 0)
    def _():
        out_ref[rows, :LANES] = fast_main
        out_ref[rows, 2 * LANES :] = slow_main


def slot_lanes(slot):
    lane = lax.broadcasted_iota(jnp.int32, (UNIT // 2, LANES), 1)
    return (lane // (LANES // 2)) == slot


def place_kernel(plan_ref, slow_ref, fast_ref, *refs):
    out_ref = refs[-1]
    half = UNIT // 2
    slot = moves(plan_ref)[3]
    mask = slot_lanes(slot)
    middle = slice(LANES, 2 * LANES)
    for unit in range(out_ref.shape[0] // UNIT):
        start, at = unit * UNIT, unit * PACK
        main, rest = slice(at, at + UNIT), slice(at + UNIT, at + PACK)
        place_main(slot, out_ref, slice(start, start + UNIT), slow_ref[main], fast_ref[main])
        slow = slow_ref[rest].astype(jnp.float32)
        fast = fast_ref[rest].astype(jnp.float32)
        out_ref[start : start + half, middle] = jnp.where(mask, slow, fast).astype(jnp.bfloat16)
        swapped = pltpu.roll(jnp.where(mask, fast, slow), LANES // 2, 1)
        out_ref[start + half : start + UNIT, middle] = swapped.astype(jnp.bfloat16)


def raw_kernel(plan_ref, raw_ref, turn_ref, fast_ref, *refs):
    out_ref = refs[-1]
    half = UNIT // 2
    slot = moves(plan_ref)[3]
    mask = slot_lanes(slot)
    middle = slice(LANES, 2 * LANES)
    for unit in range(out_ref.shape[0] // UNIT):
        start, at = unit * UNIT, unit * PACK
        rows = slice(start, start + UNIT)
        turned = dot32(raw_ref[rows], turn_ref[...])
        main = turned[:, LANES:].astype(jnp.bfloat16)
        place_main(slot, out_ref, rows, main, fast_ref[at : at + UNIT])
        fast = fast_ref[at + UNIT : at + PACK].astype(jnp.float32)
        top = jnp.where(mask, turned[:half, :LANES], fast)
        out_ref[start : start + half, middle] = top.astype(jnp.bfloat16)
        low = jnp.where(mask, turned[half:, :LANES], pltpu.roll(fast, LANES // 2, 1))
        out_ref[start + half : start + UNIT, middle] = low.astype(jnp.bfloat16)


def fill_rows(kernel, plan, sources, specs, fast, held, shape, start, count, tile):
    first = start // tile
    pack = tile // UNIT * PACK
    operands = [plan, *sources, fast]
    in_specs = [
        pl.BlockSpec(memory_space=pltpu.SMEM),
        *specs,
        pl.BlockSpec((pack, LANES), lambda i: (first + i, 0)),
    ]
    aliases = {}
    if held is not None:
        aliases = {len(operands): 0}
        operands.append(held)
        in_specs.append(pl.BlockSpec(memory_space=pl.ANY))
    return pl.pallas_call(
        kernel,
        grid=(count // tile,),
        in_specs=in_specs,
        out_specs=pl.BlockSpec((tile, shape[1]), lambda i: (first + i, 0)),
        out_shape=jax.ShapeDtypeStruct(shape, jnp.bfloat16),
        input_output_aliases=aliases,
        compiler_params=pltpu.CompilerParams(vmem_limit_bytes=VMEM_LIMIT),
        cost_estimate=pl.CostEstimate(
            flops=count * shape[1], bytes_accessed=4 * count * shape[1], transcendentals=0
        ),
        name="fill_rows",
    )(*operands)


def swapped_with(value, axis, partner):
    count = lax.axis_size(axis)
    return lax.ppermute(value, axis, [(source, partner(source, count)) for source in range(count)])


def slow_partner(source, count):
    return (source + 1) % count if source % 2 else (source + count - 1) % count


def fast_partner(source, count):
    return source ^ 1


def add_swapped(values, step):
    return values + swapped_with(values, "blk", lambda source, _: source ^ step)


def on_device(matrix, plan):
    rows, size = matrix.shape
    own, early = gram_blocks(matrix)
    if lax.axis_size("rows") == 2:
        grams = [own, swapped_with(own, "rows", fast_partner)]
    else:
        grams = [lax.psum(own, "rows")]
    raw = swapped_with(early, "blk", slow_partner)
    totals = add_swapped(gram_sums(grams), 2)
    slow_turn, fast_turn, send_turn = jacobi(plan, grams)
    slow_turn, totals = lax.optimization_barrier((slow_turn, totals))

    their_turn = swapped_with(send_turn, "blk", slow_partner)
    last_rows = rows - RAW_ROWS - FIRST_ROWS
    spans = [(RAW_ROWS, FIRST_ROWS, ROTATE_TILE), (RAW_ROWS + FIRST_ROWS, last_rows, FILL_TILE)]
    fast_pack, *packs = rotate_all(matrix, slow_turn, fast_turn, spans)
    arrived = [swapped_with(pack, "blk", slow_partner) for pack in packs]
    fast_pack, raw = lax.optimization_barrier((fast_pack, raw))
    fast = swapped_with(fast_pack, "blk", fast_partner)
    step = 1
    while step < lax.axis_size("blk"):
        if step != 2:
            totals = add_swapped(totals, step)
        step *= 2
    off_ratio = jnp.sqrt(totals[0, 0] / totals[1, 0])

    shape = (rows, size)
    raw_specs = [
        pl.BlockSpec((UNIT, size), lambda i: (i, 0)),
        pl.BlockSpec((size, 2 * LANES), lambda i: (0, 0)),
    ]
    result = fill_rows(
        raw_kernel, plan, [raw, their_turn], raw_specs, fast, None, shape, 0, RAW_ROWS, UNIT
    )
    for span, slow in zip(spans, arrived):
        pack = span[2] // UNIT * PACK
        specs = [pl.BlockSpec((pack, LANES), lambda i: (i, 0))]
        result = fill_rows(place_kernel, plan, [slow], specs, fast, result, shape, *span)
    return result, off_ratio


def solution(mesh):
    in_specs = (P("rows", "blk"), P())
    out_specs = (P("rows", "blk"), P())
    return jax.shard_map(
        on_device, mesh=mesh, in_specs=in_specs, out_specs=out_specs, check_vma=False
    )
```

```python
import jax
import jax.numpy as jnp
from jax import lax
from jax.experimental import pallas as pl
from jax.experimental.pallas import tpu as pltpu
from jax.sharding import PartitionSpec as P

ROUNDS = 24
LANES = 128
SUBS = 8
UNIT = 512
PACK = UNIT + UNIT // 2
GRAM_TILE = 512
RAW_ROWS = 1536
LAST_ROWS = 1024
IN_FLIGHT = 3
VMEM_LIMIT = 32 * 1024 * 1024
JACOBI_VMEM_LIMIT = 30 * 1024 * 1024
GRAM_VMEM_LIMIT = 58 * 1024 * 1024


def split_three(values):
    high = values.astype(jnp.bfloat16)
    rest = values - high.astype(jnp.float32)
    middle = rest.astype(jnp.bfloat16)
    low = (rest - middle.astype(jnp.float32)).astype(jnp.bfloat16)
    return high, middle, low


def dot32(left, right, dims=((1,), (0,))):
    return lax.dot_general(left, right, (dims, ((), ())), preferred_element_type=jnp.float32)


def slot_of_row(rows, groups, half):
    part = rows // half
    inside = rows % half
    index = (inside % SUBS) * groups + inside // SUBS
    return jnp.where(part == 0, index, 2 * half - 1 - index)


def slot_of_lane(lanes, half):
    part = lanes // (2 * LANES)
    odd = (lanes // LANES) % 2
    inside = lanes % LANES
    index = 2 * inside + odd
    slot = jnp.where(part == 0, index, 2 * half - 1 - index)
    return jnp.where(inside < half // 2, slot, -1)


def onehot(left, right):
    return jnp.where(left == right, 1.0, 0.0).astype(jnp.bfloat16)


def angles(head, tail, coupling):
    difference = head - tail
    sign_val = jnp.where(difference >= 0.0, 1.0, -1.0)
    across = 2.0 * coupling * sign_val
    along = jnp.abs(difference)
    scale = jnp.maximum(along, jnp.abs(across))
    empty = scale == 0.0
    inverse = 1.0 / jnp.where(empty, 1.0, scale)
    along = jnp.where(empty, 1.0, along * inverse)
    across = across * inverse
    square = along * along + across * across
    root = lax.rsqrt(square)
    root = root * (1.5 - 0.5 * square * root * root)
    cos_sq = 0.5 + 0.5 * (along * root)
    half_root = lax.rsqrt(cos_sq)
    half_root = half_root * (1.5 - 0.5 * cos_sq * half_root * half_root)
    return cos_sq * half_root, 0.5 * (across * root) * half_root


def full_gram(packed):
    first = packed[:LANES]
    block01, block02 = first[:, LANES : 2 * LANES], first[:, 2 * LANES :]
    block12 = packed[LANES:, LANES : 2 * LANES]
    second = jnp.concatenate([block01.T, packed[LANES:, : 2 * LANES]], axis=1)
    third = jnp.concatenate([block02.T, block12.T, packed[LANES:, 2 * LANES :]], axis=1)
    return jnp.concatenate([first, second, third], axis=0)


def send_columns(lanes, base, slot, width):
    section = lanes // LANES
    lane = lanes % LANES
    rest = width - LANES
    main_start = base + jnp.where(slot == 0, 0, rest)
    rest_start = base + jnp.where(slot == 0, LANES, 0)
    high = (section // 2 + slot) % 2
    inside = lane - high * (LANES - rest)
    mixed = jnp.where((inside >= 0) & (inside < rest), rest_start + inside, -1)
    return jnp.where(section == 1, main_start + lane, mixed)


def block_sums(packed):
    squares = packed * packed
    total = jnp.zeros((1, 1), jnp.float32)
    diag_sq = jnp.zeros((1, 1), jnp.float32)
    rows = lax.broadcasted_iota(jnp.int32, (LANES, LANES), 0)
    cols = lax.broadcasted_iota(jnp.int32, (LANES, LANES), 1)
    for row, col, weight in (
        (0, 0, 1.0), (0, 1, 2.0), (0, 2, 2.0), (1, 0, 1.0), (1, 1, 2.0), (1, 2, 1.0)
    ):
        block = squares[row * LANES : (row + 1) * LANES, col * LANES : (col + 1) * LANES]
        total = total + weight * jnp.sum(block, keepdims=True)
        if weight == 1.0:
            diag_sq = diag_sq + jnp.sum(jnp.where(rows == cols, block, 0.0), keepdims=True)
    sub = lax.broadcasted_iota(jnp.int32, (SUBS, LANES), 0)
    return jnp.where(sub == 0, total - diag_sq, diag_sq)


def pack_unit(values, turn, packed_ref, at):
    half = UNIT // 2
    top = dot32(values[:half], turn[:, : 2 * LANES])
    low = dot32(values[half:], turn[:, LANES:])
    packed_ref[at : at + half] = top[:, LANES:].astype(jnp.bfloat16)
    packed_ref[at + half : at + UNIT] = low[:, :LANES].astype(jnp.bfloat16)
    packed_ref[at + UNIT : at + PACK] = (top[:, :LANES] + low[:, LANES:]).astype(jnp.bfloat16)


def moves(plan_ref):
    count = plan_ref.shape[0] // 2
    position = lax.axis_index("blk")
    slow_dev = lax.rem(position + 2 * lax.rem(position, 2) - 1 + count, count)
    mine = plan_ref[2 * position], plan_ref[2 * position + 1]
    theirs = plan_ref[2 * slow_dev], plan_ref[2 * slow_dev + 1]
    first_slow = mine[0] // 2 == slow_dev
    slow_slot = lax.rem(jnp.where(first_slow, mine[0], mine[1]), 2)
    fast_slot = lax.rem(jnp.where(first_slow, mine[1], mine[0]), 2)
    in_slot = lax.rem(jnp.where(theirs[0] // 2 == position, theirs[0], theirs[1]), 2)
    return first_slow, slow_slot, fast_slot, in_slot


def jacobi_kernel(plan_ref, *refs):
    jacobi_body(plan_ref, refs[:-14], *refs[-14:])


def jacobi_body(
    plan_ref, gram_refs, matrix_ref, first_ref, last_ref, fast_ref, sums_ref,
    gram_a, gram_b, basis_a, basis_b, cos_buf, sin_buf, held, packs, sems,
):
    matrix_copy = pltpu.make_async_copy(matrix_ref.at[pl.ds(RAW_ROWS, held.shape[0])], held, sems.at[0])
    matrix_copy.start()
    size = gram_refs[0].shape[1]
    half = size // 2
    groups = half // SUBS
    last = groups - 1
    edge = half // 2 - 1
    lane_row = lax.broadcasted_iota(jnp.int32, (1, LANES), 1)
    lane = lax.broadcasted_iota(jnp.int32, (SUBS, LANES), 1)
    sub = lax.broadcasted_iota(jnp.int32, (SUBS, LANES), 0)
    spot = lane - sub * (groups // 2)

    def on_diag(group):
        return spot == group // 2

    row_slot = slot_of_row(lax.broadcasted_iota(jnp.int32, (size, 1), 0), groups, half)
    take_rows = onehot(row_slot, lax.broadcasted_iota(jnp.int32, (size, size), 1))
    lane_slot = slot_of_lane(lax.broadcasted_iota(jnp.int32, (1, 4 * LANES), 1), half)
    take_cols = onehot(lax.broadcasted_iota(jnp.int32, (size, 4 * LANES), 0), lane_slot)
    arranged = jnp.zeros((size, 4 * LANES), jnp.float32)
    packed = gram_refs[0][...]
    for other in gram_refs[1:]:
        packed = packed + other[...]
    gram_sum = full_gram(packed)
    sums_ref[...] = block_sums(packed)
    for piece in split_three(gram_sum):
        moved = dot32(take_rows, piece).astype(jnp.bfloat16)
        arranged = arranged + dot32(moved, take_cols)
    gram_a[...] = arranged.reshape(2, groups, SUBS, 4 * LANES)
    basis_a[...] = take_rows.astype(jnp.float32).reshape(2, groups, SUBS, size)

    zero = jnp.zeros((SUBS, LANES), jnp.float32)
    heads, tails, couplings = [zero, zero], [zero, zero], [zero, zero]
    for group in range(groups):
        odd = group % 2
        mask = on_diag(group)
        lead_cols = slice(odd * LANES, (odd + 1) * LANES)
        tail_cols = slice((2 + odd) * LANES, (3 + odd) * LANES)
        heads[odd] += jnp.where(mask, gram_a[0, group, :, lead_cols], 0.0)
        tails[odd] += jnp.where(mask, gram_a[1, group, :, tail_cols], 0.0)
        couplings[odd] += jnp.where(mask, gram_a[0, group, :, tail_cols], 0.0)

    def flat(values):
        return jnp.sum(values, axis=0, keepdims=True)

    def shift_lanes(lead, tail):
        lead0, lead1 = lead[:, :LANES], lead[:, LANES:]
        tail0, tail1 = tail[:, :LANES], tail[:, LANES:]
        here = lane[: lead.shape[0]]
        new_lead1 = jnp.where(here == 0, tail0, lead0)
        new_lead0 = jnp.where(here == 0, lead0, pltpu.roll(lead1, 1, 1))
        new_tail1 = jnp.where(here == edge, lead1, pltpu.roll(tail0, LANES - 1, 1))
        return new_lead0, new_lead1, tail1, new_tail1

    def turn(gram_from, gram_to, basis_from, basis_to, carry):
        heads, tails, couplings = carry
        cosines, sines, new_heads, new_tails = [], [], [], []
        for odd in range(2):
            head, tail = heads[odd], tails[odd]
            coupling = flat(couplings[odd])
            cosine, sine_val = angles(head, tail, coupling)
            cosines.append(cosine)
            sines.append(sine_val)
            first = cosine * head + sine_val * coupling
            second = cosine * coupling + sine_val * tail
            new_heads.append(cosine * first + sine_val * second)
            first = cosine * coupling - sine_val * head
            second = cosine * tail - sine_val * coupling
            new_tails.append(cosine * second - sine_val * first)
        shifted_diag = shift_lanes(
            jnp.concatenate([jnp.broadcast_to(x, (SUBS, LANES)) for x in new_heads], axis=1),
            jnp.concatenate([jnp.broadcast_to(x, (SUBS, LANES)) for x in new_tails], axis=1),
        )
        shifted_diag = [x[:1] for x in shifted_diag]
        cos_lanes = [jnp.broadcast_to(x, (SUBS, LANES)) for x in cosines]
        sin_lanes = [jnp.broadcast_to(x, (SUBS, LANES)) for x in sines]
        cos_wide = jnp.concatenate(cos_lanes, axis=1)
        sin_wide = jnp.concatenate(sin_lanes, axis=1)

        for group in range(groups):
            mask = on_diag(group)
            odd = group % 2
            for buf, lanes in ((cos_buf, cos_lanes[odd]), (sin_buf, sin_lanes[odd])):
                picked = jnp.sum(jnp.where(mask, lanes, 0.0), axis=1, keepdims=True)
                buf[group] = jnp.broadcast_to(picked, (SUBS, LANES))

        def work(group):
            cos_row = jnp.concatenate([cos_buf[group]] * 2, axis=1)
            sin_row = jnp.concatenate([sin_buf[group]] * 2, axis=1)
            cos_base = jnp.concatenate([cos_buf[group]] * (size // LANES), axis=1)
            sin_base = jnp.concatenate([sin_buf[group]] * (size // LANES), axis=1)

            def turned(part):
                values = gram_from[part, group]
                lead, tail = values[:, : 2 * LANES], values[:, 2 * LANES :]
                return cos_wide * lead + sin_wide * tail, cos_wide * tail - sin_wide * lead

            top_lead, top_tail = turned(0)
            low_lead, low_tail = turned(1)
            top = shift_lanes(
                cos_row * top_lead + sin_row * low_lead, cos_row * top_tail + sin_row * low_tail
            )
            low = shift_lanes(
                cos_row * low_lead - sin_row * top_lead, cos_row * low_tail - sin_row * top_tail
            )
            lead = basis_from[0, group]
            tail = basis_from[1, group]
            base_top = cos_base * lead + sin_base * tail
            base_low = cos_base * tail - sin_base * lead
            return (
                list(top) + [base_top[:, i : i + LANES] for i in range(0, size, LANES)],
                list(low) + [base_low[:, i : i + LANES] for i in range(0, size, LANES)],
            )

        sums = [zero, zero]

        def store(part, group, values):
            for index, value in enumerate(values[:4]):
                gram_to[part, group, :, index * LANES : (index + 1) * LANES] = value
            for index, value in enumerate(values[4:]):
                basis_to[part, group, :, index * LANES : (index + 1) * LANES] = value
            if part == 0:
                odd = group % 2
                sums[odd] += jnp.where(on_diag(group), values[2 + odd], 0.0)

        first_top, first_low = work(0)
        last_top, last_low = work(last)
        store(0, 1, [jnp.where(sub == 0, y, x) for x, y in zip(first_top, first_low)])
        store(0, 0, [jnp.where(sub == 0, x, pltpu.roll(y, 1, 0)) for x, y in zip(first_top, last_top)])
        store(1, last, [
            jnp.where(sub == SUBS - 1, y, pltpu.roll(x, SUBS - 1, 0))
            for x, y in zip(first_low, last_top)
        ])
        store(1, last - 1, last_low)
        for group in range(1, last):
            top, low = work(group)
            store(0, group + 1, top)
            store(1, group - 1, low)
        return (
            (shifted_diag[0], shifted_diag[1]), (shifted_diag[2], shifted_diag[3]), tuple(sums)
        )

    start = (
        tuple(flat(x) for x in heads), tuple(flat(x) for x in tails), tuple(couplings)
    )

    def two_turns(_, carry):
        carry = turn(gram_a, gram_b, basis_a, basis_b, carry)
        return turn(gram_b, gram_a, basis_b, basis_a, carry)

    lax.fori_loop(0, ROUNDS // 2, two_turns, start)

    held_slot = jnp.where(row_slot == 0, 0, 1 + (row_slot + (size - 2 - ROUNDS % (size - 1))) % (size - 1))
    basis = basis_a[...].reshape(size, size).astype(jnp.bfloat16)
    lanes = lax.broadcasted_iota(jnp.int32, (1, size), 1)
    first_slow, slow_slot, fast_slot, _ = moves(plan_ref)
    slow_base = jnp.where(first_slow, 0, half)
    def turned(base, slot):
        place = onehot(held_slot, send_columns(lanes, base, slot, half))
        return dot32(basis, place, ((0,), (0,))).astype(jnp.bfloat16)

    fast_ref[...] = turned(half - slow_base, fast_slot)[:, : 2 * LANES]
    slow = turned(slow_base, slow_slot)
    packs[:size] = slow[:, :LANES]
    packs[size : 2 * size] = slow[:, LANES : 2 * LANES]
    matrix_copy.wait()
    copies = []

    def leave(start, count, ref):
        copies.append(
            pltpu.make_async_copy(packs.at[pl.ds(start, count)], ref, sems.at[1 + len(copies)])
        )
        copies[-1].start()

    first_count = first_ref.shape[0]
    leave(0, PACK, first_ref.at[pl.ds(0, PACK)])
    for unit in range(held.shape[0] // UNIT):
        at = (1 + unit) * PACK
        pack_unit(held[unit * UNIT : (unit + 1) * UNIT], slow, packs, at)
        if at < first_count:
            leave(at, PACK, first_ref.at[pl.ds(at, PACK)])
        else:
            leave(at, PACK, last_ref.at[pl.ds(at - first_count, PACK)])
    for copy in copies:
        copy.wait()


def jacobi(plan, grams, matrix):
    rows, size = matrix.shape
    groups = size // 2 // SUBS
    moved = rows - RAW_ROWS
    blocks = 1 + moved // UNIT
    last = LAST_ROWS // UNIT * PACK
    return pl.pallas_call(
        jacobi_kernel,
        out_shape=(
            jax.ShapeDtypeStruct((blocks * PACK - last, LANES), jnp.bfloat16),
            jax.ShapeDtypeStruct((last, LANES), jnp.bfloat16),
            jax.ShapeDtypeStruct((size, 2 * LANES), jnp.bfloat16),
            jax.ShapeDtypeStruct((SUBS, LANES), jnp.float32),
        ),
        in_specs=[pl.BlockSpec(memory_space=pltpu.SMEM)]
        + [pl.BlockSpec(memory_space=pltpu.VMEM)] * len(grams)
        + [pl.BlockSpec(memory_space=pl.ANY)],
        out_specs=[pl.BlockSpec(memory_space=pl.ANY)] * 2
        + [pl.BlockSpec(memory_space=pltpu.VMEM)] * 2,
        scratch_shapes=[
            pltpu.VMEM((2, groups, SUBS, 4 * LANES), jnp.float32),
            pltpu.VMEM((2, groups, SUBS, 4 * LANES), jnp.float32),
            pltpu.VMEM((2, groups, SUBS, size), jnp.float32),
            pltpu.VMEM((2, groups, SUBS, size), jnp.float32),
            pltpu.VMEM((groups, SUBS, LANES), jnp.float32),
            pltpu.VMEM((groups, SUBS, LANES), jnp.float32),
            pltpu.VMEM((moved, size), jnp.bfloat16),
            pltpu.VMEM((blocks * PACK, LANES), jnp.bfloat16),
            pltpu.SemaphoreType.DMA((1 + blocks,)),
        ],
        compiler_params=pltpu.CompilerParams(vmem_limit_bytes=JACOBI_VMEM_LIMIT),
        cost_estimate=pl.CostEstimate(
            flops=ROUNDS * 600 * size * size, bytes_accessed=4 * rows * size, transcendentals=0
        ),
        name="jacobi_turns",
    )(plan, *grams, matrix)


def gram_kernel(matrix_ref, packed_ref, raw_ref, held, upper_ref, corner_ref, sems, raw_sem):
    rows = held.shape[0]
    copies = []
    for index in range(rows // GRAM_TILE):
        part = pl.ds(index * GRAM_TILE, GRAM_TILE)
        copies.append(pltpu.make_async_copy(matrix_ref.at[part], held.at[part], sems.at[index]))
    for copy in copies[:IN_FLIGHT]:
        copy.start()
    early = pl.ds(0, RAW_ROWS)
    leave = pltpu.make_async_copy(held.at[early], raw_ref, raw_sem)
    for index, copy in enumerate(copies):
        copy.wait()
        if index + IN_FLIGHT < len(copies):
            copies[index + IN_FLIGHT].start()
        if (index + 1) * GRAM_TILE == RAW_ROWS:
            leave.start()
        values = held[index * GRAM_TILE : (index + 1) * GRAM_TILE]
        right = values[:, 2 * LANES :]
        upper = dot32(values[:, : 2 * LANES], values, ((0,), (0,)))
        corner = dot32(right, right, ((0,), (0,)))
        if index == 0:
            upper_ref[...] = upper
            corner_ref[...] = corner
        else:
            upper_ref[...] += upper
            corner_ref[...] += corner
    packed_ref[:LANES] = upper_ref[:LANES]
    packed_ref[LANES:, : 2 * LANES] = upper_ref[LANES:, LANES:]
    packed_ref[LANES:, 2 * LANES :] = corner_ref[...]
    leave.wait()


def gram_blocks(matrix):
    rows, size = matrix.shape
    return pl.pallas_call(
        gram_kernel,
        in_specs=[pl.BlockSpec(memory_space=pl.ANY)],
        out_specs=[pl.BlockSpec(memory_space=pltpu.VMEM), pl.BlockSpec(memory_space=pl.ANY)],
        out_shape=(
            jax.ShapeDtypeStruct((2 * LANES, size), jnp.float32),
            jax.ShapeDtypeStruct((RAW_ROWS, size), jnp.bfloat16),
        ),
        scratch_shapes=[
            pltpu.VMEM((rows, size), jnp.bfloat16),
            pltpu.VMEM((2 * LANES, size), jnp.float32),
            pltpu.VMEM((LANES, LANES), jnp.float32),
            pltpu.SemaphoreType.DMA((rows // GRAM_TILE,)),
            pltpu.SemaphoreType.DMA,
        ],
        compiler_params=pltpu.CompilerParams(vmem_limit_bytes=GRAM_VMEM_LIMIT),
        cost_estimate=pl.CostEstimate(
            flops=2 * rows * size * size, bytes_accessed=2 * rows * size, transcendentals=0
        ),
        name="gram_blocks",
    )(matrix)


def place_main(slot, out_ref, slow_main, fast_main):
    @pl.when(slot == 0)
    def _():
        out_ref[:, :LANES] = slow_main
        out_ref[:, 2 * LANES :] = fast_main

    @pl.when(slot != 0)
    def _():
        out_ref[:, :LANES] = fast_main
        out_ref[:, 2 * LANES :] = slow_main


def fill_kernel(plan_ref, slow_ref, near_ref, near_turn_ref, *refs):
    out_ref = refs[-1]
    half = UNIT // 2
    slot = moves(plan_ref)[3]
    middle = slice(LANES, 2 * LANES)
    near = dot32(near_ref[...], near_turn_ref[...])
    place_main(slot, out_ref, slow_ref[:UNIT], near[:, LANES:].astype(jnp.bfloat16))
    lane = lax.broadcasted_iota(jnp.int32, (half, LANES), 1)
    mask = (lane // (LANES // 2)) == slot
    slow = slow_ref[UNIT:].astype(jnp.float32)
    top = jnp.where(mask, slow, near[:half, :LANES])
    low = jnp.where(mask, pltpu.roll(slow, LANES // 2, 1), near[half:, :LANES])
    out_ref[:half, middle] = top.astype(jnp.bfloat16)
    out_ref[half:, middle] = low.astype(jnp.bfloat16)


def raw_kernel(plan_ref, slow_ref, slow_turn_ref, near_ref, near_turn_ref, out_ref):
    size = slow_ref.shape[1]
    slot = moves(plan_ref)[3]
    near = dot32(near_ref[...], near_turn_ref[...])
    mixed = dot32(slow_ref[...], slow_turn_ref[:size])
    main = dot32(slow_ref[...], slow_turn_ref[size:])
    place_main(slot, out_ref, main.astype(jnp.bfloat16), near[:, LANES:].astype(jnp.bfloat16))
    lane = lax.broadcasted_iota(jnp.int32, mixed.shape, 1)
    mask = (lane // (LANES // 2)) == slot
    middle = jnp.where(mask, mixed, near[:, :LANES])
    out_ref[:, LANES : 2 * LANES] = middle.astype(jnp.bfloat16)


def fill_rows(kernel, plan, sources, specs, near, near_turn, result, start, count):
    shape = near.shape
    first = start // UNIT
    operands = [plan, *sources, near, near_turn]
    row_spec = pl.BlockSpec((UNIT, shape[1]), lambda i: (first + i, 0))
    in_specs = [
        pl.BlockSpec(memory_space=pltpu.SMEM),
        *specs,
        row_spec,
        pl.BlockSpec(near_turn.shape, lambda i: (0, 0)),
    ]
    aliases = {}
    if result is not None:
        aliases = {len(operands): 0}
        operands.append(result)
        in_specs.append(pl.BlockSpec(memory_space=pl.ANY))
    return pl.pallas_call(
        kernel,
        grid=(count // UNIT,),
        in_specs=in_specs,
        out_specs=row_spec,
        out_shape=jax.ShapeDtypeStruct(shape, jnp.bfloat16),
        input_output_aliases=aliases,
        compiler_params=pltpu.CompilerParams(vmem_limit_bytes=VMEM_LIMIT),
        cost_estimate=pl.CostEstimate(
            flops=count * shape[1], bytes_accessed=4 * count * shape[1], transcendentals=0
        ),
        name="fill_rows",
    )(*operands)


def swapped_with(value, axis, partner):
    count = lax.axis_size(axis)
    return lax.ppermute(value, axis, [(source, partner(source, count)) for source in range(count)])


def slow_partner(source, count):
    return (source + 1) % count if source % 2 else (source + count - 1) % count


def fast_partner(source, count):
    return source ^ 1


def permuted(value, pairs):
    return lax.ppermute(value, "blk", pairs)


def cycle_sums(sums):
    count = lax.axis_size("blk")
    outer = [place for place in range(count) if place % 4 in (0, 3)]
    inner = [place for place in range(count) if place % 4 in (1, 2)]
    is_outer = (lax.axis_index("blk") + 1) % 4 < 2
    sums = sums + permuted(sums, [(place, place ^ 1) for place in range(count)])
    sums = sums + permuted(sums, [(place, place ^ 3) for place in outer])
    moved = permuted(sums, [(place, place ^ 1) for place in outer])
    sums = jnp.where(is_outer, sums, moved)
    step = 4
    while step < count:
        sums = sums + permuted(sums, [(place, place ^ step) for place in inner])
        step *= 2
    moved = permuted(sums, [(place, place ^ 1) for place in inner])
    return jnp.where(is_outer, moved, sums)


def on_device(matrix, plan):
    rows, size = matrix.shape
    own, early = gram_blocks(matrix)
    matrix_after = matrix
    if lax.axis_size("rows") == 2:
        other = swapped_with(own, "rows", fast_partner)
        matrix_after, other = lax.optimization_barrier((matrix, other))
        grams = [own, other]
    else:
        grams = [lax.psum(own, "rows")]
    raw = swapped_with(early, "blk", slow_partner)
    near = swapped_with(matrix_after, "blk", fast_partner)
    first, last, near_turn, sums = jacobi(plan, grams, matrix)
    near_turn, sums, raw, near = lax.optimization_barrier((near_turn, sums, raw, near))

    first = swapped_with(first, "blk", slow_partner)
    last = swapped_with(last, "blk", slow_partner)
    near_turn = swapped_with(near_turn, "blk", fast_partner)
    totals = cycle_sums(sums)
    off_ratio = jnp.sqrt(totals[0, 0] / totals[1, 0])

    turn_spec = pl.BlockSpec((PACK, LANES), lambda i: (0, 0))
    raw_spec = pl.BlockSpec((UNIT, size), lambda i: (i, 0))
    first_spec = pl.BlockSpec((PACK, LANES), lambda i: (1 + i, 0))
    last_spec = pl.BlockSpec((PACK, LANES), lambda i: (i, 0))
    middle = rows - RAW_ROWS - LAST_ROWS
    result = fill_rows(
        raw_kernel, plan, [raw, first], [raw_spec, turn_spec], near, near_turn, None, 0, RAW_ROWS
    )
    result = fill_rows(
        fill_kernel, plan, [first], [first_spec], near, near_turn, result, RAW_ROWS, middle
    )
    result = fill_rows(
        fill_kernel, plan, [last], [last_spec], near, near_turn, result, rows - LAST_ROWS, LAST_ROWS
    )
    return result, off_ratio


def solution(mesh):
    in_specs = (P("rows", "blk"), P())
    out_specs = (P("rows", "blk"), P())
    return jax.shard_map(
        on_device, mesh=mesh, in_specs=in_specs, out_specs=out_specs, check_vma=False
    )
```

```python
import jax
import jax.numpy as jnp
from jax import lax
from jax.experimental import pallas as pl
from jax.experimental.pallas import tpu as pltpu
from jax.sharding import PartitionSpec as P

ROUNDS = 24
LANES = 128
SUBS = 8
UNIT = 512
PACK = UNIT + UNIT // 2
GRAM_PARTS = (512, 1024)
GRAM_TILE = 1536
RAW_ROWS = 1536
LAST_ROWS = 2560
IN_FLIGHT = 2
VMEM_LIMIT = 32 * 1024 * 1024
JACOBI_VMEM_LIMIT = 30 * 1024 * 1024
GRAM_VMEM_LIMIT = 58 * 1024 * 1024


def split_three(values):
    high = values.astype(jnp.bfloat16)
    rest = values - high.astype(jnp.float32)
    middle = rest.astype(jnp.bfloat16)
    low = (rest - middle.astype(jnp.float32)).astype(jnp.bfloat16)
    return high, middle, low


def dot32(left, right, dims=((1,), (0,))):
    return lax.dot_general(left, right, (dims, ((), ())), preferred_element_type=jnp.float32)


def slot_of_row(rows, groups, half):
    part = rows // half
    inside = rows % half
    index = (inside % SUBS) * groups + inside // SUBS
    return jnp.where(part == 0, index, 2 * half - 1 - index)


def slot_of_lane(lanes, half):
    part = lanes // (2 * LANES)
    odd = (lanes // LANES) % 2
    inside = lanes % LANES
    index = 2 * inside + odd
    slot = jnp.where(part == 0, index, 2 * half - 1 - index)
    return jnp.where(inside < half // 2, slot, -1)


def onehot(left, right):
    return jnp.where(left == right, 1.0, 0.0).astype(jnp.bfloat16)


def angles(head, tail, coupling):
    difference = head - tail
    sign_val = jnp.where(difference >= 0.0, 1.0, -1.0)
    across = 2.0 * coupling * sign_val
    along = jnp.abs(difference)
    scale = jnp.maximum(along, jnp.abs(across))
    empty = scale == 0.0
    inverse = 1.0 / jnp.where(empty, 1.0, scale)
    along = jnp.where(empty, 1.0, along * inverse)
    across = across * inverse
    square = along * along + across * across
    root = lax.rsqrt(square)
    root = root * (1.5 - 0.5 * square * root * root)
    cos_sq = 0.5 + 0.5 * (along * root)
    half_root = lax.rsqrt(cos_sq)
    half_root = half_root * (1.5 - 0.5 * cos_sq * half_root * half_root)
    return cos_sq * half_root, 0.5 * (across * root) * half_root


def full_gram(packed):
    first = packed[:LANES]
    block01, block02 = first[:, LANES : 2 * LANES], first[:, 2 * LANES :]
    block12 = packed[LANES:, LANES : 2 * LANES]
    second = jnp.concatenate([block01.T, packed[LANES:, : 2 * LANES]], axis=1)
    third = jnp.concatenate([block02.T, block12.T, packed[LANES:, 2 * LANES :]], axis=1)
    return jnp.concatenate([first, second, third], axis=0)


def send_columns(lanes, base, slot, width):
    section = lanes // LANES
    lane = lanes % LANES
    rest = width - LANES
    main_start = base + jnp.where(slot == 0, 0, rest)
    rest_start = base + jnp.where(slot == 0, LANES, 0)
    high = (section // 2 + slot) % 2
    inside = lane - high * (LANES - rest)
    mixed = jnp.where((inside >= 0) & (inside < rest), rest_start + inside, -1)
    return jnp.where(section == 1, main_start + lane, mixed)


def block_sums(packed):
    squares = packed * packed
    total = jnp.zeros((1, 1), jnp.float32)
    diag_sq = jnp.zeros((1, 1), jnp.float32)
    rows = lax.broadcasted_iota(jnp.int32, (LANES, LANES), 0)
    cols = lax.broadcasted_iota(jnp.int32, (LANES, LANES), 1)
    for row, col, weight in (
        (0, 0, 1.0), (0, 1, 2.0), (0, 2, 2.0), (1, 0, 1.0), (1, 1, 2.0), (1, 2, 1.0)
    ):
        block = squares[row * LANES : (row + 1) * LANES, col * LANES : (col + 1) * LANES]
        total = total + weight * jnp.sum(block, keepdims=True)
        if weight == 1.0:
            diag_sq = diag_sq + jnp.sum(jnp.where(rows == cols, block, 0.0), keepdims=True)
    sub = lax.broadcasted_iota(jnp.int32, (SUBS, LANES), 0)
    return jnp.where(sub == 0, total - diag_sq, diag_sq)


def pack_unit(values, turn, packed_ref, at):
    half = UNIT // 2
    top = dot32(values[:half], turn[:, : 2 * LANES])
    low = dot32(values[half:], turn[:, LANES:])
    packed_ref[at : at + half] = top[:, LANES:].astype(jnp.bfloat16)
    packed_ref[at + half : at + UNIT] = low[:, :LANES].astype(jnp.bfloat16)
    packed_ref[at + UNIT : at + PACK] = (top[:, :LANES] + low[:, LANES:]).astype(jnp.bfloat16)


def moves(plan_ref):
    count = plan_ref.shape[0] // 2
    position = lax.axis_index("blk")
    slow_dev = lax.rem(position + 2 * lax.rem(position, 2) - 1 + count, count)
    mine = plan_ref[2 * position], plan_ref[2 * position + 1]
    theirs = plan_ref[2 * slow_dev], plan_ref[2 * slow_dev + 1]
    first_slow = mine[0] // 2 == slow_dev
    slow_slot = lax.rem(jnp.where(first_slow, mine[0], mine[1]), 2)
    fast_slot = lax.rem(jnp.where(first_slow, mine[1], mine[0]), 2)
    in_slot = lax.rem(jnp.where(theirs[0] // 2 == position, theirs[0], theirs[1]), 2)
    return first_slow, slow_slot, fast_slot, in_slot


def jacobi_kernel(plan_ref, *refs):
    jacobi_body(plan_ref, refs[:-14], *refs[-14:])


def jacobi_body(
    plan_ref, gram_refs, matrix_ref, first_ref, last_ref, fast_ref, sums_ref,
    gram_a, gram_b, basis_a, basis_b, cos_buf, sin_buf, held, packs, sems,
):
    matrix_copy = pltpu.make_async_copy(matrix_ref.at[pl.ds(RAW_ROWS, held.shape[0])], held, sems.at[0])
    matrix_copy.start()
    size = gram_refs[0].shape[1]
    half = size // 2
    groups = half // SUBS
    last = groups - 1
    edge = half // 2 - 1
    lane_row = lax.broadcasted_iota(jnp.int32, (1, LANES), 1)
    lane = lax.broadcasted_iota(jnp.int32, (SUBS, LANES), 1)
    sub = lax.broadcasted_iota(jnp.int32, (SUBS, LANES), 0)
    spot = lane - sub * (groups // 2)

    def on_diag(group):
        return spot == group // 2

    row_slot = slot_of_row(lax.broadcasted_iota(jnp.int32, (size, 1), 0), groups, half)
    take_rows = onehot(row_slot, lax.broadcasted_iota(jnp.int32, (size, size), 1))
    lane_slot = slot_of_lane(lax.broadcasted_iota(jnp.int32, (1, 4 * LANES), 1), half)
    take_cols = onehot(lax.broadcasted_iota(jnp.int32, (size, 4 * LANES), 0), lane_slot)
    arranged = jnp.zeros((size, 4 * LANES), jnp.float32)
    packed = gram_refs[0][...]
    for other in gram_refs[1:]:
        packed = packed + other[...]
    gram_sum = full_gram(packed)
    sums_ref[...] = block_sums(packed)
    for piece in split_three(gram_sum):
        moved = dot32(take_rows, piece).astype(jnp.bfloat16)
        arranged = arranged + dot32(moved, take_cols)
    gram_a[...] = arranged.reshape(2, groups, SUBS, 4 * LANES)
    basis_a[...] = take_rows.astype(jnp.float32).reshape(2, groups, SUBS, size)

    zero = jnp.zeros((SUBS, LANES), jnp.float32)
    heads, tails, couplings = [zero, zero], [zero, zero], [zero, zero]
    for group in range(groups):
        odd = group % 2
        mask = on_diag(group)
        lead_cols = slice(odd * LANES, (odd + 1) * LANES)
        tail_cols = slice((2 + odd) * LANES, (3 + odd) * LANES)
        heads[odd] += jnp.where(mask, gram_a[0, group, :, lead_cols], 0.0)
        tails[odd] += jnp.where(mask, gram_a[1, group, :, tail_cols], 0.0)
        couplings[odd] += jnp.where(mask, gram_a[0, group, :, tail_cols], 0.0)

    def flat(values):
        return jnp.sum(values, axis=0, keepdims=True)

    def shift_lanes(lead, tail):
        lead0, lead1 = lead[:, :LANES], lead[:, LANES:]
        tail0, tail1 = tail[:, :LANES], tail[:, LANES:]
        here = lane[: lead.shape[0]]
        new_lead1 = jnp.where(here == 0, tail0, lead0)
        new_lead0 = jnp.where(here == 0, lead0, pltpu.roll(lead1, 1, 1))
        new_tail1 = jnp.where(here == edge, lead1, pltpu.roll(tail0, LANES - 1, 1))
        return new_lead0, new_lead1, tail1, new_tail1

    def turn(gram_from, gram_to, basis_from, basis_to, carry):
        heads, tails, couplings = carry
        cosines, sines, new_heads, new_tails = [], [], [], []
        for odd in range(2):
            head, tail = heads[odd], tails[odd]
            coupling = flat(couplings[odd])
            cosine, sine_val = angles(head, tail, coupling)
            cosines.append(cosine)
            sines.append(sine_val)
            first = cosine * head + sine_val * coupling
            second = cosine * coupling + sine_val * tail
            new_heads.append(cosine * first + sine_val * second)
            first = cosine * coupling - sine_val * head
            second = cosine * tail - sine_val * coupling
            new_tails.append(cosine * second - sine_val * first)
        shifted_diag = shift_lanes(
            jnp.concatenate([jnp.broadcast_to(x, (SUBS, LANES)) for x in new_heads], axis=1),
            jnp.concatenate([jnp.broadcast_to(x, (SUBS, LANES)) for x in new_tails], axis=1),
        )
        shifted_diag = [x[:1] for x in shifted_diag]
        cos_lanes = [jnp.broadcast_to(x, (SUBS, LANES)) for x in cosines]
        sin_lanes = [jnp.broadcast_to(x, (SUBS, LANES)) for x in sines]
        cos_wide = jnp.concatenate(cos_lanes, axis=1)
        sin_wide = jnp.concatenate(sin_lanes, axis=1)

        for group in range(groups):
            mask = on_diag(group)
            odd = group % 2
            for buf, lanes in ((cos_buf, cos_lanes[odd]), (sin_buf, sin_lanes[odd])):
                picked = jnp.sum(jnp.where(mask, lanes, 0.0), axis=1, keepdims=True)
                buf[group] = jnp.broadcast_to(picked, (SUBS, LANES))

        def work(group):
            cos_row = jnp.concatenate([cos_buf[group]] * 2, axis=1)
            sin_row = jnp.concatenate([sin_buf[group]] * 2, axis=1)
            cos_base = jnp.concatenate([cos_buf[group]] * (size // LANES), axis=1)
            sin_base = jnp.concatenate([sin_buf[group]] * (size // LANES), axis=1)

            def turned(part):
                values = gram_from[part, group]
                lead, tail = values[:, : 2 * LANES], values[:, 2 * LANES :]
                return cos_wide * lead + sin_wide * tail, cos_wide * tail - sin_wide * lead

            top_lead, top_tail = turned(0)
            low_lead, low_tail = turned(1)
            top = shift_lanes(
                cos_row * top_lead + sin_row * low_lead, cos_row * top_tail + sin_row * low_tail
            )
            low = shift_lanes(
                cos_row * low_lead - sin_row * top_lead, cos_row * low_tail - sin_row * top_tail
            )
            lead = basis_from[0, group]
            tail = basis_from[1, group]
            base_top = cos_base * lead + sin_base * tail
            base_low = cos_base * tail - sin_base * lead
            return (
                list(top) + [base_top[:, i : i + LANES] for i in range(0, size, LANES)],
                list(low) + [base_low[:, i : i + LANES] for i in range(0, size, LANES)],
            )

        sums = [zero, zero]

        def store(part, group, values):
            for index, value in enumerate(values[:4]):
                gram_to[part, group, :, index * LANES : (index + 1) * LANES] = value
            for index, value in enumerate(values[4:]):
                basis_to[part, group, :, index * LANES : (index + 1) * LANES] = value
            if part == 0:
                odd = group % 2
                sums[odd] += jnp.where(on_diag(group), values[2 + odd], 0.0)

        first_top, first_low = work(0)
        last_top, last_low = work(last)
        store(0, 1, [jnp.where(sub == 0, y, x) for x, y in zip(first_top, first_low)])
        store(0, 0, [jnp.where(sub == 0, x, pltpu.roll(y, 1, 0)) for x, y in zip(first_top, last_top)])
        store(1, last, [
            jnp.where(sub == SUBS - 1, y, pltpu.roll(x, SUBS - 1, 0))
            for x, y in zip(first_low, last_top)
        ])
        store(1, last - 1, last_low)
        for group in range(1, last):
            top, low = work(group)
            store(0, group + 1, top)
            store(1, group - 1, low)
        return (
            (shifted_diag[0], shifted_diag[1]), (shifted_diag[2], shifted_diag[3]), tuple(sums)
        )

    start = (
        tuple(flat(x) for x in heads), tuple(flat(x) for x in tails), tuple(couplings)
    )

    def two_turns(_, carry):
        carry = turn(gram_a, gram_b, basis_a, basis_b, carry)
        return turn(gram_b, gram_a, basis_b, basis_a, carry)

    lax.fori_loop(0, ROUNDS // 2, two_turns, start)

    held_slot = jnp.where(row_slot == 0, 0, 1 + (row_slot + (size - 2 - ROUNDS % (size - 1))) % (size - 1))
    basis = basis_a[...].reshape(size, size).astype(jnp.bfloat16)
    lanes = lax.broadcasted_iota(jnp.int32, (1, size), 1)
    first_slow, slow_slot, fast_slot, _ = moves(plan_ref)
    slow_base = jnp.where(first_slow, 0, half)
    def turned(base, slot):
        place = onehot(held_slot, send_columns(lanes, base, slot, half))
        return dot32(basis, place, ((0,), (0,))).astype(jnp.bfloat16)

    fast_ref[...] = turned(half - slow_base, fast_slot)[:, : 2 * LANES]
    slow = turned(slow_base, slow_slot)
    packs[:size] = slow[:, :LANES]
    packs[size : 2 * size] = slow[:, LANES : 2 * LANES]
    matrix_copy.wait()
    copies = []

    def leave(start, count, ref):
        copies.append(
            pltpu.make_async_copy(packs.at[pl.ds(start, count)], ref, sems.at[1 + len(copies)])
        )
        copies[-1].start()

    first_count = first_ref.shape[0]
    leave(0, PACK, first_ref.at[pl.ds(0, PACK)])
    for unit in range(held.shape[0] // UNIT):
        at = (1 + unit) * PACK
        pack_unit(held[unit * UNIT : (unit + 1) * UNIT], slow, packs, at)
        if at < first_count:
            leave(at, PACK, first_ref.at[pl.ds(at, PACK)])
        else:
            leave(at, PACK, last_ref.at[pl.ds(at - first_count, PACK)])
    for copy in copies:
        copy.wait()


def jacobi(plan, grams, matrix):
    rows, size = matrix.shape
    groups = size // 2 // SUBS
    moved = rows - RAW_ROWS
    blocks = 1 + moved // UNIT
    last = LAST_ROWS // UNIT * PACK
    return pl.pallas_call(
        jacobi_kernel,
        out_shape=(
            jax.ShapeDtypeStruct((blocks * PACK - last, LANES), jnp.bfloat16),
            jax.ShapeDtypeStruct((last, LANES), jnp.bfloat16),
            jax.ShapeDtypeStruct((size, 2 * LANES), jnp.bfloat16),
            jax.ShapeDtypeStruct((SUBS, LANES), jnp.float32),
        ),
        in_specs=[pl.BlockSpec(memory_space=pltpu.SMEM)]
        + [pl.BlockSpec(memory_space=pltpu.VMEM)] * len(grams)
        + [pl.BlockSpec(memory_space=pl.ANY)],
        out_specs=[pl.BlockSpec(memory_space=pl.ANY)] * 2
        + [pl.BlockSpec(memory_space=pltpu.VMEM)] * 2,
        scratch_shapes=[
            pltpu.VMEM((2, groups, SUBS, 4 * LANES), jnp.float32),
            pltpu.VMEM((2, groups, SUBS, 4 * LANES), jnp.float32),
            pltpu.VMEM((2, groups, SUBS, size), jnp.float32),
            pltpu.VMEM((2, groups, SUBS, size), jnp.float32),
            pltpu.VMEM((groups, SUBS, LANES), jnp.float32),
            pltpu.VMEM((groups, SUBS, LANES), jnp.float32),
            pltpu.VMEM((moved, size), jnp.bfloat16),
            pltpu.VMEM((blocks * PACK, LANES), jnp.bfloat16),
            pltpu.SemaphoreType.DMA((1 + blocks,)),
        ],
        compiler_params=pltpu.CompilerParams(vmem_limit_bytes=JACOBI_VMEM_LIMIT),
        cost_estimate=pl.CostEstimate(
            flops=size, bytes_accessed=size, transcendentals=0
        ),
        name="jacobi_turns",
    )(plan, *grams, matrix)


def gram_spans(rows):
    spans = []
    start = 0
    while start < rows:
        wanted = GRAM_PARTS[len(spans)] if len(spans) < len(GRAM_PARTS) else GRAM_TILE
        spans.append((start, min(wanted, rows - start)))
        start += spans[-1][1]
    return spans


def gram_kernel(matrix_ref, packed_ref, raw_ref, held, upper_ref, corner_ref, sems, raw_sem):
    rows = held.shape[0]
    copies = []
    spans = gram_spans(rows)
    for index, (start, count) in enumerate(spans):
        part = pl.ds(start, count)
        copies.append(pltpu.make_async_copy(matrix_ref.at[part], held.at[part], sems.at[index]))
    for copy in copies[:IN_FLIGHT]:
        copy.start()
    early = pl.ds(0, RAW_ROWS)
    leave = pltpu.make_async_copy(held.at[early], raw_ref, raw_sem)
    for index, copy in enumerate(copies):
        copy.wait()
        if index + IN_FLIGHT < len(copies):
            copies[index + IN_FLIGHT].start()
        start, count = spans[index]
        if start + count == RAW_ROWS:
            leave.start()
        values = held[start : start + count]
        right = values[:, 2 * LANES :]
        upper = dot32(values[:, : 2 * LANES], values, ((0,), (0,)))
        corner = dot32(right, right, ((0,), (0,)))
        if index == 0:
            upper_ref[...] = upper
            corner_ref[...] = corner
        else:
            upper_ref[...] += upper
            corner_ref[...] += corner
    packed_ref[:LANES] = upper_ref[:LANES]
    packed_ref[LANES:, : 2 * LANES] = upper_ref[LANES:, LANES:]
    packed_ref[LANES:, 2 * LANES :] = corner_ref[...]
    leave.wait()


def gram_blocks(matrix):
    rows, size = matrix.shape
    return pl.pallas_call(
        gram_kernel,
        in_specs=[pl.BlockSpec(memory_space=pl.ANY)],
        out_specs=[pl.BlockSpec(memory_space=pltpu.VMEM), pl.BlockSpec(memory_space=pl.ANY)],
        out_shape=(
            jax.ShapeDtypeStruct((2 * LANES, size), jnp.float32),
            jax.ShapeDtypeStruct((RAW_ROWS, size), jnp.bfloat16),
        ),
        scratch_shapes=[
            pltpu.VMEM((rows, size), jnp.bfloat16),
            pltpu.VMEM((2 * LANES, size), jnp.float32),
            pltpu.VMEM((LANES, LANES), jnp.float32),
            pltpu.SemaphoreType.DMA((len(gram_spans(rows)),)),
            pltpu.SemaphoreType.DMA,
        ],
        compiler_params=pltpu.CompilerParams(vmem_limit_bytes=GRAM_VMEM_LIMIT),
        cost_estimate=pl.CostEstimate(
            flops=2 * rows * size * size, bytes_accessed=2 * rows * size, transcendentals=0
        ),
        name="gram_blocks",
    )(matrix)


def place_main(slot, out_ref, slow_main, fast_main):
    @pl.when(slot == 0)
    def _():
        out_ref[:, :LANES] = slow_main
        out_ref[:, 2 * LANES :] = fast_main

    @pl.when(slot != 0)
    def _():
        out_ref[:, :LANES] = fast_main
        out_ref[:, 2 * LANES :] = slow_main


def fill_kernel(plan_ref, slow_ref, near_ref, near_turn_ref, *refs):
    out_ref = refs[-1]
    half = UNIT // 2
    slot = moves(plan_ref)[3]
    middle = slice(LANES, 2 * LANES)
    near = dot32(near_ref[...], near_turn_ref[...])
    place_main(slot, out_ref, slow_ref[:UNIT], near[:, LANES:].astype(jnp.bfloat16))
    lane = lax.broadcasted_iota(jnp.int32, (half, LANES), 1)
    mask = (lane // (LANES // 2)) == slot
    slow = slow_ref[UNIT:].astype(jnp.float32)
    top = jnp.where(mask, slow, near[:half, :LANES])
    low = jnp.where(mask, pltpu.roll(slow, LANES // 2, 1), near[half:, :LANES])
    out_ref[:half, middle] = top.astype(jnp.bfloat16)
    out_ref[half:, middle] = low.astype(jnp.bfloat16)


def raw_kernel(plan_ref, slow_ref, slow_turn_ref, near_ref, near_turn_ref, out_ref):
    size = slow_ref.shape[1]
    slot = moves(plan_ref)[3]
    near = dot32(near_ref[...], near_turn_ref[...])
    mixed = dot32(slow_ref[...], slow_turn_ref[:size])
    main = dot32(slow_ref[...], slow_turn_ref[size:])
    place_main(slot, out_ref, main.astype(jnp.bfloat16), near[:, LANES:].astype(jnp.bfloat16))
    lane = lax.broadcasted_iota(jnp.int32, mixed.shape, 1)
    mask = (lane // (LANES // 2)) == slot
    middle = jnp.where(mask, mixed, near[:, :LANES])
    out_ref[:, LANES : 2 * LANES] = middle.astype(jnp.bfloat16)


def fill_rows(kernel, plan, sources, specs, near, near_turn, result, start, count):
    shape = near.shape
    first = start // UNIT
    operands = [plan, *sources, near, near_turn]
    row_spec = pl.BlockSpec((UNIT, shape[1]), lambda i: (first + i, 0))
    in_specs = [
        pl.BlockSpec(memory_space=pltpu.SMEM),
        *specs,
        row_spec,
        pl.BlockSpec(near_turn.shape, lambda i: (0, 0)),
    ]
    aliases = {}
    if result is not None:
        aliases = {len(operands): 0}
        operands.append(result)
        in_specs.append(pl.BlockSpec(memory_space=pl.ANY))
    return pl.pallas_call(
        kernel,
        grid=(count // UNIT,),
        in_specs=in_specs,
        out_specs=row_spec,
        out_shape=jax.ShapeDtypeStruct(shape, jnp.bfloat16),
        input_output_aliases=aliases,
        compiler_params=pltpu.CompilerParams(vmem_limit_bytes=VMEM_LIMIT),
        cost_estimate=pl.CostEstimate(
            flops=count * shape[1], bytes_accessed=4 * count * shape[1], transcendentals=0
        ),
        name="fill_rows",
    )(*operands)


def swapped_with(value, axis, partner):
    count = lax.axis_size(axis)
    return lax.ppermute(value, axis, [(source, partner(source, count)) for source in range(count)])


def slow_partner(source, count):
    return (source + 1) % count if source % 2 else (source + count - 1) % count


def fast_partner(source, count):
    return source ^ 1


def permuted(value, pairs):
    return lax.ppermute(value, "blk", pairs)


def cycle_sums(sums):
    count = lax.axis_size("blk")
    outer = [place for place in range(count) if place % 4 in (0, 3)]
    inner = [place for place in range(count) if place % 4 in (1, 2)]
    is_outer = (lax.axis_index("blk") + 1) % 4 < 2
    sums = sums + permuted(sums, [(place, place ^ 1) for place in range(count)])
    sums = sums + permuted(sums, [(place, place ^ 3) for place in outer])
    moved = permuted(sums, [(place, place ^ 1) for place in outer])
    sums = jnp.where(is_outer, sums, moved)
    step = 4
    while step < count:
        sums = sums + permuted(sums, [(place, place ^ step) for place in inner])
        step *= 2
    moved = permuted(sums, [(place, place ^ 1) for place in inner])
    return jnp.where(is_outer, moved, sums)


def on_device(matrix, plan):
    rows, size = matrix.shape
    own, early = gram_blocks(matrix)
    matrix_after, own = lax.optimization_barrier((matrix, own))
    if lax.axis_size("rows") == 2:
        other = swapped_with(own, "rows", fast_partner)
        grams = [own, other]
    else:
        grams = [lax.psum(own, "rows")]
    raw = swapped_with(early, "blk", slow_partner)
    near = swapped_with(matrix_after, "blk", fast_partner)
    first, last, near_turn, sums = jacobi(plan, grams, matrix)
    near_turn, raw, near = lax.optimization_barrier((near_turn, raw, near))

    first = swapped_with(first, "blk", slow_partner)
    last = swapped_with(last, "blk", slow_partner)
    near_turn = swapped_with(near_turn, "blk", fast_partner)
    totals = cycle_sums(sums)
    off_ratio = jnp.sqrt(totals[0, 0] / totals[1, 0])

    turn_spec = pl.BlockSpec((PACK, LANES), lambda i: (0, 0))
    raw_spec = pl.BlockSpec((UNIT, size), lambda i: (i, 0))
    first_spec = pl.BlockSpec((PACK, LANES), lambda i: (1 + i, 0))
    last_spec = pl.BlockSpec((PACK, LANES), lambda i: (i, 0))
    middle = rows - RAW_ROWS - LAST_ROWS
    result = fill_rows(
        raw_kernel, plan, [raw, first], [raw_spec, turn_spec], near, near_turn, None, 0, RAW_ROWS
    )
    result = fill_rows(
        fill_kernel, plan, [first], [first_spec], near, near_turn, result, RAW_ROWS, middle
    )
    result = fill_rows(
        fill_kernel, plan, [last], [last_spec], near, near_turn, result, rows - LAST_ROWS, LAST_ROWS
    )
    return result, off_ratio


def solution(mesh):
    in_specs = (P("rows", "blk"), P())
    out_specs = (P("rows", "blk"), P())
    return jax.shard_map(
        on_device, mesh=mesh, in_specs=in_specs, out_specs=out_specs, check_vma=False
    )
```

```python
import jax
import jax.numpy as jnp
from jax import lax
from jax.experimental import pallas as pl
from jax.experimental.pallas import tpu as pltpu
from jax.sharding import PartitionSpec as P

ROUNDS = 24
LANES = 128
SUBS = 8
UNIT = 512
PACK = UNIT + UNIT // 2
GRAM_PARTS = (512, 1536)
GRAM_TILE = 2048
RAW_ROWS = 2048
LAST_ROWS = 2048
FILL_TILE = 1024
SUM_ROWS = 16
IN_FLIGHT = 2
VMEM_LIMIT = 32 * 1024 * 1024
JACOBI_VMEM_LIMIT = 30 * 1024 * 1024
GRAM_VMEM_LIMIT = 58 * 1024 * 1024


def split_three(values):
    high = values.astype(jnp.bfloat16)
    rest = values - high.astype(jnp.float32)
    middle = rest.astype(jnp.bfloat16)
    low = (rest - middle.astype(jnp.float32)).astype(jnp.bfloat16)
    return high, middle, low


def dot32(left, right, dims=((1,), (0,))):
    return lax.dot_general(left, right, (dims, ((), ())), preferred_element_type=jnp.float32)


def slot_of_row(rows, groups, half):
    part = rows // half
    inside = rows % half
    index = (inside % SUBS) * groups + inside // SUBS
    return jnp.where(part == 0, index, 2 * half - 1 - index)


def slot_of_lane(lanes, half):
    part = lanes // (2 * LANES)
    odd = (lanes // LANES) % 2
    inside = lanes % LANES
    index = 2 * inside + odd
    slot = jnp.where(part == 0, index, 2 * half - 1 - index)
    return jnp.where(inside < half // 2, slot, -1)


def onehot(left, right):
    return jnp.where(left == right, 1.0, 0.0).astype(jnp.bfloat16)


def angles(head, tail, coupling):
    difference = head - tail
    sign_val = jnp.where(difference >= 0.0, 1.0, -1.0)
    across = 2.0 * coupling * sign_val
    along = jnp.abs(difference)
    scale = jnp.maximum(along, jnp.abs(across))
    empty = scale == 0.0
    inverse = 1.0 / jnp.where(empty, 1.0, scale)
    along = jnp.where(empty, 1.0, along * inverse)
    across = across * inverse
    square = along * along + across * across
    root = lax.rsqrt(square)
    root = root * (1.5 - 0.5 * square * root * root)
    cos_sq = 0.5 + 0.5 * (along * root)
    half_root = lax.rsqrt(cos_sq)
    half_root = half_root * (1.5 - 0.5 * cos_sq * half_root * half_root)
    return cos_sq * half_root, 0.5 * (across * root) * half_root


def full_gram(packed):
    first = packed[:LANES]
    block01, block02 = first[:, LANES : 2 * LANES], first[:, 2 * LANES :]
    block12 = packed[LANES:, LANES : 2 * LANES]
    second = jnp.concatenate([block01.T, packed[LANES:, : 2 * LANES]], axis=1)
    third = jnp.concatenate([block02.T, block12.T, packed[LANES:, 2 * LANES :]], axis=1)
    return jnp.concatenate([first, second, third], axis=0)


def send_columns(lanes, base, slot, width):
    section = lanes // LANES
    lane = lanes % LANES
    rest = width - LANES
    main_start = base + jnp.where(slot == 0, 0, rest)
    rest_start = base + jnp.where(slot == 0, LANES, 0)
    high = (section // 2 + slot) % 2
    inside = lane - high * (LANES - rest)
    mixed = jnp.where((inside >= 0) & (inside < rest), rest_start + inside, -1)
    return jnp.where(section == 1, main_start + lane, mixed)


def block_sums(packed):
    squares = packed * packed
    total = jnp.zeros((1, 1), jnp.float32)
    diag_sq = jnp.zeros((1, 1), jnp.float32)
    rows = lax.broadcasted_iota(jnp.int32, (LANES, LANES), 0)
    cols = lax.broadcasted_iota(jnp.int32, (LANES, LANES), 1)
    for row, col, weight in (
        (0, 0, 1.0), (0, 1, 2.0), (0, 2, 2.0), (1, 0, 1.0), (1, 1, 2.0), (1, 2, 1.0)
    ):
        block = squares[row * LANES : (row + 1) * LANES, col * LANES : (col + 1) * LANES]
        total = total + weight * jnp.sum(block, keepdims=True)
        if weight == 1.0:
            diag_sq = diag_sq + jnp.sum(jnp.where(rows == cols, block, 0.0), keepdims=True)
    row = lax.broadcasted_iota(jnp.int32, (SUM_ROWS, LANES), 0)
    pieces = jnp.zeros((SUM_ROWS, LANES), jnp.float32)
    for index, piece in enumerate(split_three(total - diag_sq) + split_three(diag_sq)):
        pieces = jnp.where(row == index, piece.astype(jnp.float32), pieces)
    return pieces.astype(jnp.bfloat16)


def pack_unit(values, turn, packed_ref, at):
    half = UNIT // 2
    top = dot32(values[:half], turn[:, : 2 * LANES])
    low = dot32(values[half:], turn[:, LANES:])
    packed_ref[at : at + half] = top[:, LANES:].astype(jnp.bfloat16)
    packed_ref[at + half : at + UNIT] = low[:, :LANES].astype(jnp.bfloat16)
    packed_ref[at + UNIT : at + PACK] = (top[:, :LANES] + low[:, LANES:]).astype(jnp.bfloat16)


def moves(plan_ref):
    count = plan_ref.shape[0] // 2
    position = lax.axis_index("blk")
    slow_dev = lax.rem(position + 2 * lax.rem(position, 2) - 1 + count, count)
    mine = plan_ref[2 * position], plan_ref[2 * position + 1]
    theirs = plan_ref[2 * slow_dev], plan_ref[2 * slow_dev + 1]
    first_slow = mine[0] // 2 == slow_dev
    slow_slot = lax.rem(jnp.where(first_slow, mine[0], mine[1]), 2)
    fast_slot = lax.rem(jnp.where(first_slow, mine[1], mine[0]), 2)
    in_slot = lax.rem(jnp.where(theirs[0] // 2 == position, theirs[0], theirs[1]), 2)
    return first_slow, slow_slot, fast_slot, in_slot


def jacobi_kernel(plan_ref, *refs):
    jacobi_body(plan_ref, refs[:-14], *refs[-14:])


def jacobi_body(
    plan_ref, gram_refs, matrix_ref, first_ref, last_ref, fast_ref, sums_ref,
    gram_a, gram_b, basis_a, basis_b, cos_buf, sin_buf, held, packs, sems,
):
    matrix_copy = pltpu.make_async_copy(matrix_ref.at[pl.ds(RAW_ROWS, held.shape[0])], held, sems.at[0])
    matrix_copy.start()
    size = gram_refs[0].shape[1]
    half = size // 2
    groups = half // SUBS
    last = groups - 1
    edge = half // 2 - 1
    lane_row = lax.broadcasted_iota(jnp.int32, (1, LANES), 1)
    lane = lax.broadcasted_iota(jnp.int32, (SUBS, LANES), 1)
    sub = lax.broadcasted_iota(jnp.int32, (SUBS, LANES), 0)
    spot = lane - sub * (groups // 2)

    def on_diag(group):
        return spot == group // 2

    row_slot = slot_of_row(lax.broadcasted_iota(jnp.int32, (size, 1), 0), groups, half)
    take_rows = onehot(row_slot, lax.broadcasted_iota(jnp.int32, (size, size), 1))
    lane_slot = slot_of_lane(lax.broadcasted_iota(jnp.int32, (1, 4 * LANES), 1), half)
    take_cols = onehot(lax.broadcasted_iota(jnp.int32, (size, 4 * LANES), 0), lane_slot)
    arranged = jnp.zeros((size, 4 * LANES), jnp.float32)
    packed = gram_refs[0][...]
    for other in gram_refs[1:]:
        packed = packed + other[...]
    gram_sum = full_gram(packed)
    sums_ref[...] = block_sums(packed)
    for piece in split_three(gram_sum):
        moved = dot32(take_rows, piece).astype(jnp.bfloat16)
        arranged = arranged + dot32(moved, take_cols)
    gram_a[...] = arranged.reshape(2, groups, SUBS, 4 * LANES)
    basis_a[...] = take_rows.astype(jnp.float32).reshape(2, groups, SUBS, size)

    zero = jnp.zeros((SUBS, LANES), jnp.float32)
    heads, tails, couplings = [zero, zero], [zero, zero], [zero, zero]
    for group in range(groups):
        odd = group % 2
        mask = on_diag(group)
        lead_cols = slice(odd * LANES, (odd + 1) * LANES)
        tail_cols = slice((2 + odd) * LANES, (3 + odd) * LANES)
        heads[odd] += jnp.where(mask, gram_a[0, group, :, lead_cols], 0.0)
        tails[odd] += jnp.where(mask, gram_a[1, group, :, tail_cols], 0.0)
        couplings[odd] += jnp.where(mask, gram_a[0, group, :, tail_cols], 0.0)

    def flat(values):
        return jnp.sum(values, axis=0, keepdims=True)

    def shift_lanes(lead, tail):
        lead0, lead1 = lead[:, :LANES], lead[:, LANES:]
        tail0, tail1 = tail[:, :LANES], tail[:, LANES:]
        here = lane[: lead.shape[0]]
        new_lead1 = jnp.where(here == 0, tail0, lead0)
        new_lead0 = jnp.where(here == 0, lead0, pltpu.roll(lead1, 1, 1))
        new_tail1 = jnp.where(here == edge, lead1, pltpu.roll(tail0, LANES - 1, 1))
        return new_lead0, new_lead1, tail1, new_tail1

    def turn(gram_from, gram_to, basis_from, basis_to, carry):
        heads, tails, couplings = carry
        cosines, sines, new_heads, new_tails = [], [], [], []
        for odd in range(2):
            head, tail = heads[odd], tails[odd]
            coupling = flat(couplings[odd])
            cosine, sine_val = angles(head, tail, coupling)
            cosines.append(cosine)
            sines.append(sine_val)
            first = cosine * head + sine_val * coupling
            second = cosine * coupling + sine_val * tail
            new_heads.append(cosine * first + sine_val * second)
            first = cosine * coupling - sine_val * head
            second = cosine * tail - sine_val * coupling
            new_tails.append(cosine * second - sine_val * first)
        shifted_diag = shift_lanes(
            jnp.concatenate([jnp.broadcast_to(x, (SUBS, LANES)) for x in new_heads], axis=1),
            jnp.concatenate([jnp.broadcast_to(x, (SUBS, LANES)) for x in new_tails], axis=1),
        )
        shifted_diag = [x[:1] for x in shifted_diag]
        cos_lanes = [jnp.broadcast_to(x, (SUBS, LANES)) for x in cosines]
        sin_lanes = [jnp.broadcast_to(x, (SUBS, LANES)) for x in sines]
        cos_wide = jnp.concatenate(cos_lanes, axis=1)
        sin_wide = jnp.concatenate(sin_lanes, axis=1)

        for group in range(groups):
            mask = on_diag(group)
            odd = group % 2
            for buf, lanes in ((cos_buf, cos_lanes[odd]), (sin_buf, sin_lanes[odd])):
                picked = jnp.sum(jnp.where(mask, lanes, 0.0), axis=1, keepdims=True)
                buf[group] = jnp.broadcast_to(picked, (SUBS, LANES))

        def work(group):
            cos_row = jnp.concatenate([cos_buf[group]] * 2, axis=1)
            sin_row = jnp.concatenate([sin_buf[group]] * 2, axis=1)
            cos_base = jnp.concatenate([cos_buf[group]] * (size // LANES), axis=1)
            sin_base = jnp.concatenate([sin_buf[group]] * (size // LANES), axis=1)

            def turned(part):
                values = gram_from[part, group]
                lead, tail = values[:, : 2 * LANES], values[:, 2 * LANES :]
                return cos_wide * lead + sin_wide * tail, cos_wide * tail - sin_wide * lead

            top_lead, top_tail = turned(0)
            low_lead, low_tail = turned(1)
            top = shift_lanes(
                cos_row * top_lead + sin_row * low_lead, cos_row * top_tail + sin_row * low_tail
            )
            low = shift_lanes(
                cos_row * low_lead - sin_row * top_lead, cos_row * low_tail - sin_row * top_tail
            )
            lead = basis_from[0, group]
            tail = basis_from[1, group]
            base_top = cos_base * lead + sin_base * tail
            base_low = cos_base * tail - sin_base * lead
            return (
                list(top) + [base_top[:, i : i + LANES] for i in range(0, size, LANES)],
                list(low) + [base_low[:, i : i + LANES] for i in range(0, size, LANES)],
            )

        sums = [zero, zero]

        def store(part, group, values):
            for index, value in enumerate(values[:4]):
                gram_to[part, group, :, index * LANES : (index + 1) * LANES] = value
            for index, value in enumerate(values[4:]):
                basis_to[part, group, :, index * LANES : (index + 1) * LANES] = value
            if part == 0:
                odd = group % 2
                sums[odd] += jnp.where(on_diag(group), values[2 + odd], 0.0)

        first_top, first_low = work(0)
        last_top, last_low = work(last)
        store(0, 1, [jnp.where(sub == 0, y, x) for x, y in zip(first_top, first_low)])
        store(0, 0, [jnp.where(sub == 0, x, pltpu.roll(y, 1, 0)) for x, y in zip(first_top, last_top)])
        store(1, last, [
            jnp.where(sub == SUBS - 1, y, pltpu.roll(x, SUBS - 1, 0))
            for x, y in zip(first_low, last_top)
        ])
        store(1, last - 1, last_low)
        for group in range(1, last):
            top, low = work(group)
            store(0, group + 1, top)
            store(1, group - 1, low)
        return (
            (shifted_diag[0], shifted_diag[1]), (shifted_diag[2], shifted_diag[3]), tuple(sums)
        )

    start = (
        tuple(flat(x) for x in heads), tuple(flat(x) for x in tails), tuple(couplings)
    )

    def two_turns(_, carry):
        carry = turn(gram_a, gram_b, basis_a, basis_b, carry)
        return turn(gram_b, gram_a, basis_b, basis_a, carry)

    lax.fori_loop(0, ROUNDS // 2, two_turns, start)

    held_slot = jnp.where(row_slot == 0, 0, 1 + (row_slot + (size - 2 - ROUNDS % (size - 1))) % (size - 1))
    basis = basis_a[...].reshape(size, size).astype(jnp.bfloat16)
    lanes = lax.broadcasted_iota(jnp.int32, (1, size), 1)
    first_slow, slow_slot, fast_slot, _ = moves(plan_ref)
    slow_base = jnp.where(first_slow, 0, half)
    def turned(base, slot):
        place = onehot(held_slot, send_columns(lanes, base, slot, half))
        return dot32(basis, place, ((0,), (0,))).astype(jnp.bfloat16)

    fast_ref[...] = turned(half - slow_base, fast_slot)[:, : 2 * LANES]
    slow = turned(slow_base, slow_slot)
    packs[:size] = slow[:, :LANES]
    packs[size : 2 * size] = slow[:, LANES : 2 * LANES]
    matrix_copy.wait()
    copies = []

    def leave(start, count, ref):
        copies.append(
            pltpu.make_async_copy(packs.at[pl.ds(start, count)], ref, sems.at[1 + len(copies)])
        )
        copies[-1].start()

    first_count = first_ref.shape[0] - SUM_ROWS
    leave(0, PACK, first_ref.at[pl.ds(0, PACK)])
    copies.append(
        pltpu.make_async_copy(sums_ref, first_ref.at[pl.ds(first_count, SUM_ROWS)], sems.at[2])
    )
    copies[-1].start()
    for unit in range(held.shape[0] // UNIT):
        at = (1 + unit) * PACK
        pack_unit(held[unit * UNIT : (unit + 1) * UNIT], slow, packs, at)
        if at < first_count:
            leave(at, PACK, first_ref.at[pl.ds(at, PACK)])
        else:
            leave(at, PACK, last_ref.at[pl.ds(at - first_count, PACK)])
    for copy in copies:
        copy.wait()


def jacobi(plan, grams, matrix):
    rows, size = matrix.shape
    groups = size // 2 // SUBS
    moved = rows - RAW_ROWS
    blocks = 1 + moved // UNIT
    last = LAST_ROWS // UNIT * PACK
    return pl.pallas_call(
        jacobi_kernel,
        out_shape=(
            jax.ShapeDtypeStruct((blocks * PACK - last + SUM_ROWS, LANES), jnp.bfloat16),
            jax.ShapeDtypeStruct((last, LANES), jnp.bfloat16),
            jax.ShapeDtypeStruct((size, 2 * LANES), jnp.bfloat16),
            jax.ShapeDtypeStruct((SUM_ROWS, LANES), jnp.bfloat16),
        ),
        in_specs=[pl.BlockSpec(memory_space=pltpu.SMEM)]
        + [pl.BlockSpec(memory_space=pltpu.VMEM)] * len(grams)
        + [pl.BlockSpec(memory_space=pl.ANY)],
        out_specs=[pl.BlockSpec(memory_space=pl.ANY)] * 2
        + [pl.BlockSpec(memory_space=pltpu.VMEM)] * 2,
        scratch_shapes=[
            pltpu.VMEM((2, groups, SUBS, 4 * LANES), jnp.float32),
            pltpu.VMEM((2, groups, SUBS, 4 * LANES), jnp.float32),
            pltpu.VMEM((2, groups, SUBS, size), jnp.float32),
            pltpu.VMEM((2, groups, SUBS, size), jnp.float32),
            pltpu.VMEM((groups, SUBS, LANES), jnp.float32),
            pltpu.VMEM((groups, SUBS, LANES), jnp.float32),
            pltpu.VMEM((moved, size), jnp.bfloat16),
            pltpu.VMEM((blocks * PACK, LANES), jnp.bfloat16),
            pltpu.SemaphoreType.DMA((2 + blocks,)),
        ],
        compiler_params=pltpu.CompilerParams(vmem_limit_bytes=JACOBI_VMEM_LIMIT),
        cost_estimate=pl.CostEstimate(
            flops=size, bytes_accessed=size, transcendentals=0
        ),
        name="jacobi_turns",
    )(plan, *grams, matrix)


def gram_spans(rows):
    spans = []
    start = 0
    while start < rows:
        wanted = GRAM_PARTS[len(spans)] if len(spans) < len(GRAM_PARTS) else GRAM_TILE
        spans.append((start, min(wanted, rows - start)))
        start += spans[-1][1]
    return spans


def gram_kernel(matrix_ref, packed_ref, raw_ref, held, upper_ref, corner_ref, sems, raw_sem):
    rows = held.shape[0]
    copies = []
    spans = gram_spans(rows)
    for index, (start, count) in enumerate(spans):
        part = pl.ds(start, count)
        copies.append(pltpu.make_async_copy(matrix_ref.at[part], held.at[part], sems.at[index]))
    for copy in copies[:IN_FLIGHT]:
        copy.start()
    early = pl.ds(0, RAW_ROWS)
    leave = pltpu.make_async_copy(held.at[early], raw_ref, raw_sem)
    for index, copy in enumerate(copies):
        copy.wait()
        if index + IN_FLIGHT < len(copies):
            copies[index + IN_FLIGHT].start()
        start, count = spans[index]
        if start + count == RAW_ROWS:
            leave.start()
        values = held[start : start + count]
        right = values[:, 2 * LANES :]
        upper = dot32(values[:, : 2 * LANES], values, ((0,), (0,)))
        corner = dot32(right, right, ((0,), (0,)))
        if index == 0:
            upper_ref[...] = upper
            corner_ref[...] = corner
        else:
            upper_ref[...] += upper
            corner_ref[...] += corner
    packed_ref[:LANES] = upper_ref[:LANES]
    packed_ref[LANES:, : 2 * LANES] = upper_ref[LANES:, LANES:]
    packed_ref[LANES:, 2 * LANES :] = corner_ref[...]
    leave.wait()


def gram_blocks(matrix):
    rows, size = matrix.shape
    return pl.pallas_call(
        gram_kernel,
        in_specs=[pl.BlockSpec(memory_space=pl.ANY)],
        out_specs=[pl.BlockSpec(memory_space=pltpu.VMEM), pl.BlockSpec(memory_space=pl.ANY)],
        out_shape=(
            jax.ShapeDtypeStruct((2 * LANES, size), jnp.float32),
            jax.ShapeDtypeStruct((RAW_ROWS, size), jnp.bfloat16),
        ),
        scratch_shapes=[
            pltpu.VMEM((rows, size), jnp.bfloat16),
            pltpu.VMEM((2 * LANES, size), jnp.float32),
            pltpu.VMEM((LANES, LANES), jnp.float32),
            pltpu.SemaphoreType.DMA((len(gram_spans(rows)),)),
            pltpu.SemaphoreType.DMA,
        ],
        compiler_params=pltpu.CompilerParams(vmem_limit_bytes=GRAM_VMEM_LIMIT),
        cost_estimate=pl.CostEstimate(
            flops=2 * rows * size * size, bytes_accessed=2 * rows * size, transcendentals=0
        ),
        name="gram_blocks",
    )(matrix)


def place_main(slot, out_ref, rows, slow_main, near_main):
    @pl.when(slot == 0)
    def _():
        out_ref[rows, :LANES] = slow_main
        out_ref[rows, 2 * LANES :] = near_main

    @pl.when(slot != 0)
    def _():
        out_ref[rows, :LANES] = near_main
        out_ref[rows, 2 * LANES :] = slow_main


def slot_lanes(slot, rows):
    lane = lax.broadcasted_iota(jnp.int32, (rows, LANES), 1)
    return (lane // (LANES // 2)) == slot


def fill_kernel(plan_ref, near_ref, near_turn_ref, *refs):
    slow_refs, out_ref = refs[:-2], refs[-1]
    half = UNIT // 2
    slot = moves(plan_ref)[3]
    mask = slot_lanes(slot, half)
    middle = slice(LANES, 2 * LANES)
    for unit, slow_ref in enumerate(slow_refs):
        start = unit * UNIT
        rows = slice(start, start + UNIT)
        near = dot32(near_ref[rows], near_turn_ref[...])
        place_main(slot, out_ref, rows, slow_ref[:UNIT], near[:, LANES:].astype(jnp.bfloat16))
        slow = slow_ref[UNIT:].astype(jnp.float32)
        top = jnp.where(mask, slow, near[:half, :LANES])
        low = jnp.where(mask, pltpu.roll(slow, LANES // 2, 1), near[half:, :LANES])
        out_ref[start : start + half, middle] = top.astype(jnp.bfloat16)
        out_ref[start + half : start + UNIT, middle] = low.astype(jnp.bfloat16)


def raw_kernel(plan_ref, near_ref, near_turn_ref, slow_ref, slow_turn_ref, out_ref):
    size = slow_ref.shape[1]
    slot = moves(plan_ref)[3]
    mask = slot_lanes(slot, UNIT)
    slow_turn = jnp.concatenate([slow_turn_ref[:size], slow_turn_ref[size:]], axis=1)
    for unit in range(out_ref.shape[0] // UNIT):
        rows = slice(unit * UNIT, (unit + 1) * UNIT)
        near = dot32(near_ref[rows], near_turn_ref[...])
        slow = dot32(slow_ref[rows], slow_turn)
        near_main = near[:, LANES:].astype(jnp.bfloat16)
        place_main(slot, out_ref, rows, slow[:, LANES:].astype(jnp.bfloat16), near_main)
        middle = jnp.where(mask, slow[:, :LANES], near[:, :LANES])
        out_ref[rows, LANES : 2 * LANES] = middle.astype(jnp.bfloat16)


def fill_rows(kernel, plan, sources, specs, near, near_turn, result, start, count):
    shape = near.shape
    first = start // FILL_TILE
    operands = [plan, near, near_turn, *sources]
    row_spec = pl.BlockSpec((FILL_TILE, shape[1]), lambda i: (first + i, 0))
    in_specs = [
        pl.BlockSpec(memory_space=pltpu.SMEM),
        row_spec,
        pl.BlockSpec(near_turn.shape, lambda i: (0, 0)),
        *specs,
    ]
    aliases = {}
    if result is not None:
        aliases = {len(operands): 0}
        operands.append(result)
        in_specs.append(pl.BlockSpec(memory_space=pl.ANY))
    return pl.pallas_call(
        kernel,
        grid=(count // FILL_TILE,),
        in_specs=in_specs,
        out_specs=row_spec,
        out_shape=jax.ShapeDtypeStruct(shape, jnp.bfloat16),
        input_output_aliases=aliases,
        compiler_params=pltpu.CompilerParams(vmem_limit_bytes=VMEM_LIMIT),
        cost_estimate=pl.CostEstimate(
            flops=count * shape[1], bytes_accessed=4 * count * shape[1], transcendentals=0
        ),
        name="fill_rows",
    )(*operands)


def swapped_with(value, axis, partner):
    count = lax.axis_size(axis)
    return lax.ppermute(value, axis, [(source, partner(source, count)) for source in range(count)])


def slow_partner(source, count):
    return (source + 1) % count if source % 2 else (source + count - 1) % count


def fast_partner(source, count):
    return source ^ 1


def permuted(value, pairs):
    return lax.ppermute(value, "blk", pairs)


def joined(pieces):
    values = pieces.astype(jnp.float32)
    row = lax.broadcasted_iota(jnp.int32, (SUBS, LANES), 0)
    off = values[0:1] + values[1:2] + values[2:3]
    diag = values[3:4] + values[4:5] + values[5:6]
    return jnp.where(row == 0, off, diag)


def add_pairs(left, right):
    total = left[0] + right[0]
    moved = total - left[0]
    lost = (left[0] - (total - moved)) + (right[0] - moved)
    small = left[1] + right[1] + lost
    high = total + small
    return high, small - (high - total)


def cycle_sums(mine, theirs):
    count = lax.axis_size("blk")
    zero = jnp.zeros((SUBS, LANES), jnp.float32)
    sums = add_pairs((joined(mine), zero), (joined(theirs), zero))
    step = 1
    while step < count:
        if step != 2:
            pairs = [(place, place ^ step) for place in range(count)]
            moved = permuted(jnp.concatenate(sums, axis=0), pairs)
            sums = add_pairs(sums, (moved[:SUBS], moved[SUBS:]))
        step *= 2
    return sums[0]


def on_device(matrix, plan):
    rows, size = matrix.shape
    own, early = gram_blocks(matrix)
    matrix_after, own = lax.optimization_barrier((matrix, own))
    if lax.axis_size("rows") == 2:
        other = swapped_with(own, "rows", fast_partner)
        grams = [own, other]
    else:
        grams = [lax.psum(own, "rows")]
    raw = swapped_with(early, "blk", slow_partner)
    near = swapped_with(matrix_after, "blk", fast_partner)
    first, last, near_turn, sums = jacobi(plan, grams, matrix)
    near_turn, raw, near = lax.optimization_barrier((near_turn, raw, near))

    first = swapped_with(first, "blk", slow_partner)
    last = swapped_with(last, "blk", slow_partner)
    near_turn = swapped_with(near_turn, "blk", fast_partner)
    theirs = first[first.shape[0] - SUM_ROWS :]
    theirs, near_turn = lax.optimization_barrier((theirs, near_turn))
    totals = cycle_sums(sums, theirs)
    off_ratio = jnp.sqrt(totals[0, 0] / totals[1, 0])

    def pack_specs(skip):
        units = FILL_TILE // UNIT
        return [
            pl.BlockSpec((PACK, LANES), lambda i, unit=unit: (skip + units * i + unit, 0))
            for unit in range(units)
        ]

    units = FILL_TILE // UNIT
    turn_spec = pl.BlockSpec((PACK, LANES), lambda i: (0, 0))
    raw_spec = pl.BlockSpec((FILL_TILE, size), lambda i: (i, 0))
    middle = rows - RAW_ROWS - LAST_ROWS
    result = fill_rows(
        raw_kernel, plan, [raw, first], [raw_spec, turn_spec], near, near_turn, None, 0, RAW_ROWS
    )
    result = fill_rows(
        fill_kernel, plan, [first] * units, pack_specs(1), near, near_turn, result, RAW_ROWS, middle
    )
    result = fill_rows(
        fill_kernel, plan, [last] * units, pack_specs(0), near, near_turn, result,
        rows - LAST_ROWS, LAST_ROWS,
    )
    return result, off_ratio


def solution(mesh):
    in_specs = (P("rows", "blk"), P())
    out_specs = (P("rows", "blk"), P())
    return jax.shard_map(
        on_device, mesh=mesh, in_specs=in_specs, out_specs=out_specs, check_vma=False
    )
```

```python
import jax
import jax.numpy as jnp
from jax import lax
from jax.experimental import pallas as pl
from jax.experimental.pallas import tpu as pltpu
from jax.sharding import PartitionSpec as P

ROUNDS = 24
LANES = 128
SUBS = 8
UNIT = 512
PACK = UNIT + UNIT // 2
GRAM_PARTS = (512, 1024)
GRAM_TILE = 1536
RAW_ROWS = 1536
LAST_ROWS = 1536
FILL_TILE = 512
SUM_ROWS = 16
IN_FLIGHT = 2
VMEM_LIMIT = 60 * 1024 * 1024
FILL_VMEM_LIMIT = 32 * 1024 * 1024


def split_three(values):
    high = values.astype(jnp.bfloat16)
    rest = values - high.astype(jnp.float32)
    middle = rest.astype(jnp.bfloat16)
    low = (rest - middle.astype(jnp.float32)).astype(jnp.bfloat16)
    return high, middle, low


def dot32(left, right, dims=((1,), (0,))):
    return lax.dot_general(left, right, (dims, ((), ())), preferred_element_type=jnp.float32)


def slot_of_row(rows, groups, half):
    part = rows // half
    inside = rows % half
    index = (inside % SUBS) * groups + inside // SUBS
    return jnp.where(part == 0, index, 2 * half - 1 - index)


def slot_of_lane(lanes, half):
    part = lanes // (2 * LANES)
    odd = (lanes // LANES) % 2
    inside = lanes % LANES
    index = 2 * inside + odd
    slot = jnp.where(part == 0, index, 2 * half - 1 - index)
    return jnp.where(inside < half // 2, slot, -1)


def onehot(left, right):
    return jnp.where(left == right, 1.0, 0.0).astype(jnp.bfloat16)


def angles(head, tail, coupling):
    difference = head - tail
    sign_val = jnp.where(difference >= 0.0, 1.0, -1.0)
    across = 2.0 * coupling * sign_val
    along = jnp.abs(difference)
    scale = jnp.maximum(along, jnp.abs(across))
    empty = scale == 0.0
    inverse = 1.0 / jnp.where(empty, 1.0, scale)
    along = jnp.where(empty, 1.0, along * inverse)
    across = across * inverse
    square = along * along + across * across
    root = lax.rsqrt(square)
    root = root * (1.5 - 0.5 * square * root * root)
    cos_sq = 0.5 + 0.5 * (along * root)
    half_root = lax.rsqrt(cos_sq)
    half_root = half_root * (1.5 - 0.5 * cos_sq * half_root * half_root)
    return cos_sq * half_root, 0.5 * (across * root) * half_root


def full_gram(packed):
    first = packed[:LANES]
    block01, block02 = first[:, LANES : 2 * LANES], first[:, 2 * LANES :]
    block12 = packed[LANES:, LANES : 2 * LANES]
    second = jnp.concatenate([block01.T, packed[LANES:, : 2 * LANES]], axis=1)
    third = jnp.concatenate([block02.T, block12.T, packed[LANES:, 2 * LANES :]], axis=1)
    return jnp.concatenate([first, second, third], axis=0)


def send_columns(lanes, base, slot, width):
    section = lanes // LANES
    lane = lanes % LANES
    rest = width - LANES
    main_start = base + jnp.where(slot == 0, 0, rest)
    rest_start = base + jnp.where(slot == 0, LANES, 0)
    high = (section // 2 + slot) % 2
    inside = lane - high * (LANES - rest)
    mixed = jnp.where((inside >= 0) & (inside < rest), rest_start + inside, -1)
    return jnp.where(section == 1, main_start + lane, mixed)


def block_sums(packed):
    squares = packed * packed
    total = jnp.zeros((1, 1), jnp.float32)
    diag_sq = jnp.zeros((1, 1), jnp.float32)
    rows = lax.broadcasted_iota(jnp.int32, (LANES, LANES), 0)
    cols = lax.broadcasted_iota(jnp.int32, (LANES, LANES), 1)
    for row, col, weight in (
        (0, 0, 1.0), (0, 1, 2.0), (0, 2, 2.0), (1, 0, 1.0), (1, 1, 2.0), (1, 2, 1.0)
    ):
        block = squares[row * LANES : (row + 1) * LANES, col * LANES : (col + 1) * LANES]
        total = total + weight * jnp.sum(block, keepdims=True)
        if weight == 1.0:
            diag_sq = diag_sq + jnp.sum(jnp.where(rows == cols, block, 0.0), keepdims=True)
    row = lax.broadcasted_iota(jnp.int32, (SUM_ROWS, LANES), 0)
    pieces = jnp.zeros((SUM_ROWS, LANES), jnp.float32)
    for index, piece in enumerate(split_three(total - diag_sq) + split_three(diag_sq)):
        pieces = jnp.where(row == index, piece.astype(jnp.float32), pieces)
    return pieces.astype(jnp.bfloat16)


def pack_unit(values, turn, packed_ref, at):
    half = UNIT // 2
    top = dot32(values[:half], turn[:, : 2 * LANES])
    low = dot32(values[half:], turn[:, LANES:])
    packed_ref[at : at + half] = top[:, LANES:].astype(jnp.bfloat16)
    packed_ref[at + half : at + UNIT] = low[:, :LANES].astype(jnp.bfloat16)
    packed_ref[at + UNIT : at + PACK] = (top[:, :LANES] + low[:, LANES:]).astype(jnp.bfloat16)


def moves(plan_ref):
    count = plan_ref.shape[0] // 2
    position = lax.axis_index("blk")
    slow_dev = lax.rem(position + 2 * lax.rem(position, 2) - 1 + count, count)
    mine = plan_ref[2 * position], plan_ref[2 * position + 1]
    theirs = plan_ref[2 * slow_dev], plan_ref[2 * slow_dev + 1]
    first_slow = mine[0] // 2 == slow_dev
    slow_slot = lax.rem(jnp.where(first_slow, mine[0], mine[1]), 2)
    fast_slot = lax.rem(jnp.where(first_slow, mine[1], mine[0]), 2)
    in_slot = lax.rem(jnp.where(theirs[0] // 2 == position, theirs[0], theirs[1]), 2)
    return first_slow, slow_slot, fast_slot, in_slot


def jacobi_kernel(plan_ref, *refs):
    jacobi_body(plan_ref, refs[:-17], *refs[-17:])


def jacobi_body(
    plan_ref, gram_refs, matrix_ref, head_ref, first_ref, last_ref, fast_ref, sums_ref,
    gram_a, gram_b, basis_a, basis_b, cos_buf, sin_buf, held, packs, gram_held, gram_sems, sems,
):
    gram_copies = [
        pltpu.make_async_copy(ref, gram_held.at[index], gram_sems.at[index])
        for index, ref in enumerate(gram_refs)
    ]
    for copy in gram_copies:
        copy.start()
    matrix_copy = pltpu.make_async_copy(matrix_ref.at[pl.ds(RAW_ROWS, held.shape[0])], held, sems.at[0])
    matrix_copy.start()
    size = gram_refs[0].shape[1]
    half = size // 2
    groups = half // SUBS
    last = groups - 1
    edge = half // 2 - 1
    lane_row = lax.broadcasted_iota(jnp.int32, (1, LANES), 1)
    lane = lax.broadcasted_iota(jnp.int32, (SUBS, LANES), 1)
    sub = lax.broadcasted_iota(jnp.int32, (SUBS, LANES), 0)
    spot = lane - sub * (groups // 2)

    def on_diag(group):
        return spot == group // 2

    row_slot = slot_of_row(lax.broadcasted_iota(jnp.int32, (size, 1), 0), groups, half)
    take_rows = onehot(row_slot, lax.broadcasted_iota(jnp.int32, (size, size), 1))
    lane_slot = slot_of_lane(lax.broadcasted_iota(jnp.int32, (1, 4 * LANES), 1), half)
    take_cols = onehot(lax.broadcasted_iota(jnp.int32, (size, 4 * LANES), 0), lane_slot)
    arranged = jnp.zeros((size, 4 * LANES), jnp.float32)
    for copy in gram_copies:
        copy.wait()
    packed = gram_held[0]
    for index in range(1, len(gram_refs)):
        packed = packed + gram_held[index]
    gram_sum = full_gram(packed)
    sums_ref[...] = block_sums(packed)
    for piece in split_three(gram_sum):
        moved = dot32(take_rows, piece).astype(jnp.bfloat16)
        arranged = arranged + dot32(moved, take_cols)
    gram_a[...] = arranged.reshape(2, groups, SUBS, 4 * LANES)
    basis_a[...] = take_rows.astype(jnp.float32).reshape(2, groups, SUBS, size)

    zero = jnp.zeros((SUBS, LANES), jnp.float32)
    heads, tails, couplings = [zero, zero], [zero, zero], [zero, zero]
    for group in range(groups):
        odd = group % 2
        mask = on_diag(group)
        lead_cols = slice(odd * LANES, (odd + 1) * LANES)
        tail_cols = slice((2 + odd) * LANES, (3 + odd) * LANES)
        heads[odd] += jnp.where(mask, gram_a[0, group, :, lead_cols], 0.0)
        tails[odd] += jnp.where(mask, gram_a[1, group, :, tail_cols], 0.0)
        couplings[odd] += jnp.where(mask, gram_a[0, group, :, tail_cols], 0.0)

    def flat(values):
        return jnp.sum(values, axis=0, keepdims=True)

    def shift_lanes(lead, tail):
        lead0, lead1 = lead[:, :LANES], lead[:, LANES:]
        tail0, tail1 = tail[:, :LANES], tail[:, LANES:]
        here = lane[: lead.shape[0]]
        new_lead1 = jnp.where(here == 0, tail0, lead0)
        new_lead0 = jnp.where(here == 0, lead0, pltpu.roll(lead1, 1, 1))
        new_tail1 = jnp.where(here == edge, lead1, pltpu.roll(tail0, LANES - 1, 1))
        return new_lead0, new_lead1, tail1, new_tail1

    def turn(gram_from, gram_to, basis_from, basis_to, carry):
        heads, tails, couplings = carry
        cosines, sines, new_heads, new_tails = [], [], [], []
        for odd in range(2):
            head, tail = heads[odd], tails[odd]
            coupling = flat(couplings[odd])
            cosine, sine_val = angles(head, tail, coupling)
            cosines.append(cosine)
            sines.append(sine_val)
            first = cosine * head + sine_val * coupling
            second = cosine * coupling + sine_val * tail
            new_heads.append(cosine * first + sine_val * second)
            first = cosine * coupling - sine_val * head
            second = cosine * tail - sine_val * coupling
            new_tails.append(cosine * second - sine_val * first)
        shifted_diag = shift_lanes(
            jnp.concatenate([jnp.broadcast_to(x, (SUBS, LANES)) for x in new_heads], axis=1),
            jnp.concatenate([jnp.broadcast_to(x, (SUBS, LANES)) for x in new_tails], axis=1),
        )
        shifted_diag = [x[:1] for x in shifted_diag]
        cos_lanes = [jnp.broadcast_to(x, (SUBS, LANES)) for x in cosines]
        sin_lanes = [jnp.broadcast_to(x, (SUBS, LANES)) for x in sines]
        cos_wide = jnp.concatenate(cos_lanes, axis=1)
        sin_wide = jnp.concatenate(sin_lanes, axis=1)

        for group in range(groups):
            mask = on_diag(group)
            odd = group % 2
            for buf, lanes in ((cos_buf, cos_lanes[odd]), (sin_buf, sin_lanes[odd])):
                picked = jnp.sum(jnp.where(mask, lanes, 0.0), axis=1, keepdims=True)
                buf[group] = jnp.broadcast_to(picked, (SUBS, LANES))

        def work(group):
            cos_row = jnp.concatenate([cos_buf[group]] * 2, axis=1)
            sin_row = jnp.concatenate([sin_buf[group]] * 2, axis=1)
            cos_base = jnp.concatenate([cos_buf[group]] * (size // LANES), axis=1)
            sin_base = jnp.concatenate([sin_buf[group]] * (size // LANES), axis=1)

            def turned(part):
                values = gram_from[part, group]
                lead, tail = values[:, : 2 * LANES], values[:, 2 * LANES :]
                return cos_wide * lead + sin_wide * tail, cos_wide * tail - sin_wide * lead

            top_lead, top_tail = turned(0)
            low_lead, low_tail = turned(1)
            top = shift_lanes(
                cos_row * top_lead + sin_row * low_lead, cos_row * top_tail + sin_row * low_tail
            )
            low = shift_lanes(
                cos_row * low_lead - sin_row * top_lead, cos_row * low_tail - sin_row * top_tail
            )
            lead = basis_from[0, group]
            tail = basis_from[1, group]
            base_top = cos_base * lead + sin_base * tail
            base_low = cos_base * tail - sin_base * lead
            return (
                list(top) + [base_top[:, i : i + LANES] for i in range(0, size, LANES)],
                list(low) + [base_low[:, i : i + LANES] for i in range(0, size, LANES)],
            )

        sums = [zero, zero]

        def store(part, group, values):
            for index, value in enumerate(values[:4]):
                gram_to[part, group, :, index * LANES : (index + 1) * LANES] = value
            for index, value in enumerate(values[4:]):
                basis_to[part, group, :, index * LANES : (index + 1) * LANES] = value
            if part == 0:
                odd = group % 2
                sums[odd] += jnp.where(on_diag(group), values[2 + odd], 0.0)

        first_top, first_low = work(0)
        last_top, last_low = work(last)
        store(0, 1, [jnp.where(sub == 0, y, x) for x, y in zip(first_top, first_low)])
        store(0, 0, [jnp.where(sub == 0, x, pltpu.roll(y, 1, 0)) for x, y in zip(first_top, last_top)])
        store(1, last, [
            jnp.where(sub == SUBS - 1, y, pltpu.roll(x, SUBS - 1, 0))
            for x, y in zip(first_low, last_top)
        ])
        store(1, last - 1, last_low)
        for group in range(1, last):
            top, low = work(group)
            store(0, group + 1, top)
            store(1, group - 1, low)
        return (
            (shifted_diag[0], shifted_diag[1]), (shifted_diag[2], shifted_diag[3]), tuple(sums)
        )

    start = (
        tuple(flat(x) for x in heads), tuple(flat(x) for x in tails), tuple(couplings)
    )

    def two_turns(_, carry):
        carry = turn(gram_a, gram_b, basis_a, basis_b, carry)
        return turn(gram_b, gram_a, basis_b, basis_a, carry)

    lax.fori_loop(0, ROUNDS // 2, two_turns, start)

    held_slot = jnp.where(row_slot == 0, 0, 1 + (row_slot + (size - 2 - ROUNDS % (size - 1))) % (size - 1))
    basis = basis_a[...].reshape(size, size).astype(jnp.bfloat16)
    lanes = lax.broadcasted_iota(jnp.int32, (1, size), 1)
    first_slow, slow_slot, fast_slot, _ = moves(plan_ref)
    slow_base = jnp.where(first_slow, 0, half)
    def turned(base, slot):
        place = onehot(held_slot, send_columns(lanes, base, slot, half))
        return dot32(basis, place, ((0,), (0,))).astype(jnp.bfloat16)

    fast_ref[...] = turned(half - slow_base, fast_slot)[:, : 2 * LANES]
    slow = turned(slow_base, slow_slot)
    packs[:size] = slow[:, :LANES]
    packs[size : 2 * size] = slow[:, LANES : 2 * LANES]
    matrix_copy.wait()
    copies = []

    def leave(start, count, ref):
        copies.append(
            pltpu.make_async_copy(packs.at[pl.ds(start, count)], ref, sems.at[1 + len(copies)])
        )
        copies[-1].start()

    leave(0, PACK, head_ref.at[pl.ds(0, PACK)])
    copies.append(pltpu.make_async_copy(sums_ref, head_ref.at[pl.ds(PACK, SUM_ROWS)], sems.at[2]))
    copies[-1].start()
    first_count = first_ref.shape[0]
    for unit in range(held.shape[0] // UNIT):
        at = (1 + unit) * PACK
        pack_unit(held[unit * UNIT : (unit + 1) * UNIT], slow, packs, at)
        place = unit * PACK
        if place < first_count:
            leave(at, PACK, first_ref.at[pl.ds(place, PACK)])
        else:
            leave(at, PACK, last_ref.at[pl.ds(place - first_count, PACK)])
    for copy in copies:
        copy.wait()


def jacobi(plan, grams, matrix):
    rows, size = matrix.shape
    groups = size // 2 // SUBS
    moved = rows - RAW_ROWS
    blocks = 1 + moved // UNIT
    last = LAST_ROWS // UNIT * PACK
    return pl.pallas_call(
        jacobi_kernel,
        out_shape=(
            jax.ShapeDtypeStruct((PACK + SUM_ROWS, LANES), jnp.bfloat16),
            jax.ShapeDtypeStruct(((blocks - 1) * PACK - last, LANES), jnp.bfloat16),
            jax.ShapeDtypeStruct((last, LANES), jnp.bfloat16),
            jax.ShapeDtypeStruct((size, 2 * LANES), jnp.bfloat16),
            jax.ShapeDtypeStruct((SUM_ROWS, LANES), jnp.bfloat16),
        ),
        in_specs=[pl.BlockSpec(memory_space=pltpu.SMEM)]
        + [pl.BlockSpec(memory_space=pl.ANY)] * (len(grams) + 1),
        out_specs=[pl.BlockSpec(memory_space=pl.ANY)] * 3
        + [pl.BlockSpec(memory_space=pltpu.VMEM)] * 2,
        scratch_shapes=[
            pltpu.VMEM((2, groups, SUBS, 4 * LANES), jnp.float32),
            pltpu.VMEM((2, groups, SUBS, 4 * LANES), jnp.float32),
            pltpu.VMEM((2, groups, SUBS, size), jnp.float32),
            pltpu.VMEM((2, groups, SUBS, size), jnp.float32),
            pltpu.VMEM((groups, SUBS, LANES), jnp.float32),
            pltpu.VMEM((groups, SUBS, LANES), jnp.float32),
            pltpu.VMEM((moved, size), jnp.bfloat16),
            pltpu.VMEM((blocks * PACK, LANES), jnp.bfloat16),
            pltpu.VMEM((len(grams), 2 * LANES, size), jnp.float32),
            pltpu.SemaphoreType.DMA((len(grams),)),
            pltpu.SemaphoreType.DMA((2 + blocks,)),
        ],
        compiler_params=pltpu.CompilerParams(vmem_limit_bytes=VMEM_LIMIT),
        cost_estimate=pl.CostEstimate(
            flops=size, bytes_accessed=size, transcendentals=0
        ),
        name="jacobi_turns",
    )(plan, *grams, matrix)


def gram_spans(rows):
    spans = []
    start = 0
    while start < rows:
        wanted = GRAM_PARTS[len(spans)] if len(spans) < len(GRAM_PARTS) else GRAM_TILE
        spans.append((start, min(wanted, rows - start)))
        start += spans[-1][1]
    return spans


def gram_kernel(matrix_ref, packed_ref, raw_ref, held, upper_ref, corner_ref, sems, raw_sem):
    rows = held.shape[0]
    copies = []
    spans = gram_spans(rows)
    for index, (start, count) in enumerate(spans):
        part = pl.ds(start, count)
        copies.append(pltpu.make_async_copy(matrix_ref.at[part], held.at[part], sems.at[index]))
    for copy in copies[:IN_FLIGHT]:
        copy.start()
    early = pl.ds(0, RAW_ROWS)
    leave = pltpu.make_async_copy(held.at[early], raw_ref, raw_sem)
    for index, copy in enumerate(copies):
        copy.wait()
        if index + IN_FLIGHT < len(copies):
            copies[index + IN_FLIGHT].start()
        start, count = spans[index]
        if start + count == RAW_ROWS:
            leave.start()
        values = held[start : start + count]
        right = values[:, 2 * LANES :]
        upper = dot32(values[:, : 2 * LANES], values, ((0,), (0,)))
        corner = dot32(right, right, ((0,), (0,)))
        if index == 0:
            upper_ref[...] = upper
            corner_ref[...] = corner
        else:
            upper_ref[...] += upper
            corner_ref[...] += corner
    packed_ref[:LANES] = upper_ref[:LANES]
    packed_ref[LANES:, : 2 * LANES] = upper_ref[LANES:, LANES:]
    packed_ref[LANES:, 2 * LANES :] = corner_ref[...]
    leave.wait()


def gram_blocks(matrix):
    rows, size = matrix.shape
    return pl.pallas_call(
        gram_kernel,
        in_specs=[pl.BlockSpec(memory_space=pl.ANY)],
        out_specs=[pl.BlockSpec(memory_space=pltpu.VMEM), pl.BlockSpec(memory_space=pl.ANY)],
        out_shape=(
            jax.ShapeDtypeStruct((2 * LANES, size), jnp.float32),
            jax.ShapeDtypeStruct((RAW_ROWS, size), jnp.bfloat16),
        ),
        scratch_shapes=[
            pltpu.VMEM((rows, size), jnp.bfloat16),
            pltpu.VMEM((2 * LANES, size), jnp.float32),
            pltpu.VMEM((LANES, LANES), jnp.float32),
            pltpu.SemaphoreType.DMA((len(gram_spans(rows)),)),
            pltpu.SemaphoreType.DMA,
        ],
        compiler_params=pltpu.CompilerParams(vmem_limit_bytes=VMEM_LIMIT),
        cost_estimate=pl.CostEstimate(
            flops=2 * rows * size * size, bytes_accessed=2 * rows * size, transcendentals=0
        ),
        name="gram_blocks",
    )(matrix)


def place_main(slot, out_ref, rows, slow_main, near_main):
    @pl.when(slot == 0)
    def _():
        out_ref[rows, :LANES] = slow_main
        out_ref[rows, 2 * LANES :] = near_main

    @pl.when(slot != 0)
    def _():
        out_ref[rows, :LANES] = near_main
        out_ref[rows, 2 * LANES :] = slow_main


def slot_lanes(slot, rows):
    lane = lax.broadcasted_iota(jnp.int32, (rows, LANES), 1)
    return (lane // (LANES // 2)) == slot


def fill_kernel(plan_ref, near_ref, near_turn_ref, *refs):
    slow_refs, out_ref = refs[:-2], refs[-1]
    half = UNIT // 2
    slot = moves(plan_ref)[3]
    mask = slot_lanes(slot, half)
    middle = slice(LANES, 2 * LANES)
    for unit, slow_ref in enumerate(slow_refs):
        start = unit * UNIT
        rows = slice(start, start + UNIT)
        near = dot32(near_ref[rows], near_turn_ref[...])
        place_main(slot, out_ref, rows, slow_ref[:UNIT], near[:, LANES:].astype(jnp.bfloat16))
        slow = slow_ref[UNIT:].astype(jnp.float32)
        top = jnp.where(mask, slow, near[:half, :LANES])
        low = jnp.where(mask, pltpu.roll(slow, LANES // 2, 1), near[half:, :LANES])
        out_ref[start : start + half, middle] = top.astype(jnp.bfloat16)
        out_ref[start + half : start + UNIT, middle] = low.astype(jnp.bfloat16)


def raw_kernel(plan_ref, near_ref, near_turn_ref, slow_ref, slow_turn_ref, out_ref):
    size = slow_ref.shape[1]
    slot = moves(plan_ref)[3]
    mask = slot_lanes(slot, UNIT)
    slow_turn = jnp.concatenate([slow_turn_ref[:size], slow_turn_ref[size:]], axis=1)
    for unit in range(out_ref.shape[0] // UNIT):
        rows = slice(unit * UNIT, (unit + 1) * UNIT)
        near = dot32(near_ref[rows], near_turn_ref[...])
        slow = dot32(slow_ref[rows], slow_turn)
        near_main = near[:, LANES:].astype(jnp.bfloat16)
        place_main(slot, out_ref, rows, slow[:, LANES:].astype(jnp.bfloat16), near_main)
        middle = jnp.where(mask, slow[:, :LANES], near[:, :LANES])
        out_ref[rows, LANES : 2 * LANES] = middle.astype(jnp.bfloat16)


def fill_rows(kernel, plan, sources, specs, near, near_turn, result, start, count):
    shape = near.shape
    first = start // FILL_TILE
    operands = [plan, near, near_turn, *sources]
    row_spec = pl.BlockSpec((FILL_TILE, shape[1]), lambda i: (first + i, 0))
    in_specs = [
        pl.BlockSpec(memory_space=pltpu.SMEM),
        row_spec,
        pl.BlockSpec(near_turn.shape, lambda i: (0, 0)),
        *specs,
    ]
    aliases = {}
    if result is not None:
        aliases = {len(operands): 0}
        operands.append(result)
        in_specs.append(pl.BlockSpec(memory_space=pl.ANY))
    return pl.pallas_call(
        kernel,
        grid=(count // FILL_TILE,),
        in_specs=in_specs,
        out_specs=row_spec,
        out_shape=jax.ShapeDtypeStruct(shape, jnp.bfloat16),
        input_output_aliases=aliases,
        compiler_params=pltpu.CompilerParams(vmem_limit_bytes=FILL_VMEM_LIMIT),
        cost_estimate=pl.CostEstimate(
            flops=count * shape[1], bytes_accessed=4 * count * shape[1], transcendentals=0
        ),
        name="fill_rows",
    )(*operands)


def swapped_with(value, axis, partner):
    count = lax.axis_size(axis)
    return lax.ppermute(value, axis, [(source, partner(source, count)) for source in range(count)])


def slow_partner(source, count):
    return (source + 1) % count if source % 2 else (source + count - 1) % count


def fast_partner(source, count):
    return source ^ 1


def permuted(value, pairs):
    return lax.ppermute(value, "blk", pairs)


def joined(pieces):
    values = pieces.astype(jnp.float32)
    row = lax.broadcasted_iota(jnp.int32, (SUBS, LANES), 0)
    off = values[0:1] + values[1:2] + values[2:3]
    diag = values[3:4] + values[4:5] + values[5:6]
    return jnp.where(row == 0, off, diag)


def add_pairs(left, right):
    total = left[0] + right[0]
    moved = total - left[0]
    lost = (left[0] - (total - moved)) + (right[0] - moved)
    small = left[1] + right[1] + lost
    high = total + small
    return high, small - (high - total)


def cycle_sums(mine, theirs):
    count = lax.axis_size("blk")
    zero = jnp.zeros((SUBS, LANES), jnp.float32)
    sums = add_pairs((joined(mine), zero), (joined(theirs), zero))
    step = 1
    while step < count:
        if step != 2:
            pairs = [(place, place ^ step) for place in range(count)]
            moved = permuted(jnp.concatenate(sums, axis=0), pairs)
            sums = add_pairs(sums, (moved[:SUBS], moved[SUBS:]))
        step *= 2
    return sums[0]


def on_device(matrix, plan):
    rows, size = matrix.shape
    own, early = gram_blocks(matrix)
    matrix_after, own = lax.optimization_barrier((matrix, own))
    if lax.axis_size("rows") == 2:
        other = swapped_with(own, "rows", fast_partner)
        grams = [own, other]
    else:
        grams = [lax.psum(own, "rows")]
    raw = swapped_with(early, "blk", slow_partner)
    near = swapped_with(matrix_after, "blk", fast_partner)
    head, first, last, near_turn, sums = jacobi(plan, grams, matrix)

    head = swapped_with(head, "blk", slow_partner)
    first = swapped_with(first, "blk", slow_partner)
    last = swapped_with(last, "blk", slow_partner)
    near_turn = swapped_with(near_turn, "blk", fast_partner)
    theirs = head[PACK:]
    theirs, near_turn, raw, near = lax.optimization_barrier((theirs, near_turn, raw, near))
    totals = cycle_sums(sums, theirs)
    off_ratio = jnp.sqrt(totals[0, 0] / totals[1, 0])

    def pack_specs(skip):
        units = FILL_TILE // UNIT
        return [
            pl.BlockSpec((PACK, LANES), lambda i, unit=unit: (skip + units * i + unit, 0))
            for unit in range(units)
        ]

    units = FILL_TILE // UNIT
    turn_spec = pl.BlockSpec((PACK, LANES), lambda i: (0, 0))
    raw_spec = pl.BlockSpec((FILL_TILE, size), lambda i: (i, 0))
    middle = rows - RAW_ROWS - LAST_ROWS
    result = fill_rows(
        raw_kernel, plan, [raw, head], [raw_spec, turn_spec], near, near_turn, None, 0, RAW_ROWS
    )
    result = fill_rows(
        fill_kernel, plan, [first] * units, pack_specs(0), near, near_turn, result, RAW_ROWS, middle
    )
    result = fill_rows(
        fill_kernel, plan, [last] * units, pack_specs(0), near, near_turn, result,
        rows - LAST_ROWS, LAST_ROWS,
    )
    return result, off_ratio


def solution(mesh):
    in_specs = (P("rows", "blk"), P())
    out_specs = (P("rows", "blk"), P())
    return jax.shard_map(
        on_device, mesh=mesh, in_specs=in_specs, out_specs=out_specs, check_vma=False
    )
```

```python
import jax
import jax.numpy as jnp
from jax import lax
from jax.experimental import pallas as pl
from jax.experimental.pallas import tpu as pltpu
from jax.sharding import PartitionSpec as P

ROUNDS = 24
LANES = 128
SUBS = 8
UNIT = 512
PACK = UNIT + UNIT // 2
GRAM_PARTS = (512, 1024)
GRAM_TILE = 1536
RAW_ROWS = 1536
LAST_ROWS = 1536
WIDE_TILE = 1536
SUM_ROWS = 16
IN_FLIGHT = 2
VMEM_LIMIT = 60 * 1024 * 1024
FILL_VMEM_LIMIT = 32 * 1024 * 1024


def split_three(values):
    high = values.astype(jnp.bfloat16)
    rest = values - high.astype(jnp.float32)
    middle = rest.astype(jnp.bfloat16)
    low = (rest - middle.astype(jnp.float32)).astype(jnp.bfloat16)
    return high, middle, low


def dot32(left, right, dims=((1,), (0,))):
    return lax.dot_general(left, right, (dims, ((), ())), preferred_element_type=jnp.float32)


def slot_of_row(rows, groups, half):
    part = rows // half
    inside = rows % half
    index = (inside % SUBS) * groups + inside // SUBS
    return jnp.where(part == 0, index, 2 * half - 1 - index)


def slot_of_lane(lanes, half):
    part = lanes // (2 * LANES)
    odd = (lanes // LANES) % 2
    inside = lanes % LANES
    index = 2 * inside + odd
    slot = jnp.where(part == 0, index, 2 * half - 1 - index)
    return jnp.where(inside < half // 2, slot, -1)


def onehot(left, right):
    return jnp.where(left == right, 1.0, 0.0).astype(jnp.bfloat16)


def angles(head, tail, coupling):
    difference = head - tail
    sign_val = jnp.where(difference >= 0.0, 1.0, -1.0)
    across = 2.0 * coupling * sign_val
    along = jnp.abs(difference)
    scale = jnp.maximum(along, jnp.abs(across))
    empty = scale == 0.0
    inverse = 1.0 / jnp.where(empty, 1.0, scale)
    along = jnp.where(empty, 1.0, along * inverse)
    across = across * inverse
    square = along * along + across * across
    root = lax.rsqrt(square)
    root = root * (1.5 - 0.5 * square * root * root)
    cos_sq = 0.5 + 0.5 * (along * root)
    half_root = lax.rsqrt(cos_sq)
    half_root = half_root * (1.5 - 0.5 * cos_sq * half_root * half_root)
    return cos_sq * half_root, 0.5 * (across * root) * half_root


def full_gram(packed):
    first = packed[:LANES]
    block01, block02 = first[:, LANES : 2 * LANES], first[:, 2 * LANES :]
    block12 = packed[LANES:, LANES : 2 * LANES]
    second = jnp.concatenate([block01.T, packed[LANES:, : 2 * LANES]], axis=1)
    third = jnp.concatenate([block02.T, block12.T, packed[LANES:, 2 * LANES :]], axis=1)
    return jnp.concatenate([first, second, third], axis=0)


def send_columns(lanes, base, slot, width):
    section = lanes // LANES
    lane = lanes % LANES
    rest = width - LANES
    main_start = base + jnp.where(slot == 0, 0, rest)
    rest_start = base + jnp.where(slot == 0, LANES, 0)
    high = (section // 2 + slot) % 2
    inside = lane - high * (LANES - rest)
    mixed = jnp.where((inside >= 0) & (inside < rest), rest_start + inside, -1)
    return jnp.where(section == 1, main_start + lane, mixed)


def block_sums(packed):
    squares = packed * packed
    total = jnp.zeros((1, 1), jnp.float32)
    diag_sq = jnp.zeros((1, 1), jnp.float32)
    rows = lax.broadcasted_iota(jnp.int32, (LANES, LANES), 0)
    cols = lax.broadcasted_iota(jnp.int32, (LANES, LANES), 1)
    for row, col, weight in (
        (0, 0, 1.0), (0, 1, 2.0), (0, 2, 2.0), (1, 0, 1.0), (1, 1, 2.0), (1, 2, 1.0)
    ):
        block = squares[row * LANES : (row + 1) * LANES, col * LANES : (col + 1) * LANES]
        total = total + weight * jnp.sum(block, keepdims=True)
        if weight == 1.0:
            diag_sq = diag_sq + jnp.sum(jnp.where(rows == cols, block, 0.0), keepdims=True)
    row = lax.broadcasted_iota(jnp.int32, (SUM_ROWS, LANES), 0)
    pieces = jnp.zeros((SUM_ROWS, LANES), jnp.float32)
    for index, piece in enumerate(split_three(total - diag_sq) + split_three(diag_sq)):
        pieces = jnp.where(row == index, piece.astype(jnp.float32), pieces)
    return pieces.astype(jnp.bfloat16)


def pack_unit(values, turn, packed_ref, at):
    half = UNIT // 2
    top = dot32(values[:half], turn[:, : 2 * LANES])
    low = dot32(values[half:], turn[:, LANES:])
    packed_ref[at : at + half] = top[:, LANES:].astype(jnp.bfloat16)
    packed_ref[at + half : at + UNIT] = low[:, :LANES].astype(jnp.bfloat16)
    packed_ref[at + UNIT : at + PACK] = (top[:, :LANES] + low[:, LANES:]).astype(jnp.bfloat16)


def moves(plan_ref):
    count = plan_ref.shape[0] // 2
    position = lax.axis_index("blk")
    slow_dev = lax.rem(position + 2 * lax.rem(position, 2) - 1 + count, count)
    mine = plan_ref[2 * position], plan_ref[2 * position + 1]
    theirs = plan_ref[2 * slow_dev], plan_ref[2 * slow_dev + 1]
    first_slow = mine[0] // 2 == slow_dev
    slow_slot = lax.rem(jnp.where(first_slow, mine[0], mine[1]), 2)
    fast_slot = lax.rem(jnp.where(first_slow, mine[1], mine[0]), 2)
    in_slot = lax.rem(jnp.where(theirs[0] // 2 == position, theirs[0], theirs[1]), 2)
    return first_slow, slow_slot, fast_slot, in_slot


def jacobi_kernel(plan_ref, *refs):
    jacobi_body(plan_ref, refs[:-17], *refs[-17:])


def jacobi_body(
    plan_ref, gram_refs, matrix_ref, head_ref, first_ref, last_ref, fast_ref, sums_ref,
    gram_a, gram_b, basis_a, basis_b, cos_buf, sin_buf, held, packs, gram_held, gram_sems, sems,
):
    gram_copies = [
        pltpu.make_async_copy(ref, gram_held.at[index], gram_sems.at[index])
        for index, ref in enumerate(gram_refs)
    ]
    for copy in gram_copies:
        copy.start()
    matrix_copy = pltpu.make_async_copy(matrix_ref.at[pl.ds(RAW_ROWS, held.shape[0])], held, sems.at[0])
    size = gram_refs[0].shape[1]
    half = size // 2
    groups = half // SUBS
    last = groups - 1
    edge = half // 2 - 1
    lane_row = lax.broadcasted_iota(jnp.int32, (1, LANES), 1)
    lane = lax.broadcasted_iota(jnp.int32, (SUBS, LANES), 1)
    sub = lax.broadcasted_iota(jnp.int32, (SUBS, LANES), 0)
    spot = lane - sub * (groups // 2)

    def on_diag(group):
        return spot == group // 2

    row_slot = slot_of_row(lax.broadcasted_iota(jnp.int32, (size, 1), 0), groups, half)
    take_rows = onehot(row_slot, lax.broadcasted_iota(jnp.int32, (size, size), 1))
    lane_slot = slot_of_lane(lax.broadcasted_iota(jnp.int32, (1, 4 * LANES), 1), half)
    take_cols = onehot(lax.broadcasted_iota(jnp.int32, (size, 4 * LANES), 0), lane_slot)
    arranged = jnp.zeros((size, 4 * LANES), jnp.float32)
    for copy in gram_copies:
        copy.wait()
    matrix_copy.start()
    packed = gram_held[0]
    for index in range(1, len(gram_refs)):
        packed = packed + gram_held[index]
    gram_sum = full_gram(packed)
    sums_ref[...] = block_sums(packed)
    for piece in split_three(gram_sum):
        moved = dot32(take_rows, piece).astype(jnp.bfloat16)
        arranged = arranged + dot32(moved, take_cols)
    gram_a[...] = arranged.reshape(2, groups, SUBS, 4 * LANES)
    basis_a[...] = take_rows.astype(jnp.float32).reshape(2, groups, SUBS, size)

    zero = jnp.zeros((SUBS, LANES), jnp.float32)
    heads, tails, couplings = [zero, zero], [zero, zero], [zero, zero]
    for group in range(groups):
        odd = group % 2
        mask = on_diag(group)
        lead_cols = slice(odd * LANES, (odd + 1) * LANES)
        tail_cols = slice((2 + odd) * LANES, (3 + odd) * LANES)
        heads[odd] += jnp.where(mask, gram_a[0, group, :, lead_cols], 0.0)
        tails[odd] += jnp.where(mask, gram_a[1, group, :, tail_cols], 0.0)
        couplings[odd] += jnp.where(mask, gram_a[0, group, :, tail_cols], 0.0)

    def flat(values):
        return jnp.sum(values, axis=0, keepdims=True)

    def shift_lanes(lead, tail):
        lead0, lead1 = lead[:, :LANES], lead[:, LANES:]
        tail0, tail1 = tail[:, :LANES], tail[:, LANES:]
        here = lane[: lead.shape[0]]
        new_lead1 = jnp.where(here == 0, tail0, lead0)
        new_lead0 = jnp.where(here == 0, lead0, pltpu.roll(lead1, 1, 1))
        new_tail1 = jnp.where(here == edge, lead1, pltpu.roll(tail0, LANES - 1, 1))
        return new_lead0, new_lead1, tail1, new_tail1

    def turn(gram_from, gram_to, basis_from, basis_to, carry):
        heads, tails, couplings = carry
        cosines, sines, new_heads, new_tails = [], [], [], []
        for odd in range(2):
            head, tail = heads[odd], tails[odd]
            coupling = flat(couplings[odd])
            cosine, sine_val = angles(head, tail, coupling)
            cosines.append(cosine)
            sines.append(sine_val)
            first = cosine * head + sine_val * coupling
            second = cosine * coupling + sine_val * tail
            new_heads.append(cosine * first + sine_val * second)
            first = cosine * coupling - sine_val * head
            second = cosine * tail - sine_val * coupling
            new_tails.append(cosine * second - sine_val * first)
        shifted_diag = shift_lanes(
            jnp.concatenate([jnp.broadcast_to(x, (SUBS, LANES)) for x in new_heads], axis=1),
            jnp.concatenate([jnp.broadcast_to(x, (SUBS, LANES)) for x in new_tails], axis=1),
        )
        shifted_diag = [x[:1] for x in shifted_diag]
        cos_lanes = [jnp.broadcast_to(x, (SUBS, LANES)) for x in cosines]
        sin_lanes = [jnp.broadcast_to(x, (SUBS, LANES)) for x in sines]
        cos_wide = jnp.concatenate(cos_lanes, axis=1)
        sin_wide = jnp.concatenate(sin_lanes, axis=1)

        for group in range(groups):
            mask = on_diag(group)
            odd = group % 2
            for buf, lanes in ((cos_buf, cos_lanes[odd]), (sin_buf, sin_lanes[odd])):
                picked = jnp.sum(jnp.where(mask, lanes, 0.0), axis=1, keepdims=True)
                buf[group] = jnp.broadcast_to(picked, (SUBS, LANES))

        def work(group):
            cos_row = jnp.concatenate([cos_buf[group]] * 2, axis=1)
            sin_row = jnp.concatenate([sin_buf[group]] * 2, axis=1)
            cos_base = jnp.concatenate([cos_buf[group]] * (size // LANES), axis=1)
            sin_base = jnp.concatenate([sin_buf[group]] * (size // LANES), axis=1)

            def turned(part):
                values = gram_from[part, group]
                lead, tail = values[:, : 2 * LANES], values[:, 2 * LANES :]
                return cos_wide * lead + sin_wide * tail, cos_wide * tail - sin_wide * lead

            top_lead, top_tail = turned(0)
            low_lead, low_tail = turned(1)
            top = shift_lanes(
                cos_row * top_lead + sin_row * low_lead, cos_row * top_tail + sin_row * low_tail
            )
            low = shift_lanes(
                cos_row * low_lead - sin_row * top_lead, cos_row * low_tail - sin_row * top_tail
            )
            lead = basis_from[0, group]
            tail = basis_from[1, group]
            base_top = cos_base * lead + sin_base * tail
            base_low = cos_base * tail - sin_base * lead
            return (
                list(top) + [base_top[:, i : i + LANES] for i in range(0, size, LANES)],
                list(low) + [base_low[:, i : i + LANES] for i in range(0, size, LANES)],
            )

        sums = [zero, zero]

        def store(part, group, values):
            for index, value in enumerate(values[:4]):
                gram_to[part, group, :, index * LANES : (index + 1) * LANES] = value
            for index, value in enumerate(values[4:]):
                basis_to[part, group, :, index * LANES : (index + 1) * LANES] = value
            if part == 0:
                odd = group % 2
                sums[odd] += jnp.where(on_diag(group), values[2 + odd], 0.0)

        first_top, first_low = work(0)
        last_top, last_low = work(last)
        store(0, 1, [jnp.where(sub == 0, y, x) for x, y in zip(first_top, first_low)])
        store(0, 0, [jnp.where(sub == 0, x, pltpu.roll(y, 1, 0)) for x, y in zip(first_top, last_top)])
        store(1, last, [
            jnp.where(sub == SUBS - 1, y, pltpu.roll(x, SUBS - 1, 0))
            for x, y in zip(first_low, last_top)
        ])
        store(1, last - 1, last_low)
        for group in range(1, last):
            top, low = work(group)
            store(0, group + 1, top)
            store(1, group - 1, low)
        return (
            (shifted_diag[0], shifted_diag[1]), (shifted_diag[2], shifted_diag[3]), tuple(sums)
        )

    start = (
        tuple(flat(x) for x in heads), tuple(flat(x) for x in tails), tuple(couplings)
    )

    def two_turns(_, carry):
        carry = turn(gram_a, gram_b, basis_a, basis_b, carry)
        return turn(gram_b, gram_a, basis_b, basis_a, carry)

    lax.fori_loop(0, ROUNDS // 2, two_turns, start)

    held_slot = jnp.where(row_slot == 0, 0, 1 + (row_slot + (size - 2 - ROUNDS % (size - 1))) % (size - 1))
    basis = basis_a[...].reshape(size, size).astype(jnp.bfloat16)
    lanes = lax.broadcasted_iota(jnp.int32, (1, size), 1)
    first_slow, slow_slot, fast_slot, _ = moves(plan_ref)
    slow_base = jnp.where(first_slow, 0, half)
    def turned(base, slot):
        place = onehot(held_slot, send_columns(lanes, base, slot, half))
        return dot32(basis, place, ((0,), (0,))).astype(jnp.bfloat16)

    fast_ref[...] = turned(half - slow_base, fast_slot)
    slow = turned(slow_base, slow_slot)
    packs[:size] = slow[:, :LANES]
    packs[size : 2 * size] = slow[:, LANES : 2 * LANES]
    matrix_copy.wait()
    copies = []

    def leave(start, count, ref):
        copies.append(
            pltpu.make_async_copy(packs.at[pl.ds(start, count)], ref, sems.at[1 + len(copies)])
        )
        copies[-1].start()

    leave(0, PACK, head_ref.at[pl.ds(0, PACK)])
    copies.append(pltpu.make_async_copy(sums_ref, head_ref.at[pl.ds(PACK, SUM_ROWS)], sems.at[2]))
    copies[-1].start()
    first_count = first_ref.shape[0]
    for unit in range(held.shape[0] // UNIT):
        at = (1 + unit) * PACK
        pack_unit(held[unit * UNIT : (unit + 1) * UNIT], slow, packs, at)
        place = unit * PACK
        if place < first_count:
            leave(at, PACK, first_ref.at[pl.ds(place, PACK)])
        else:
            leave(at, PACK, last_ref.at[pl.ds(place - first_count, PACK)])
    for copy in copies:
        copy.wait()


def jacobi(plan, grams, matrix):
    rows, size = matrix.shape
    groups = size // 2 // SUBS
    moved = rows - RAW_ROWS
    blocks = 1 + moved // UNIT
    last = LAST_ROWS // UNIT * PACK
    return pl.pallas_call(
        jacobi_kernel,
        out_shape=(
            jax.ShapeDtypeStruct((PACK + SUM_ROWS, LANES), jnp.bfloat16),
            jax.ShapeDtypeStruct(((blocks - 1) * PACK - last, LANES), jnp.bfloat16),
            jax.ShapeDtypeStruct((last, LANES), jnp.bfloat16),
            jax.ShapeDtypeStruct((size, size), jnp.bfloat16),
            jax.ShapeDtypeStruct((SUM_ROWS, LANES), jnp.bfloat16),
        ),
        in_specs=[pl.BlockSpec(memory_space=pltpu.SMEM)]
        + [pl.BlockSpec(memory_space=pl.ANY)] * (len(grams) + 1),
        out_specs=[pl.BlockSpec(memory_space=pl.ANY)] * 3
        + [pl.BlockSpec(memory_space=pltpu.VMEM)] * 2,
        scratch_shapes=[
            pltpu.VMEM((2, groups, SUBS, 4 * LANES), jnp.float32),
            pltpu.VMEM((2, groups, SUBS, 4 * LANES), jnp.float32),
            pltpu.VMEM((2, groups, SUBS, size), jnp.float32),
            pltpu.VMEM((2, groups, SUBS, size), jnp.float32),
            pltpu.VMEM((groups, SUBS, LANES), jnp.float32),
            pltpu.VMEM((groups, SUBS, LANES), jnp.float32),
            pltpu.VMEM((moved, size), jnp.bfloat16),
            pltpu.VMEM((blocks * PACK, LANES), jnp.bfloat16),
            pltpu.VMEM((len(grams), 2 * LANES, size), jnp.float32),
            pltpu.SemaphoreType.DMA((len(grams),)),
            pltpu.SemaphoreType.DMA((2 + blocks,)),
        ],
        compiler_params=pltpu.CompilerParams(vmem_limit_bytes=VMEM_LIMIT),
        cost_estimate=pl.CostEstimate(
            flops=size, bytes_accessed=size, transcendentals=0
        ),
        name="jacobi_turns",
    )(plan, *grams, matrix)


def gram_spans(rows):
    spans = []
    start = 0
    while start < rows:
        wanted = GRAM_PARTS[len(spans)] if len(spans) < len(GRAM_PARTS) else GRAM_TILE
        spans.append((start, min(wanted, rows - start)))
        start += spans[-1][1]
    return spans


def gram_kernel(matrix_ref, packed_ref, raw_ref, held, upper_ref, corner_ref, sems, raw_sem):
    rows = held.shape[0]
    copies = []
    spans = gram_spans(rows)
    for index, (start, count) in enumerate(spans):
        part = pl.ds(start, count)
        copies.append(pltpu.make_async_copy(matrix_ref.at[part], held.at[part], sems.at[index]))
    for copy in copies[:IN_FLIGHT]:
        copy.start()
    early = pl.ds(0, RAW_ROWS)
    leave = pltpu.make_async_copy(held.at[early], raw_ref, raw_sem)
    for index, copy in enumerate(copies):
        copy.wait()
        if index + IN_FLIGHT < len(copies):
            copies[index + IN_FLIGHT].start()
        start, count = spans[index]
        if start + count == RAW_ROWS:
            leave.start()
        values = held[start : start + count]
        right = values[:, 2 * LANES :]
        upper = dot32(values[:, : 2 * LANES], values, ((0,), (0,)))
        corner = dot32(right, right, ((0,), (0,)))
        if index == 0:
            upper_ref[...] = upper
            corner_ref[...] = corner
        else:
            upper_ref[...] += upper
            corner_ref[...] += corner
    packed_ref[:LANES] = upper_ref[:LANES]
    packed_ref[LANES:, : 2 * LANES] = upper_ref[LANES:, LANES:]
    packed_ref[LANES:, 2 * LANES :] = corner_ref[...]
    leave.wait()


def gram_blocks(matrix):
    rows, size = matrix.shape
    return pl.pallas_call(
        gram_kernel,
        in_specs=[pl.BlockSpec(memory_space=pl.ANY)],
        out_specs=[pl.BlockSpec(memory_space=pltpu.VMEM), pl.BlockSpec(memory_space=pl.ANY)],
        out_shape=(
            jax.ShapeDtypeStruct((2 * LANES, size), jnp.float32),
            jax.ShapeDtypeStruct((RAW_ROWS, size), jnp.bfloat16),
        ),
        scratch_shapes=[
            pltpu.VMEM((rows, size), jnp.bfloat16),
            pltpu.VMEM((2 * LANES, size), jnp.float32),
            pltpu.VMEM((LANES, LANES), jnp.float32),
            pltpu.SemaphoreType.DMA((len(gram_spans(rows)),)),
            pltpu.SemaphoreType.DMA,
        ],
        compiler_params=pltpu.CompilerParams(vmem_limit_bytes=VMEM_LIMIT),
        cost_estimate=pl.CostEstimate(
            flops=2 * rows * size * size, bytes_accessed=2 * rows * size, transcendentals=0
        ),
        name="gram_blocks",
    )(matrix)


def place_main(slot, out_ref, rows, slow_main, near_main):
    @pl.when(slot == 0)
    def _():
        out_ref[rows, :LANES] = slow_main
        out_ref[rows, 2 * LANES :] = near_main

    @pl.when(slot != 0)
    def _():
        out_ref[rows, :LANES] = near_main
        out_ref[rows, 2 * LANES :] = slow_main


def slot_lanes(slot, rows):
    lane = lax.broadcasted_iota(jnp.int32, (rows, LANES), 1)
    return (lane // (LANES // 2)) == slot


def near_kernel(near_ref, turn_ref, packed_ref):
    for unit in range(near_ref.shape[0] // UNIT):
        values = near_ref[unit * UNIT : (unit + 1) * UNIT]
        pack_unit(values, turn_ref[...], packed_ref, unit * PACK)


def rotate_near(near, turn):
    rows, size = near.shape
    pack = WIDE_TILE // UNIT * PACK
    return pl.pallas_call(
        near_kernel,
        grid=(rows // WIDE_TILE,),
        in_specs=[
            pl.BlockSpec((WIDE_TILE, size), lambda i: (i, 0)),
            pl.BlockSpec((size, size), lambda i: (0, 0)),
        ],
        out_specs=pl.BlockSpec((pack, LANES), lambda i: (i, 0)),
        out_shape=jax.ShapeDtypeStruct((rows // UNIT * PACK, LANES), jnp.bfloat16),
        compiler_params=pltpu.CompilerParams(vmem_limit_bytes=FILL_VMEM_LIMIT),
        cost_estimate=pl.CostEstimate(flops=size, bytes_accessed=size, transcendentals=0),
        name="rotate_near",
    )(near, turn)


def fill_kernel(plan_ref, near_ref, slow_ref, *refs):
    out_ref = refs[-1]
    half = UNIT // 2
    slot = moves(plan_ref)[3]
    mask = slot_lanes(slot, half)
    middle = slice(LANES, 2 * LANES)
    for unit in range(out_ref.shape[0] // UNIT):
        start, at = unit * UNIT, unit * PACK
        rows = slice(start, start + UNIT)
        main, rest = slice(at, at + UNIT), slice(at + UNIT, at + PACK)
        place_main(slot, out_ref, rows, slow_ref[main], near_ref[main])
        slow = slow_ref[rest].astype(jnp.float32)
        near = near_ref[rest].astype(jnp.float32)
        out_ref[start : start + half, middle] = jnp.where(mask, slow, near).astype(jnp.bfloat16)
        low = pltpu.roll(jnp.where(mask, near, slow), LANES // 2, 1)
        out_ref[start + half : start + UNIT, middle] = low.astype(jnp.bfloat16)


def raw_kernel(plan_ref, near_ref, slow_ref, slow_turn_ref, out_ref):
    size = slow_ref.shape[1]
    half = UNIT // 2
    slot = moves(plan_ref)[3]
    mask = slot_lanes(slot, half)
    middle = slice(LANES, 2 * LANES)
    slow_turn = jnp.concatenate([slow_turn_ref[:size], slow_turn_ref[size:]], axis=1)
    for unit in range(out_ref.shape[0] // UNIT):
        start, at = unit * UNIT, unit * PACK
        rows = slice(start, start + UNIT)
        slow = dot32(slow_ref[rows], slow_turn)
        slow_main = slow[:, LANES:].astype(jnp.bfloat16)
        place_main(slot, out_ref, rows, slow_main, near_ref[at : at + UNIT])
        near = near_ref[at + UNIT : at + PACK].astype(jnp.float32)
        top = jnp.where(mask, slow[:half, :LANES], near)
        low = jnp.where(mask, slow[half:, :LANES], pltpu.roll(near, LANES // 2, 1))
        out_ref[start : start + half, middle] = top.astype(jnp.bfloat16)
        out_ref[start + half : start + UNIT, middle] = low.astype(jnp.bfloat16)


def fill_rows(kernel, plan, sources, specs, near_pack, result, shape, start, count, tile):
    first = start // tile
    operands = [plan, near_pack, *sources]
    in_specs = [
        pl.BlockSpec(memory_space=pltpu.SMEM),
        pl.BlockSpec((tile // UNIT * PACK, LANES), lambda i: (first + i, 0)),
        *specs,
    ]
    aliases = {}
    if result is not None:
        aliases = {len(operands): 0}
        operands.append(result)
        in_specs.append(pl.BlockSpec(memory_space=pl.ANY))
    return pl.pallas_call(
        kernel,
        grid=(count // tile,),
        in_specs=in_specs,
        out_specs=pl.BlockSpec((tile, shape[1]), lambda i: (first + i, 0)),
        out_shape=jax.ShapeDtypeStruct(shape, jnp.bfloat16),
        input_output_aliases=aliases,
        compiler_params=pltpu.CompilerParams(vmem_limit_bytes=FILL_VMEM_LIMIT),
        cost_estimate=pl.CostEstimate(
            flops=count * shape[1], bytes_accessed=4 * count * shape[1], transcendentals=0
        ),
        name="fill_rows",
    )(*operands)


def swapped_with(value, axis, partner):
    count = lax.axis_size(axis)
    return lax.ppermute(value, axis, [(source, partner(source, count)) for source in range(count)])


def slow_partner(source, count):
    return (source + 1) % count if source % 2 else (source + count - 1) % count


def fast_partner(source, count):
    return source ^ 1


def permuted(value, pairs):
    return lax.ppermute(value, "blk", pairs)


def joined(pieces):
    values = pieces.astype(jnp.float32)
    row = lax.broadcasted_iota(jnp.int32, (SUBS, LANES), 0)
    off = values[0:1] + values[1:2] + values[2:3]
    diag = values[3:4] + values[4:5] + values[5:6]
    return jnp.where(row == 0, off, diag)


def add_pairs(left, right):
    total = left[0] + right[0]
    moved = total - left[0]
    lost = (left[0] - (total - moved)) + (right[0] - moved)
    small = left[1] + right[1] + lost
    high = total + small
    return high, small - (high - total)


def cycle_sums(mine, theirs):
    count = lax.axis_size("blk")
    zero = jnp.zeros((SUBS, LANES), jnp.float32)
    sums = add_pairs((joined(mine), zero), (joined(theirs), zero))
    step = 1
    while step < count:
        if step != 2:
            pairs = [(place, place ^ step) for place in range(count)]
            moved = permuted(jnp.concatenate(sums, axis=0), pairs)
            sums = add_pairs(sums, (moved[:SUBS], moved[SUBS:]))
        step *= 2
    return sums[0]


def on_device(matrix, plan):
    rows, size = matrix.shape
    own, early = gram_blocks(matrix)
    matrix_after, own = lax.optimization_barrier((matrix, own))
    if lax.axis_size("rows") == 2:
        other = swapped_with(own, "rows", fast_partner)
        grams = [own, other]
    else:
        grams = [lax.psum(own, "rows")]
    raw = swapped_with(early, "blk", slow_partner)
    near = swapped_with(matrix_after, "blk", fast_partner)
    head, first, last, near_turn, sums = jacobi(plan, grams, matrix)

    head = swapped_with(head, "blk", slow_partner)
    first = swapped_with(first, "blk", slow_partner)
    last = swapped_with(last, "blk", slow_partner)
    near_turn = swapped_with(near_turn, "blk", fast_partner)
    near_pack = rotate_near(near, near_turn)
    theirs = head[PACK:]
    theirs, near_pack, raw = lax.optimization_barrier((theirs, near_pack, raw))
    totals = cycle_sums(sums, theirs)
    off_ratio = jnp.sqrt(totals[0, 0] / totals[1, 0])

    shape = (rows, size)
    turn_spec = pl.BlockSpec((PACK, LANES), lambda i: (0, 0))
    raw_spec = pl.BlockSpec((UNIT, size), lambda i: (i, 0))
    wide_spec = pl.BlockSpec((WIDE_TILE // UNIT * PACK, LANES), lambda i: (i, 0))
    last_spec = pl.BlockSpec((PACK, LANES), lambda i: (i, 0))
    middle = rows - RAW_ROWS - LAST_ROWS
    result = fill_rows(
        raw_kernel, plan, [raw, head], [raw_spec, turn_spec], near_pack, None, shape,
        0, RAW_ROWS, UNIT,
    )
    result = fill_rows(
        fill_kernel, plan, [first], [wide_spec], near_pack, result, shape,
        RAW_ROWS, middle, WIDE_TILE,
    )
    result, off_ratio = lax.optimization_barrier((result, off_ratio))
    result = fill_rows(
        fill_kernel, plan, [last], [last_spec], near_pack, result, shape,
        rows - LAST_ROWS, LAST_ROWS, UNIT,
    )
    return result, off_ratio


def solution(mesh):
    in_specs = (P("rows", "blk"), P())
    out_specs = (P("rows", "blk"), P())
    return jax.shard_map(
        on_device, mesh=mesh, in_specs=in_specs, out_specs=out_specs, check_vma=False
    )
```

```python
import jax
import jax.numpy as jnp
from jax import lax
from jax.experimental import pallas as pl
from jax.experimental.pallas import tpu as pltpu
from jax.sharding import PartitionSpec as P

ROUNDS = 24
LANES = 128
SUBS = 8
UNIT = 512
PACK = UNIT + UNIT // 2
GRAM_PARTS = (512, 1024)
GRAM_TILE = 1536
RAW_ROWS = 1536
LAST_ROWS = 1536
WIDE_TILE = 1536
SUM_ROWS = 16
IN_FLIGHT = 2
VMEM_LIMIT = 60 * 1024 * 1024
JACOBI_VMEM_LIMIT = 58 * 1024 * 1024
FILL_VMEM_LIMIT = 32 * 1024 * 1024


def split_three(values):
    high = values.astype(jnp.bfloat16)
    rest = values - high.astype(jnp.float32)
    middle = rest.astype(jnp.bfloat16)
    low = (rest - middle.astype(jnp.float32)).astype(jnp.bfloat16)
    return high, middle, low


def dot32(left, right, dims=((1,), (0,))):
    return lax.dot_general(left, right, (dims, ((), ())), preferred_element_type=jnp.float32)


def slot_of_row(rows, groups, half):
    part = rows // half
    inside = rows % half
    index = (inside % SUBS) * groups + inside // SUBS
    return jnp.where(part == 0, index, 2 * half - 1 - index)


def slot_of_lane(lanes, half):
    part = lanes // (2 * LANES)
    odd = (lanes // LANES) % 2
    inside = lanes % LANES
    index = 2 * inside + odd
    slot = jnp.where(part == 0, index, 2 * half - 1 - index)
    return jnp.where(inside < half // 2, slot, -1)


def onehot(left, right):
    return jnp.where(left == right, 1.0, 0.0).astype(jnp.bfloat16)


def angles(head, tail, coupling):
    difference = head - tail
    sign_val = jnp.where(difference >= 0.0, 1.0, -1.0)
    across = 2.0 * coupling * sign_val
    along = jnp.abs(difference)
    scale = jnp.maximum(along, jnp.abs(across))
    empty = scale == 0.0
    inverse = 1.0 / jnp.where(empty, 1.0, scale)
    along = jnp.where(empty, 1.0, along * inverse)
    across = across * inverse
    square = along * along + across * across
    root = lax.rsqrt(square)
    root = root * (1.5 - 0.5 * square * root * root)
    cos_sq = 0.5 + 0.5 * (along * root)
    half_root = lax.rsqrt(cos_sq)
    half_root = half_root * (1.5 - 0.5 * cos_sq * half_root * half_root)
    return cos_sq * half_root, 0.5 * (across * root) * half_root


def full_gram(packed):
    first = packed[:LANES]
    block01, block02 = first[:, LANES : 2 * LANES], first[:, 2 * LANES :]
    block12 = packed[LANES:, LANES : 2 * LANES]
    second = jnp.concatenate([block01.T, packed[LANES:, : 2 * LANES]], axis=1)
    third = jnp.concatenate([block02.T, block12.T, packed[LANES:, 2 * LANES :]], axis=1)
    return jnp.concatenate([first, second, third], axis=0)


def send_columns(lanes, base, slot, width):
    section = lanes // LANES
    lane = lanes % LANES
    rest = width - LANES
    main_start = base + jnp.where(slot == 0, 0, rest)
    rest_start = base + jnp.where(slot == 0, LANES, 0)
    high = (section // 2 + slot) % 2
    inside = lane - high * (LANES - rest)
    mixed = jnp.where((inside >= 0) & (inside < rest), rest_start + inside, -1)
    return jnp.where(section == 1, main_start + lane, mixed)


def block_sums(packed):
    squares = packed * packed
    total = jnp.zeros((1, 1), jnp.float32)
    diag_sq = jnp.zeros((1, 1), jnp.float32)
    rows = lax.broadcasted_iota(jnp.int32, (LANES, LANES), 0)
    cols = lax.broadcasted_iota(jnp.int32, (LANES, LANES), 1)
    for row, col, weight in (
        (0, 0, 1.0), (0, 1, 2.0), (0, 2, 2.0), (1, 0, 1.0), (1, 1, 2.0), (1, 2, 1.0)
    ):
        block = squares[row * LANES : (row + 1) * LANES, col * LANES : (col + 1) * LANES]
        total = total + weight * jnp.sum(block, keepdims=True)
        if weight == 1.0:
            diag_sq = diag_sq + jnp.sum(jnp.where(rows == cols, block, 0.0), keepdims=True)
    row = lax.broadcasted_iota(jnp.int32, (SUM_ROWS, LANES), 0)
    pieces = jnp.zeros((SUM_ROWS, LANES), jnp.float32)
    for index, piece in enumerate(split_three(total - diag_sq) + split_three(diag_sq)):
        pieces = jnp.where(row == index, piece.astype(jnp.float32), pieces)
    return pieces.astype(jnp.bfloat16)


def pack_unit(values, turn, packed_ref, at):
    half = UNIT // 2
    top = dot32(values[:half], turn[:, : 2 * LANES])
    low = dot32(values[half:], turn[:, LANES:])
    packed_ref[at : at + half] = top[:, LANES:].astype(jnp.bfloat16)
    packed_ref[at + half : at + UNIT] = low[:, :LANES].astype(jnp.bfloat16)
    packed_ref[at + UNIT : at + PACK] = (top[:, :LANES] + low[:, LANES:]).astype(jnp.bfloat16)


def moves(plan_ref):
    count = plan_ref.shape[0] // 2
    position = lax.axis_index("blk")
    slow_dev = lax.rem(position + 2 * lax.rem(position, 2) - 1 + count, count)
    mine = plan_ref[2 * position], plan_ref[2 * position + 1]
    theirs = plan_ref[2 * slow_dev], plan_ref[2 * slow_dev + 1]
    first_slow = mine[0] // 2 == slow_dev
    slow_slot = lax.rem(jnp.where(first_slow, mine[0], mine[1]), 2)
    fast_slot = lax.rem(jnp.where(first_slow, mine[1], mine[0]), 2)
    in_slot = lax.rem(jnp.where(theirs[0] // 2 == position, theirs[0], theirs[1]), 2)
    return first_slow, slow_slot, fast_slot, in_slot


def jacobi_kernel(plan_ref, *refs):
    jacobi_body(plan_ref, refs[:-15], *refs[-15:])


def jacobi_body(
    plan_ref, gram_refs, matrix_ref, head_ref, first_ref, last_ref, fast_ref, sums_ref,
    gram_a, gram_b, basis_a, basis_b, cos_buf, sin_buf, held, packs, sems,
):
    matrix_copy = pltpu.make_async_copy(matrix_ref.at[pl.ds(RAW_ROWS, held.shape[0])], held, sems.at[0])
    size = gram_refs[0].shape[1]
    half = size // 2
    groups = half // SUBS
    last = groups - 1
    edge = half // 2 - 1
    lane_row = lax.broadcasted_iota(jnp.int32, (1, LANES), 1)
    lane = lax.broadcasted_iota(jnp.int32, (SUBS, LANES), 1)
    sub = lax.broadcasted_iota(jnp.int32, (SUBS, LANES), 0)
    spot = lane - sub * (groups // 2)

    def on_diag(group):
        return spot == group // 2

    row_slot = slot_of_row(lax.broadcasted_iota(jnp.int32, (size, 1), 0), groups, half)
    take_rows = onehot(row_slot, lax.broadcasted_iota(jnp.int32, (size, size), 1))
    lane_slot = slot_of_lane(lax.broadcasted_iota(jnp.int32, (1, 4 * LANES), 1), half)
    take_cols = onehot(lax.broadcasted_iota(jnp.int32, (size, 4 * LANES), 0), lane_slot)
    arranged = jnp.zeros((size, 4 * LANES), jnp.float32)
    matrix_copy.start()
    packed = gram_refs[0][...]
    for other in gram_refs[1:]:
        packed = packed + other[...]
    gram_sum = full_gram(packed)
    sums_ref[...] = block_sums(packed)
    for piece in split_three(gram_sum):
        moved = dot32(take_rows, piece).astype(jnp.bfloat16)
        arranged = arranged + dot32(moved, take_cols)
    gram_a[...] = arranged.reshape(2, groups, SUBS, 4 * LANES)
    basis_a[...] = take_rows.astype(jnp.float32).reshape(2, groups, SUBS, size)

    zero = jnp.zeros((SUBS, LANES), jnp.float32)
    heads, tails, couplings = [zero, zero], [zero, zero], [zero, zero]
    for group in range(groups):
        odd = group % 2
        mask = on_diag(group)
        lead_cols = slice(odd * LANES, (odd + 1) * LANES)
        tail_cols = slice((2 + odd) * LANES, (3 + odd) * LANES)
        heads[odd] += jnp.where(mask, gram_a[0, group, :, lead_cols], 0.0)
        tails[odd] += jnp.where(mask, gram_a[1, group, :, tail_cols], 0.0)
        couplings[odd] += jnp.where(mask, gram_a[0, group, :, tail_cols], 0.0)

    def flat(values):
        return jnp.sum(values, axis=0, keepdims=True)

    def shift_lanes(lead, tail):
        lead0, lead1 = lead[:, :LANES], lead[:, LANES:]
        tail0, tail1 = tail[:, :LANES], tail[:, LANES:]
        here = lane[: lead.shape[0]]
        new_lead1 = jnp.where(here == 0, tail0, lead0)
        new_lead0 = jnp.where(here == 0, lead0, pltpu.roll(lead1, 1, 1))
        new_tail1 = jnp.where(here == edge, lead1, pltpu.roll(tail0, LANES - 1, 1))
        return new_lead0, new_lead1, tail1, new_tail1

    def turn(gram_from, gram_to, basis_from, basis_to, carry):
        heads, tails, couplings = carry
        cosines, sines, new_heads, new_tails = [], [], [], []
        for odd in range(2):
            head, tail = heads[odd], tails[odd]
            coupling = flat(couplings[odd])
            cosine, sine_val = angles(head, tail, coupling)
            cosines.append(cosine)
            sines.append(sine_val)
            first = cosine * head + sine_val * coupling
            second = cosine * coupling + sine_val * tail
            new_heads.append(cosine * first + sine_val * second)
            first = cosine * coupling - sine_val * head
            second = cosine * tail - sine_val * coupling
            new_tails.append(cosine * second - sine_val * first)
        shifted_diag = shift_lanes(
            jnp.concatenate([jnp.broadcast_to(x, (SUBS, LANES)) for x in new_heads], axis=1),
            jnp.concatenate([jnp.broadcast_to(x, (SUBS, LANES)) for x in new_tails], axis=1),
        )
        shifted_diag = [x[:1] for x in shifted_diag]
        cos_lanes = [jnp.broadcast_to(x, (SUBS, LANES)) for x in cosines]
        sin_lanes = [jnp.broadcast_to(x, (SUBS, LANES)) for x in sines]
        cos_wide = jnp.concatenate(cos_lanes, axis=1)
        sin_wide = jnp.concatenate(sin_lanes, axis=1)

        for group in range(groups):
            mask = on_diag(group)
            odd = group % 2
            for buf, lanes in ((cos_buf, cos_lanes[odd]), (sin_buf, sin_lanes[odd])):
                picked = jnp.sum(jnp.where(mask, lanes, 0.0), axis=1, keepdims=True)
                buf[group] = jnp.broadcast_to(picked, (SUBS, LANES))

        def work(group):
            cos_row = jnp.concatenate([cos_buf[group]] * 2, axis=1)
            sin_row = jnp.concatenate([sin_buf[group]] * 2, axis=1)
            cos_base = jnp.concatenate([cos_buf[group]] * (size // LANES), axis=1)
            sin_base = jnp.concatenate([sin_buf[group]] * (size // LANES), axis=1)

            def turned(part):
                values = gram_from[part, group]
                lead, tail = values[:, : 2 * LANES], values[:, 2 * LANES :]
                return cos_wide * lead + sin_wide * tail, cos_wide * tail - sin_wide * lead

            top_lead, top_tail = turned(0)
            low_lead, low_tail = turned(1)
            top = shift_lanes(
                cos_row * top_lead + sin_row * low_lead, cos_row * top_tail + sin_row * low_tail
            )
            low = shift_lanes(
                cos_row * low_lead - sin_row * top_lead, cos_row * low_tail - sin_row * top_tail
            )
            lead = basis_from[0, group]
            tail = basis_from[1, group]
            base_top = cos_base * lead + sin_base * tail
            base_low = cos_base * tail - sin_base * lead
            return (
                list(top) + [base_top[:, i : i + LANES] for i in range(0, size, LANES)],
                list(low) + [base_low[:, i : i + LANES] for i in range(0, size, LANES)],
            )

        sums = [zero, zero]

        def store(part, group, values):
            for index, value in enumerate(values[:4]):
                gram_to[part, group, :, index * LANES : (index + 1) * LANES] = value
            for index, value in enumerate(values[4:]):
                basis_to[part, group, :, index * LANES : (index + 1) * LANES] = value
            if part == 0:
                odd = group % 2
                sums[odd] += jnp.where(on_diag(group), values[2 + odd], 0.0)

        first_top, first_low = work(0)
        last_top, last_low = work(last)
        store(0, 1, [jnp.where(sub == 0, y, x) for x, y in zip(first_top, first_low)])
        store(0, 0, [jnp.where(sub == 0, x, pltpu.roll(y, 1, 0)) for x, y in zip(first_top, last_top)])
        store(1, last, [
            jnp.where(sub == SUBS - 1, y, pltpu.roll(x, SUBS - 1, 0))
            for x, y in zip(first_low, last_top)
        ])
        store(1, last - 1, last_low)
        for group in range(1, last):
            top, low = work(group)
            store(0, group + 1, top)
            store(1, group - 1, low)
        return (
            (shifted_diag[0], shifted_diag[1]), (shifted_diag[2], shifted_diag[3]), tuple(sums)
        )

    start = (
        tuple(flat(x) for x in heads), tuple(flat(x) for x in tails), tuple(couplings)
    )

    def two_turns(_, carry):
        carry = turn(gram_a, gram_b, basis_a, basis_b, carry)
        return turn(gram_b, gram_a, basis_b, basis_a, carry)

    lax.fori_loop(0, ROUNDS // 2, two_turns, start)

    held_slot = jnp.where(row_slot == 0, 0, 1 + (row_slot + (size - 2 - ROUNDS % (size - 1))) % (size - 1))
    basis = basis_a[...].reshape(size, size).astype(jnp.bfloat16)
    lanes = lax.broadcasted_iota(jnp.int32, (1, size), 1)
    first_slow, slow_slot, fast_slot, _ = moves(plan_ref)
    slow_base = jnp.where(first_slow, 0, half)
    def turned(base, slot):
        place = onehot(held_slot, send_columns(lanes, base, slot, half))
        return dot32(basis, place, ((0,), (0,))).astype(jnp.bfloat16)

    fast_ref[...] = turned(half - slow_base, fast_slot)
    slow = turned(slow_base, slow_slot)
    head_rows = size + half
    packs[:size] = slow[:, LANES : 2 * LANES]
    packs[size:head_rows] = slow[:half, :LANES] + slow[half:, 2 * LANES :]
    matrix_copy.wait()
    copies = []

    def leave(start, count, ref):
        copies.append(
            pltpu.make_async_copy(packs.at[pl.ds(start, count)], ref, sems.at[1 + len(copies)])
        )
        copies[-1].start()

    leave(0, head_rows, head_ref.at[pl.ds(0, head_rows)])
    tail = head_ref.at[pl.ds(head_rows, SUM_ROWS)]
    copies.append(pltpu.make_async_copy(sums_ref, tail, sems.at[2]))
    copies[-1].start()
    first_count = first_ref.shape[0]
    for unit in range(held.shape[0] // UNIT):
        at = (1 + unit) * PACK
        pack_unit(held[unit * UNIT : (unit + 1) * UNIT], slow, packs, at)
        place = unit * PACK
        if place < first_count:
            leave(at, PACK, first_ref.at[pl.ds(place, PACK)])
        else:
            leave(at, PACK, last_ref.at[pl.ds(place - first_count, PACK)])
    for copy in copies:
        copy.wait()


def jacobi(plan, grams, matrix):
    rows, size = matrix.shape
    groups = size // 2 // SUBS
    moved = rows - RAW_ROWS
    blocks = 1 + moved // UNIT
    last = LAST_ROWS // UNIT * PACK
    return pl.pallas_call(
        jacobi_kernel,
        out_shape=(
            jax.ShapeDtypeStruct((size + size // 2 + SUM_ROWS, LANES), jnp.bfloat16),
            jax.ShapeDtypeStruct(((blocks - 1) * PACK - last, LANES), jnp.bfloat16),
            jax.ShapeDtypeStruct((last, LANES), jnp.bfloat16),
            jax.ShapeDtypeStruct((size, size), jnp.bfloat16),
            jax.ShapeDtypeStruct((SUM_ROWS, LANES), jnp.bfloat16),
        ),
        in_specs=[pl.BlockSpec(memory_space=pltpu.SMEM)]
        + [pl.BlockSpec(memory_space=pltpu.VMEM)] * len(grams)
        + [pl.BlockSpec(memory_space=pl.ANY)],
        out_specs=[pl.BlockSpec(memory_space=pl.ANY)] * 3
        + [pl.BlockSpec(memory_space=pltpu.VMEM)] * 2,
        scratch_shapes=[
            pltpu.VMEM((2, groups, SUBS, 4 * LANES), jnp.float32),
            pltpu.VMEM((2, groups, SUBS, 4 * LANES), jnp.float32),
            pltpu.VMEM((2, groups, SUBS, size), jnp.float32),
            pltpu.VMEM((2, groups, SUBS, size), jnp.float32),
            pltpu.VMEM((groups, SUBS, LANES), jnp.float32),
            pltpu.VMEM((groups, SUBS, LANES), jnp.float32),
            pltpu.VMEM((moved, size), jnp.bfloat16),
            pltpu.VMEM((blocks * PACK, LANES), jnp.bfloat16),
            pltpu.SemaphoreType.DMA((2 + blocks,)),
        ],
        compiler_params=pltpu.CompilerParams(vmem_limit_bytes=JACOBI_VMEM_LIMIT),
        cost_estimate=pl.CostEstimate(
            flops=size, bytes_accessed=size, transcendentals=0
        ),
        name="jacobi_turns",
    )(plan, *grams, matrix)


def gram_spans(rows):
    spans = []
    start = 0
    while start < rows:
        wanted = GRAM_PARTS[len(spans)] if len(spans) < len(GRAM_PARTS) else GRAM_TILE
        spans.append((start, min(wanted, rows - start)))
        start += spans[-1][1]
    return spans


def gram_kernel(matrix_ref, packed_ref, raw_ref, held, upper_ref, corner_ref, sems, raw_sem):
    rows = held.shape[0]
    copies = []
    spans = gram_spans(rows)
    for index, (start, count) in enumerate(spans):
        part = pl.ds(start, count)
        copies.append(pltpu.make_async_copy(matrix_ref.at[part], held.at[part], sems.at[index]))
    for copy in copies[:IN_FLIGHT]:
        copy.start()
    early = pl.ds(0, RAW_ROWS)
    leave = pltpu.make_async_copy(held.at[early], raw_ref, raw_sem)
    for index, copy in enumerate(copies):
        copy.wait()
        if index + IN_FLIGHT < len(copies):
            copies[index + IN_FLIGHT].start()
        start, count = spans[index]
        if start + count == RAW_ROWS:
            leave.start()
        values = held[start : start + count]
        right = values[:, 2 * LANES :]
        upper = dot32(values[:, : 2 * LANES], values, ((0,), (0,)))
        corner = dot32(right, right, ((0,), (0,)))
        if index == 0:
            upper_ref[...] = upper
            corner_ref[...] = corner
        else:
            upper_ref[...] += upper
            corner_ref[...] += corner
    packed_ref[:LANES] = upper_ref[:LANES]
    packed_ref[LANES:, : 2 * LANES] = upper_ref[LANES:, LANES:]
    packed_ref[LANES:, 2 * LANES :] = corner_ref[...]
    leave.wait()


def gram_blocks(matrix):
    rows, size = matrix.shape
    return pl.pallas_call(
        gram_kernel,
        in_specs=[pl.BlockSpec(memory_space=pl.ANY)],
        out_specs=[pl.BlockSpec(memory_space=pltpu.VMEM), pl.BlockSpec(memory_space=pl.ANY)],
        out_shape=(
            jax.ShapeDtypeStruct((2 * LANES, size), jnp.float32),
            jax.ShapeDtypeStruct((RAW_ROWS, size), jnp.bfloat16),
        ),
        scratch_shapes=[
            pltpu.VMEM((rows, size), jnp.bfloat16),
            pltpu.VMEM((2 * LANES, size), jnp.float32),
            pltpu.VMEM((LANES, LANES), jnp.float32),
            pltpu.SemaphoreType.DMA((len(gram_spans(rows)),)),
            pltpu.SemaphoreType.DMA,
        ],
        compiler_params=pltpu.CompilerParams(vmem_limit_bytes=VMEM_LIMIT),
        cost_estimate=pl.CostEstimate(
            flops=2 * rows * size * size, bytes_accessed=2 * rows * size, transcendentals=0
        ),
        name="gram_blocks",
    )(matrix)


def place_main(slot, out_ref, rows, slow_main, near_main):
    @pl.when(slot == 0)
    def _():
        out_ref[rows, :LANES] = slow_main
        out_ref[rows, 2 * LANES :] = near_main

    @pl.when(slot != 0)
    def _():
        out_ref[rows, :LANES] = near_main
        out_ref[rows, 2 * LANES :] = slow_main


def slot_lanes(slot, rows):
    lane = lax.broadcasted_iota(jnp.int32, (rows, LANES), 1)
    return (lane // (LANES // 2)) == slot


def near_kernel(near_ref, turn_ref, packed_ref):
    for unit in range(near_ref.shape[0] // UNIT):
        values = near_ref[unit * UNIT : (unit + 1) * UNIT]
        pack_unit(values, turn_ref[...], packed_ref, unit * PACK)


def rotate_near(near, turn):
    rows, size = near.shape
    pack = WIDE_TILE // UNIT * PACK
    return pl.pallas_call(
        near_kernel,
        grid=(rows // WIDE_TILE,),
        in_specs=[
            pl.BlockSpec((WIDE_TILE, size), lambda i: (i, 0)),
            pl.BlockSpec((size, size), lambda i: (0, 0)),
        ],
        out_specs=pl.BlockSpec((pack, LANES), lambda i: (i, 0)),
        out_shape=jax.ShapeDtypeStruct((rows // UNIT * PACK, LANES), jnp.bfloat16),
        compiler_params=pltpu.CompilerParams(vmem_limit_bytes=FILL_VMEM_LIMIT),
        cost_estimate=pl.CostEstimate(flops=size, bytes_accessed=size, transcendentals=0),
        name="rotate_near",
    )(near, turn)


def fill_kernel(plan_ref, near_ref, slow_ref, *refs):
    out_ref = refs[-1]
    half = UNIT // 2
    slot = moves(plan_ref)[3]
    mask = slot_lanes(slot, half)
    middle = slice(LANES, 2 * LANES)
    for unit in range(out_ref.shape[0] // UNIT):
        start, at = unit * UNIT, unit * PACK
        rows = slice(start, start + UNIT)
        main, rest = slice(at, at + UNIT), slice(at + UNIT, at + PACK)
        place_main(slot, out_ref, rows, slow_ref[main], near_ref[main])
        slow = slow_ref[rest].astype(jnp.float32)
        near = near_ref[rest].astype(jnp.float32)
        out_ref[start : start + half, middle] = jnp.where(mask, slow, near).astype(jnp.bfloat16)
        low = pltpu.roll(jnp.where(mask, near, slow), LANES // 2, 1)
        out_ref[start + half : start + UNIT, middle] = low.astype(jnp.bfloat16)


def raw_kernel(plan_ref, near_ref, slow_ref, slow_turn_ref, out_ref):
    size = slow_ref.shape[1]
    half = UNIT // 2
    slot = moves(plan_ref)[3]
    mask = slot_lanes(slot, half)
    middle = slice(LANES, 2 * LANES)
    mixed = slow_turn_ref[size : size + size // 2].astype(jnp.float32)
    side = slot_lanes(slot, size // 2)
    mixed = jnp.concatenate(
        [jnp.where(side, mixed, 0.0), pltpu.roll(jnp.where(side, 0.0, mixed), LANES // 2, 1)], axis=0
    )
    slow_turn = jnp.concatenate([mixed.astype(jnp.bfloat16), slow_turn_ref[:size]], axis=1)
    for unit in range(out_ref.shape[0] // UNIT):
        start, at = unit * UNIT, unit * PACK
        rows = slice(start, start + UNIT)
        slow = dot32(slow_ref[rows], slow_turn)
        slow_main = slow[:, LANES:].astype(jnp.bfloat16)
        place_main(slot, out_ref, rows, slow_main, near_ref[at : at + UNIT])
        near = near_ref[at + UNIT : at + PACK].astype(jnp.float32)
        top = jnp.where(mask, slow[:half, :LANES], near)
        low = jnp.where(mask, slow[half:, :LANES], pltpu.roll(near, LANES // 2, 1))
        out_ref[start : start + half, middle] = top.astype(jnp.bfloat16)
        out_ref[start + half : start + UNIT, middle] = low.astype(jnp.bfloat16)


def fill_rows(kernel, plan, sources, specs, near_pack, result, shape, start, count, tile):
    first = start // tile
    operands = [plan, near_pack, *sources]
    in_specs = [
        pl.BlockSpec(memory_space=pltpu.SMEM),
        pl.BlockSpec((tile // UNIT * PACK, LANES), lambda i: (first + i, 0)),
        *specs,
    ]
    aliases = {}
    if result is not None:
        aliases = {len(operands): 0}
        operands.append(result)
        in_specs.append(pl.BlockSpec(memory_space=pl.ANY))
    return pl.pallas_call(
        kernel,
        grid=(count // tile,),
        in_specs=in_specs,
        out_specs=pl.BlockSpec((tile, shape[1]), lambda i: (first + i, 0)),
        out_shape=jax.ShapeDtypeStruct(shape, jnp.bfloat16),
        input_output_aliases=aliases,
        compiler_params=pltpu.CompilerParams(vmem_limit_bytes=FILL_VMEM_LIMIT),
        cost_estimate=pl.CostEstimate(
            flops=count * shape[1], bytes_accessed=4 * count * shape[1], transcendentals=0
        ),
        name="fill_rows",
    )(*operands)


def swapped_with(value, axis, partner):
    count = lax.axis_size(axis)
    return lax.ppermute(value, axis, [(source, partner(source, count)) for source in range(count)])


def slow_partner(source, count):
    return (source + 1) % count if source % 2 else (source + count - 1) % count


def fast_partner(source, count):
    return source ^ 1


def permuted(value, pairs):
    return lax.ppermute(value, "blk", pairs)


def joined(pieces):
    values = pieces.astype(jnp.float32)
    row = lax.broadcasted_iota(jnp.int32, (SUBS, LANES), 0)
    off = values[0:1] + values[1:2] + values[2:3]
    diag = values[3:4] + values[4:5] + values[5:6]
    return jnp.where(row == 0, off, diag)


def add_pairs(left, right):
    total = left[0] + right[0]
    moved = total - left[0]
    lost = (left[0] - (total - moved)) + (right[0] - moved)
    small = left[1] + right[1] + lost
    high = total + small
    return high, small - (high - total)


def cycle_sums(mine, theirs):
    count = lax.axis_size("blk")
    zero = jnp.zeros((SUBS, LANES), jnp.float32)
    sums = add_pairs((joined(mine), zero), (joined(theirs), zero))
    step = 1
    while step < count:
        if step != 2:
            pairs = [(place, place ^ step) for place in range(count)]
            moved = permuted(jnp.concatenate(sums, axis=0), pairs)
            sums = add_pairs(sums, (moved[:SUBS], moved[SUBS:]))
        step *= 2
    return sums[0]


def on_device(matrix, plan):
    rows, size = matrix.shape
    own, early = gram_blocks(matrix)
    matrix_after, own = lax.optimization_barrier((matrix, own))
    if lax.axis_size("rows") == 2:
        grams = [own, swapped_with(own, "rows", fast_partner)]
    else:
        grams = [lax.psum(own, "rows")]
    raw = swapped_with(early, "blk", slow_partner)
    near = swapped_with(matrix_after, "blk", fast_partner)
    head, first, last, near_turn, sums = jacobi(plan, grams, matrix)

    head = swapped_with(head, "blk", slow_partner)
    first = swapped_with(first, "blk", slow_partner)
    last = swapped_with(last, "blk", slow_partner)
    near_turn = swapped_with(near_turn, "blk", fast_partner)
    near_pack = rotate_near(near, near_turn)
    theirs = head[size + size // 2 :]
    theirs, near_pack, raw = lax.optimization_barrier((theirs, near_pack, raw))
    totals = cycle_sums(sums, theirs)
    off_ratio = jnp.sqrt(totals[0, 0] / totals[1, 0])

    shape = (rows, size)
    turn_spec = pl.BlockSpec(head.shape, lambda i: (0, 0))
    raw_spec = pl.BlockSpec((UNIT, size), lambda i: (i, 0))
    wide_spec = pl.BlockSpec((WIDE_TILE // UNIT * PACK, LANES), lambda i: (i, 0))
    last_spec = pl.BlockSpec((PACK, LANES), lambda i: (i, 0))
    middle = rows - RAW_ROWS - LAST_ROWS
    result = fill_rows(
        raw_kernel, plan, [raw, head], [raw_spec, turn_spec], near_pack, None, shape,
        0, RAW_ROWS, UNIT,
    )
    result = fill_rows(
        fill_kernel, plan, [first], [wide_spec], near_pack, result, shape,
        RAW_ROWS, middle, WIDE_TILE,
    )
    result, off_ratio = lax.optimization_barrier((result, off_ratio))
    result = fill_rows(
        fill_kernel, plan, [last], [last_spec], near_pack, result, shape,
        rows - LAST_ROWS, LAST_ROWS, UNIT,
    )
    return result, off_ratio


def solution(mesh):
    in_specs = (P("rows", "blk"), P())
    out_specs = (P("rows", "blk"), P())
    return jax.shard_map(
        on_device, mesh=mesh, in_specs=in_specs, out_specs=out_specs, check_vma=False
    )
```

```python
import jax
import jax.numpy as jnp
from jax import lax
from jax.experimental import pallas as pl
from jax.experimental.pallas import tpu as pltpu
from jax.sharding import PartitionSpec as P

ROUNDS = 24
LANES = 128
SUBS = 8
UNIT = 512
PACK = UNIT + UNIT // 2
GRAM_PARTS = (512, 1024)
GRAM_TILE = 1536
RAW_ROWS = 1536
LAST_ROWS = 1536
WIDE_TILE = 1536
SUM_ROWS = 16
IN_FLIGHT = 2
VMEM_LIMIT = 60 * 1024 * 1024
JACOBI_VMEM_LIMIT = 58 * 1024 * 1024
FILL_VMEM_LIMIT = 32 * 1024 * 1024


def split_three(values):
    high = values.astype(jnp.bfloat16)
    rest = values - high.astype(jnp.float32)
    middle = rest.astype(jnp.bfloat16)
    low = (rest - middle.astype(jnp.float32)).astype(jnp.bfloat16)
    return high, middle, low


def dot32(left, right, dims=((1,), (0,))):
    return lax.dot_general(left, right, (dims, ((), ())), preferred_element_type=jnp.float32)


def slot_of_row(rows, groups, half):
    part = rows // half
    inside = rows % half
    index = (inside % SUBS) * groups + inside // SUBS
    return jnp.where(part == 0, index, 2 * half - 1 - index)


def slot_of_lane(lanes, half):
    part = lanes // (2 * LANES)
    odd = (lanes // LANES) % 2
    inside = lanes % LANES
    index = 2 * inside + odd
    slot = jnp.where(part == 0, index, 2 * half - 1 - index)
    return jnp.where(inside < half // 2, slot, -1)


def onehot(left, right):
    return jnp.where(left == right, 1.0, 0.0).astype(jnp.bfloat16)


def angles(head, tail, coupling):
    difference = head - tail
    sign_val = jnp.where(difference >= 0.0, 1.0, -1.0)
    across = 2.0 * coupling * sign_val
    along = jnp.abs(difference)
    scale = jnp.maximum(along, jnp.abs(across))
    empty = scale == 0.0
    inverse = 1.0 / jnp.where(empty, 1.0, scale)
    along = jnp.where(empty, 1.0, along * inverse)
    across = across * inverse
    square = along * along + across * across
    root = lax.rsqrt(square)
    root = root * (1.5 - 0.5 * square * root * root)
    cos_sq = 0.5 + 0.5 * (along * root)
    half_root = lax.rsqrt(cos_sq)
    half_root = half_root * (1.5 - 0.5 * cos_sq * half_root * half_root)
    return cos_sq * half_root, 0.5 * (across * root) * half_root


def triangle():
    rows = lax.broadcasted_iota(jnp.int32, (LANES, LANES), 0)
    cols = lax.broadcasted_iota(jnp.int32, (LANES, LANES), 1)
    return rows, cols


def full_gram(packed):
    shared, block01, block02, block12, block22 = (
        packed[index * LANES : (index + 1) * LANES] for index in range(5)
    )
    diag11 = packed[5 * LANES : 5 * LANES + 1]
    rows, cols = triangle()
    flipped = shared.T
    block00 = jnp.where(rows <= cols, shared, flipped)
    block11 = jnp.where(rows > cols, shared, jnp.where(rows < cols, flipped, diag11))
    first = jnp.concatenate([block00, block01, block02], axis=1)
    second = jnp.concatenate([block01.T, block11, block12], axis=1)
    third = jnp.concatenate([block02.T, block12.T, block22], axis=1)
    return jnp.concatenate([first, second, third], axis=0)


def send_columns(lanes, base, slot, width):
    section = lanes // LANES
    lane = lanes % LANES
    rest = width - LANES
    main_start = base + jnp.where(slot == 0, 0, rest)
    rest_start = base + jnp.where(slot == 0, LANES, 0)
    high = (section // 2 + slot) % 2
    inside = lane - high * (LANES - rest)
    mixed = jnp.where((inside >= 0) & (inside < rest), rest_start + inside, -1)
    return jnp.where(section == 1, main_start + lane, mixed)


def block_sums(gram_sum):
    squares = gram_sum * gram_sum
    rows = lax.broadcasted_iota(jnp.int32, squares.shape, 0)
    cols = lax.broadcasted_iota(jnp.int32, squares.shape, 1)
    total = jnp.sum(squares, keepdims=True)
    diag_sq = jnp.sum(jnp.where(rows == cols, squares, 0.0), keepdims=True)
    row = lax.broadcasted_iota(jnp.int32, (SUM_ROWS, LANES), 0)
    pieces = jnp.zeros((SUM_ROWS, LANES), jnp.float32)
    for index, piece in enumerate(split_three(total - diag_sq) + split_three(diag_sq)):
        pieces = jnp.where(row == index, piece.astype(jnp.float32), pieces)
    return pieces.astype(jnp.bfloat16)


def pack_unit(values, turn, packed_ref, at):
    half = UNIT // 2
    top = dot32(values[:half], turn[:, : 2 * LANES])
    low = dot32(values[half:], turn[:, LANES:])
    packed_ref[at : at + half] = top[:, LANES:].astype(jnp.bfloat16)
    packed_ref[at + half : at + UNIT] = low[:, :LANES].astype(jnp.bfloat16)
    packed_ref[at + UNIT : at + PACK] = (top[:, :LANES] + low[:, LANES:]).astype(jnp.bfloat16)


def moves(plan_ref):
    count = plan_ref.shape[0] // 2
    position = lax.axis_index("blk")
    slow_dev = lax.rem(position + 2 * lax.rem(position, 2) - 1 + count, count)
    mine = plan_ref[2 * position], plan_ref[2 * position + 1]
    theirs = plan_ref[2 * slow_dev], plan_ref[2 * slow_dev + 1]
    first_slow = mine[0] // 2 == slow_dev
    slow_slot = lax.rem(jnp.where(first_slow, mine[0], mine[1]), 2)
    fast_slot = lax.rem(jnp.where(first_slow, mine[1], mine[0]), 2)
    in_slot = lax.rem(jnp.where(theirs[0] // 2 == position, theirs[0], theirs[1]), 2)
    return first_slow, slow_slot, fast_slot, in_slot


def jacobi_kernel(plan_ref, *refs):
    jacobi_body(plan_ref, refs[:-15], *refs[-15:])


def jacobi_body(
    plan_ref, gram_refs, matrix_ref, head_ref, first_ref, last_ref, fast_ref, sums_ref,
    gram_a, gram_b, basis_a, basis_b, cos_buf, sin_buf, held, packs, sems,
):
    matrix_copy = pltpu.make_async_copy(matrix_ref.at[pl.ds(RAW_ROWS, held.shape[0])], held, sems.at[0])
    size = matrix_ref.shape[1]
    half = size // 2
    groups = half // SUBS
    last = groups - 1
    edge = half // 2 - 1
    lane_row = lax.broadcasted_iota(jnp.int32, (1, LANES), 1)
    lane = lax.broadcasted_iota(jnp.int32, (SUBS, LANES), 1)
    sub = lax.broadcasted_iota(jnp.int32, (SUBS, LANES), 0)
    spot = lane - sub * (groups // 2)

    def on_diag(group):
        return spot == group // 2

    row_slot = slot_of_row(lax.broadcasted_iota(jnp.int32, (size, 1), 0), groups, half)
    take_rows = onehot(row_slot, lax.broadcasted_iota(jnp.int32, (size, size), 1))
    lane_slot = slot_of_lane(lax.broadcasted_iota(jnp.int32, (1, 4 * LANES), 1), half)
    take_cols = onehot(lax.broadcasted_iota(jnp.int32, (size, 4 * LANES), 0), lane_slot)
    arranged = jnp.zeros((size, 4 * LANES), jnp.float32)
    matrix_copy.start()
    packed = gram_refs[0][...]
    for other in gram_refs[1:]:
        packed = packed + other[...]
    gram_sum = full_gram(packed)
    sums_ref[...] = block_sums(gram_sum)
    for piece in split_three(gram_sum):
        moved = dot32(take_rows, piece).astype(jnp.bfloat16)
        arranged = arranged + dot32(moved, take_cols)
    gram_a[...] = arranged.reshape(2, groups, SUBS, 4 * LANES)
    basis_a[...] = take_rows.astype(jnp.float32).reshape(2, groups, SUBS, size)

    zero = jnp.zeros((SUBS, LANES), jnp.float32)
    heads, tails, couplings = [zero, zero], [zero, zero], [zero, zero]
    for group in range(groups):
        odd = group % 2
        mask = on_diag(group)
        lead_cols = slice(odd * LANES, (odd + 1) * LANES)
        tail_cols = slice((2 + odd) * LANES, (3 + odd) * LANES)
        heads[odd] += jnp.where(mask, gram_a[0, group, :, lead_cols], 0.0)
        tails[odd] += jnp.where(mask, gram_a[1, group, :, tail_cols], 0.0)
        couplings[odd] += jnp.where(mask, gram_a[0, group, :, tail_cols], 0.0)

    def flat(values):
        return jnp.sum(values, axis=0, keepdims=True)

    def shift_lanes(lead, tail):
        lead0, lead1 = lead[:, :LANES], lead[:, LANES:]
        tail0, tail1 = tail[:, :LANES], tail[:, LANES:]
        here = lane[: lead.shape[0]]
        new_lead1 = jnp.where(here == 0, tail0, lead0)
        new_lead0 = jnp.where(here == 0, lead0, pltpu.roll(lead1, 1, 1))
        new_tail1 = jnp.where(here == edge, lead1, pltpu.roll(tail0, LANES - 1, 1))
        return new_lead0, new_lead1, tail1, new_tail1

    def turn(gram_from, gram_to, basis_from, basis_to, carry):
        heads, tails, couplings = carry
        cosines, sines, new_heads, new_tails = [], [], [], []
        for odd in range(2):
            head, tail = heads[odd], tails[odd]
            coupling = flat(couplings[odd])
            cosine, sine_val = angles(head, tail, coupling)
            cosines.append(cosine)
            sines.append(sine_val)
            first = cosine * head + sine_val * coupling
            second = cosine * coupling + sine_val * tail
            new_heads.append(cosine * first + sine_val * second)
            first = cosine * coupling - sine_val * head
            second = cosine * tail - sine_val * coupling
            new_tails.append(cosine * second - sine_val * first)
        shifted_diag = shift_lanes(
            jnp.concatenate([jnp.broadcast_to(x, (SUBS, LANES)) for x in new_heads], axis=1),
            jnp.concatenate([jnp.broadcast_to(x, (SUBS, LANES)) for x in new_tails], axis=1),
        )
        shifted_diag = [x[:1] for x in shifted_diag]
        cos_lanes = [jnp.broadcast_to(x, (SUBS, LANES)) for x in cosines]
        sin_lanes = [jnp.broadcast_to(x, (SUBS, LANES)) for x in sines]
        cos_wide = jnp.concatenate(cos_lanes, axis=1)
        sin_wide = jnp.concatenate(sin_lanes, axis=1)

        for group in range(groups):
            mask = on_diag(group)
            odd = group % 2
            for buf, lanes in ((cos_buf, cos_lanes[odd]), (sin_buf, sin_lanes[odd])):
                picked = jnp.sum(jnp.where(mask, lanes, 0.0), axis=1, keepdims=True)
                buf[group] = jnp.broadcast_to(picked, (SUBS, LANES))

        def work(group):
            cos_row = jnp.concatenate([cos_buf[group]] * 2, axis=1)
            sin_row = jnp.concatenate([sin_buf[group]] * 2, axis=1)
            cos_base = jnp.concatenate([cos_buf[group]] * (size // LANES), axis=1)
            sin_base = jnp.concatenate([sin_buf[group]] * (size // LANES), axis=1)

            def turned(part):
                values = gram_from[part, group]
                lead, tail = values[:, : 2 * LANES], values[:, 2 * LANES :]
                return cos_wide * lead + sin_wide * tail, cos_wide * tail - sin_wide * lead

            top_lead, top_tail = turned(0)
            low_lead, low_tail = turned(1)
            top = shift_lanes(
                cos_row * top_lead + sin_row * low_lead, cos_row * top_tail + sin_row * low_tail
            )
            low = shift_lanes(
                cos_row * low_lead - sin_row * top_lead, cos_row * low_tail - sin_row * top_tail
            )
            lead = basis_from[0, group]
            tail = basis_from[1, group]
            base_top = cos_base * lead + sin_base * tail
            base_low = cos_base * tail - sin_base * lead
            return (
                list(top) + [base_top[:, i : i + LANES] for i in range(0, size, LANES)],
                list(low) + [base_low[:, i : i + LANES] for i in range(0, size, LANES)],
            )

        sums = [zero, zero]

        def store(part, group, values):
            for index, value in enumerate(values[:4]):
                gram_to[part, group, :, index * LANES : (index + 1) * LANES] = value
            for index, value in enumerate(values[4:]):
                basis_to[part, group, :, index * LANES : (index + 1) * LANES] = value
            if part == 0:
                odd = group % 2
                sums[odd] += jnp.where(on_diag(group), values[2 + odd], 0.0)

        first_top, first_low = work(0)
        last_top, last_low = work(last)
        store(0, 1, [jnp.where(sub == 0, y, x) for x, y in zip(first_top, first_low)])
        store(0, 0, [jnp.where(sub == 0, x, pltpu.roll(y, 1, 0)) for x, y in zip(first_top, last_top)])
        store(1, last, [
            jnp.where(sub == SUBS - 1, y, pltpu.roll(x, SUBS - 1, 0))
            for x, y in zip(first_low, last_top)
        ])
        store(1, last - 1, last_low)
        for group in range(1, last):
            top, low = work(group)
            store(0, group + 1, top)
            store(1, group - 1, low)
        return (
            (shifted_diag[0], shifted_diag[1]), (shifted_diag[2], shifted_diag[3]), tuple(sums)
        )

    start = (
        tuple(flat(x) for x in heads), tuple(flat(x) for x in tails), tuple(couplings)
    )

    def two_turns(_, carry):
        carry = turn(gram_a, gram_b, basis_a, basis_b, carry)
        return turn(gram_b, gram_a, basis_b, basis_a, carry)

    lax.fori_loop(0, ROUNDS // 2, two_turns, start)

    held_slot = jnp.where(row_slot == 0, 0, 1 + (row_slot + (size - 2 - ROUNDS % (size - 1))) % (size - 1))
    basis = basis_a[...].reshape(size, size).astype(jnp.bfloat16)
    lanes = lax.broadcasted_iota(jnp.int32, (1, size), 1)
    first_slow, slow_slot, fast_slot, _ = moves(plan_ref)
    slow_base = jnp.where(first_slow, 0, half)
    def turned(base, slot):
        place = onehot(held_slot, send_columns(lanes, base, slot, half))
        return dot32(basis, place, ((0,), (0,))).astype(jnp.bfloat16)

    fast_ref[...] = turned(half - slow_base, fast_slot)
    slow = turned(slow_base, slow_slot)
    head_rows = size + half
    packs[:size] = slow[:, LANES : 2 * LANES]
    packs[size:head_rows] = slow[:half, :LANES] + slow[half:, 2 * LANES :]
    matrix_copy.wait()
    copies = []

    def leave(start, count, ref):
        copies.append(
            pltpu.make_async_copy(packs.at[pl.ds(start, count)], ref, sems.at[1 + len(copies)])
        )
        copies[-1].start()

    leave(0, head_rows, head_ref.at[pl.ds(0, head_rows)])
    tail = head_ref.at[pl.ds(head_rows, SUM_ROWS)]
    copies.append(pltpu.make_async_copy(sums_ref, tail, sems.at[2]))
    copies[-1].start()
    first_count = first_ref.shape[0]
    for unit in range(held.shape[0] // UNIT):
        at = (1 + unit) * PACK
        pack_unit(held[unit * UNIT : (unit + 1) * UNIT], slow, packs, at)
        place = unit * PACK
        if place < first_count:
            leave(at, PACK, first_ref.at[pl.ds(place, PACK)])
        else:
            leave(at, PACK, last_ref.at[pl.ds(place - first_count, PACK)])
    for copy in copies:
        copy.wait()


def jacobi(plan, grams, matrix):
    rows, size = matrix.shape
    groups = size // 2 // SUBS
    moved = rows - RAW_ROWS
    blocks = 1 + moved // UNIT
    last = LAST_ROWS // UNIT * PACK
    return pl.pallas_call(
        jacobi_kernel,
        out_shape=(
            jax.ShapeDtypeStruct((size + size // 2 + SUM_ROWS, LANES), jnp.bfloat16),
            jax.ShapeDtypeStruct(((blocks - 1) * PACK - last, LANES), jnp.bfloat16),
            jax.ShapeDtypeStruct((last, LANES), jnp.bfloat16),
            jax.ShapeDtypeStruct((size, size), jnp.bfloat16),
            jax.ShapeDtypeStruct((SUM_ROWS, LANES), jnp.bfloat16),
        ),
        in_specs=[pl.BlockSpec(memory_space=pltpu.SMEM)]
        + [pl.BlockSpec(memory_space=pltpu.VMEM)] * len(grams)
        + [pl.BlockSpec(memory_space=pl.ANY)],
        out_specs=[pl.BlockSpec(memory_space=pl.ANY)] * 3
        + [pl.BlockSpec(memory_space=pltpu.VMEM)] * 2,
        scratch_shapes=[
            pltpu.VMEM((2, groups, SUBS, 4 * LANES), jnp.float32),
            pltpu.VMEM((2, groups, SUBS, 4 * LANES), jnp.float32),
            pltpu.VMEM((2, groups, SUBS, size), jnp.float32),
            pltpu.VMEM((2, groups, SUBS, size), jnp.float32),
            pltpu.VMEM((groups, SUBS, LANES), jnp.float32),
            pltpu.VMEM((groups, SUBS, LANES), jnp.float32),
            pltpu.VMEM((moved, size), jnp.bfloat16),
            pltpu.VMEM((blocks * PACK, LANES), jnp.bfloat16),
            pltpu.SemaphoreType.DMA((2 + blocks,)),
        ],
        compiler_params=pltpu.CompilerParams(vmem_limit_bytes=JACOBI_VMEM_LIMIT),
        cost_estimate=pl.CostEstimate(
            flops=size, bytes_accessed=size, transcendentals=0
        ),
        name="jacobi_turns",
    )(plan, *grams, matrix)


def gram_spans(rows):
    spans = []
    start = 0
    while start < rows:
        wanted = GRAM_PARTS[len(spans)] if len(spans) < len(GRAM_PARTS) else GRAM_TILE
        spans.append((start, min(wanted, rows - start)))
        start += spans[-1][1]
    return spans


def gram_kernel(matrix_ref, packed_ref, raw_ref, held, upper_ref, corner_ref, sems, raw_sem):
    rows = held.shape[0]
    copies = []
    spans = gram_spans(rows)
    for index, (start, count) in enumerate(spans):
        part = pl.ds(start, count)
        copies.append(pltpu.make_async_copy(matrix_ref.at[part], held.at[part], sems.at[index]))
    for copy in copies[:IN_FLIGHT]:
        copy.start()
    early = pl.ds(0, RAW_ROWS)
    leave = pltpu.make_async_copy(held.at[early], raw_ref, raw_sem)
    for index, copy in enumerate(copies):
        copy.wait()
        if index + IN_FLIGHT < len(copies):
            copies[index + IN_FLIGHT].start()
        start, count = spans[index]
        if start + count == RAW_ROWS:
            leave.start()
        values = held[start : start + count]
        right = values[:, 2 * LANES :]
        upper = dot32(values[:, : 2 * LANES], values, ((0,), (0,)))
        corner = dot32(right, right, ((0,), (0,)))
        if index == 0:
            upper_ref[...] = upper
            corner_ref[...] = corner
        else:
            upper_ref[...] += upper
            corner_ref[...] += corner
    rows_at, cols_at = triangle()
    block11 = upper_ref[LANES:, LANES : 2 * LANES]
    packed_ref[:LANES] = jnp.where(rows_at <= cols_at, upper_ref[:LANES, :LANES], block11)
    packed_ref[LANES : 2 * LANES] = upper_ref[:LANES, LANES : 2 * LANES]
    packed_ref[2 * LANES : 3 * LANES] = upper_ref[:LANES, 2 * LANES :]
    packed_ref[3 * LANES : 4 * LANES] = upper_ref[LANES:, 2 * LANES :]
    packed_ref[4 * LANES : 5 * LANES] = corner_ref[...]
    diag11 = jnp.sum(jnp.where(rows_at == cols_at, block11, 0.0), axis=0, keepdims=True)
    packed_ref[5 * LANES :] = jnp.broadcast_to(diag11, (SUBS, LANES))
    leave.wait()


def gram_blocks(matrix):
    rows, size = matrix.shape
    return pl.pallas_call(
        gram_kernel,
        in_specs=[pl.BlockSpec(memory_space=pl.ANY)],
        out_specs=[pl.BlockSpec(memory_space=pltpu.VMEM), pl.BlockSpec(memory_space=pl.ANY)],
        out_shape=(
            jax.ShapeDtypeStruct((5 * LANES + SUBS, LANES), jnp.float32),
            jax.ShapeDtypeStruct((RAW_ROWS, size), jnp.bfloat16),
        ),
        scratch_shapes=[
            pltpu.VMEM((rows, size), jnp.bfloat16),
            pltpu.VMEM((2 * LANES, size), jnp.float32),
            pltpu.VMEM((LANES, LANES), jnp.float32),
            pltpu.SemaphoreType.DMA((len(gram_spans(rows)),)),
            pltpu.SemaphoreType.DMA,
        ],
        compiler_params=pltpu.CompilerParams(vmem_limit_bytes=VMEM_LIMIT),
        cost_estimate=pl.CostEstimate(
            flops=2 * rows * size * size, bytes_accessed=2 * rows * size, transcendentals=0
        ),
        name="gram_blocks",
    )(matrix)


def place_main(slot, out_ref, rows, slow_main, near_main):
    @pl.when(slot == 0)
    def _():
        out_ref[rows, :LANES] = slow_main
        out_ref[rows, 2 * LANES :] = near_main

    @pl.when(slot != 0)
    def _():
        out_ref[rows, :LANES] = near_main
        out_ref[rows, 2 * LANES :] = slow_main


def slot_lanes(slot, rows):
    lane = lax.broadcasted_iota(jnp.int32, (rows, LANES), 1)
    return (lane // (LANES // 2)) == slot


def near_kernel(near_ref, turn_ref, packed_ref):
    for unit in range(near_ref.shape[0] // UNIT):
        values = near_ref[unit * UNIT : (unit + 1) * UNIT]
        pack_unit(values, turn_ref[...], packed_ref, unit * PACK)


def rotate_near(near, turn):
    rows, size = near.shape
    pack = WIDE_TILE // UNIT * PACK
    return pl.pallas_call(
        near_kernel,
        grid=(rows // WIDE_TILE,),
        in_specs=[
            pl.BlockSpec((WIDE_TILE, size), lambda i: (i, 0)),
            pl.BlockSpec((size, size), lambda i: (0, 0)),
        ],
        out_specs=pl.BlockSpec((pack, LANES), lambda i: (i, 0)),
        out_shape=jax.ShapeDtypeStruct((rows // UNIT * PACK, LANES), jnp.bfloat16),
        compiler_params=pltpu.CompilerParams(vmem_limit_bytes=FILL_VMEM_LIMIT),
        cost_estimate=pl.CostEstimate(flops=size, bytes_accessed=size, transcendentals=0),
        name="rotate_near",
    )(near, turn)


def fill_kernel(plan_ref, near_ref, slow_ref, *refs):
    out_ref = refs[-1]
    half = UNIT // 2
    slot = moves(plan_ref)[3]
    mask = slot_lanes(slot, half)
    middle = slice(LANES, 2 * LANES)
    for unit in range(out_ref.shape[0] // UNIT):
        start, at = unit * UNIT, unit * PACK
        rows = slice(start, start + UNIT)
        main, rest = slice(at, at + UNIT), slice(at + UNIT, at + PACK)
        place_main(slot, out_ref, rows, slow_ref[main], near_ref[main])
        slow = slow_ref[rest].astype(jnp.float32)
        near = near_ref[rest].astype(jnp.float32)
        out_ref[start : start + half, middle] = jnp.where(mask, slow, near).astype(jnp.bfloat16)
        low = pltpu.roll(jnp.where(mask, near, slow), LANES // 2, 1)
        out_ref[start + half : start + UNIT, middle] = low.astype(jnp.bfloat16)


def raw_kernel(plan_ref, near_ref, slow_ref, slow_turn_ref, out_ref):
    size = slow_ref.shape[1]
    half = UNIT // 2
    slot = moves(plan_ref)[3]
    mask = slot_lanes(slot, half)
    middle = slice(LANES, 2 * LANES)
    mixed = slow_turn_ref[size : size + size // 2].astype(jnp.float32)
    side = slot_lanes(slot, size // 2)
    mixed = jnp.concatenate(
        [jnp.where(side, mixed, 0.0), pltpu.roll(jnp.where(side, 0.0, mixed), LANES // 2, 1)], axis=0
    )
    slow_turn = jnp.concatenate([mixed.astype(jnp.bfloat16), slow_turn_ref[:size]], axis=1)
    for unit in range(out_ref.shape[0] // UNIT):
        start, at = unit * UNIT, unit * PACK
        rows = slice(start, start + UNIT)
        slow = dot32(slow_ref[rows], slow_turn)
        slow_main = slow[:, LANES:].astype(jnp.bfloat16)
        place_main(slot, out_ref, rows, slow_main, near_ref[at : at + UNIT])
        near = near_ref[at + UNIT : at + PACK].astype(jnp.float32)
        top = jnp.where(mask, slow[:half, :LANES], near)
        low = jnp.where(mask, slow[half:, :LANES], pltpu.roll(near, LANES // 2, 1))
        out_ref[start : start + half, middle] = top.astype(jnp.bfloat16)
        out_ref[start + half : start + UNIT, middle] = low.astype(jnp.bfloat16)


def fill_rows(kernel, plan, sources, specs, near_pack, result, shape, start, count, tile):
    first = start // tile
    operands = [plan, near_pack, *sources]
    in_specs = [
        pl.BlockSpec(memory_space=pltpu.SMEM),
        pl.BlockSpec((tile // UNIT * PACK, LANES), lambda i: (first + i, 0)),
        *specs,
    ]
    aliases = {}
    if result is not None:
        aliases = {len(operands): 0}
        operands.append(result)
        in_specs.append(pl.BlockSpec(memory_space=pl.ANY))
    return pl.pallas_call(
        kernel,
        grid=(count // tile,),
        in_specs=in_specs,
        out_specs=pl.BlockSpec((tile, shape[1]), lambda i: (first + i, 0)),
        out_shape=jax.ShapeDtypeStruct(shape, jnp.bfloat16),
        input_output_aliases=aliases,
        compiler_params=pltpu.CompilerParams(vmem_limit_bytes=FILL_VMEM_LIMIT),
        cost_estimate=pl.CostEstimate(
            flops=count * shape[1], bytes_accessed=4 * count * shape[1], transcendentals=0
        ),
        name="fill_rows",
    )(*operands)


def swapped_with(value, axis, partner):
    count = lax.axis_size(axis)
    return lax.ppermute(value, axis, [(source, partner(source, count)) for source in range(count)])


def slow_partner(source, count):
    return (source + 1) % count if source % 2 else (source + count - 1) % count


def fast_partner(source, count):
    return source ^ 1


def permuted(value, pairs):
    return lax.ppermute(value, "blk", pairs)


def joined(pieces):
    values = pieces.astype(jnp.float32)
    row = lax.broadcasted_iota(jnp.int32, (SUBS, LANES), 0)
    off = values[0:1] + values[1:2] + values[2:3]
    diag = values[3:4] + values[4:5] + values[5:6]
    return jnp.where(row == 0, off, diag)


def add_pairs(left, right):
    total = left[0] + right[0]
    moved = total - left[0]
    lost = (left[0] - (total - moved)) + (right[0] - moved)
    small = left[1] + right[1] + lost
    high = total + small
    return high, small - (high - total)


def cycle_sums(mine, theirs):
    count = lax.axis_size("blk")
    zero = jnp.zeros((SUBS, LANES), jnp.float32)
    sums = add_pairs((joined(mine), zero), (joined(theirs), zero))
    step = 1
    while step < count:
        if step != 2:
            pairs = [(place, place ^ step) for place in range(count)]
            moved = permuted(jnp.concatenate(sums, axis=0), pairs)
            sums = add_pairs(sums, (moved[:SUBS], moved[SUBS:]))
        step *= 2
    return sums[0]


def on_device(matrix, plan):
    rows, size = matrix.shape
    own, early = gram_blocks(matrix)
    matrix_after, own = lax.optimization_barrier((matrix, own))
    if lax.axis_size("rows") == 2:
        grams = [own, swapped_with(own, "rows", fast_partner)]
    else:
        grams = [lax.psum(own, "rows")]
    raw = swapped_with(early, "blk", slow_partner)
    near = swapped_with(matrix_after, "blk", fast_partner)
    head, first, last, near_turn, sums = jacobi(plan, grams, matrix)

    head = swapped_with(head, "blk", slow_partner)
    first = swapped_with(first, "blk", slow_partner)
    last = swapped_with(last, "blk", slow_partner)
    near_turn = swapped_with(near_turn, "blk", fast_partner)
    near_pack = rotate_near(near, near_turn)
    theirs = head[size + size // 2 :]
    theirs, near_pack, raw = lax.optimization_barrier((theirs, near_pack, raw))
    totals = cycle_sums(sums, theirs)
    off_ratio = jnp.sqrt(totals[0, 0] / totals[1, 0])

    shape = (rows, size)
    turn_spec = pl.BlockSpec(head.shape, lambda i: (0, 0))
    raw_spec = pl.BlockSpec((UNIT, size), lambda i: (i, 0))
    wide_spec = pl.BlockSpec((WIDE_TILE // UNIT * PACK, LANES), lambda i: (i, 0))
    last_spec = pl.BlockSpec((PACK, LANES), lambda i: (i, 0))
    middle = rows - RAW_ROWS - LAST_ROWS
    result = fill_rows(
        raw_kernel, plan, [raw, head], [raw_spec, turn_spec], near_pack, None, shape,
        0, RAW_ROWS, UNIT,
    )
    result = fill_rows(
        fill_kernel, plan, [first], [wide_spec], near_pack, result, shape,
        RAW_ROWS, middle, WIDE_TILE,
    )
    result, off_ratio = lax.optimization_barrier((result, off_ratio))
    result = fill_rows(
        fill_kernel, plan, [last], [last_spec], near_pack, result, shape,
        rows - LAST_ROWS, LAST_ROWS, UNIT,
    )
    return result, off_ratio


def solution(mesh):
    in_specs = (P("rows", "blk"), P())
    out_specs = (P("rows", "blk"), P())
    return jax.shard_map(
        on_device, mesh=mesh, in_specs=in_specs, out_specs=out_specs, check_vma=False
    )
```

```python
import jax
import jax.numpy as jnp
from jax import lax
from jax.experimental import pallas as pl
from jax.experimental.pallas import tpu as pltpu
from jax.sharding import PartitionSpec as P

ROUNDS = 24
LANES = 128
SUBS = 8
UNIT = 512
PACK = UNIT + UNIT // 2
GRAM_PARTS = (512, 1024)
GRAM_TILE = 1536
RAW_ROWS = 1536
LAST_ROWS = 1536
WIDE_TILE = 1536
SUM_ROWS = 16
IN_FLIGHT = 2
VMEM_LIMIT = 60 * 1024 * 1024
JACOBI_VMEM_LIMIT = 58 * 1024 * 1024
FILL_VMEM_LIMIT = 32 * 1024 * 1024


def split_three(values):
    high = values.astype(jnp.bfloat16)
    rest = values - high.astype(jnp.float32)
    middle = rest.astype(jnp.bfloat16)
    low = (rest - middle.astype(jnp.float32)).astype(jnp.bfloat16)
    return high, middle, low


def dot32(left, right, dims=((1,), (0,))):
    return lax.dot_general(left, right, (dims, ((), ())), preferred_element_type=jnp.float32)


def slot_of_row(rows, groups, half):
    part = rows // half
    inside = rows % half
    index = (inside % SUBS) * groups + inside // SUBS
    return jnp.where(part == 0, index, 2 * half - 1 - index)


def slot_of_lane(lanes, half):
    part = lanes // (2 * LANES)
    odd = (lanes // LANES) % 2
    inside = lanes % LANES
    index = 2 * inside + odd
    slot = jnp.where(part == 0, index, 2 * half - 1 - index)
    return jnp.where(inside < half // 2, slot, -1)


def onehot(left, right):
    return jnp.where(left == right, 1.0, 0.0).astype(jnp.bfloat16)


def angles(head, tail, coupling):
    difference = head - tail
    sign_val = jnp.where(difference >= 0.0, 1.0, -1.0)
    across = 2.0 * coupling * sign_val
    along = jnp.abs(difference)
    scale = jnp.maximum(along, jnp.abs(across))
    empty = scale == 0.0
    inverse = 1.0 / jnp.where(empty, 1.0, scale)
    along = jnp.where(empty, 1.0, along * inverse)
    across = across * inverse
    square = along * along + across * across
    root = lax.rsqrt(square)
    root = root * (1.5 - 0.5 * square * root * root)
    cos_sq = 0.5 + 0.5 * (along * root)
    half_root = lax.rsqrt(cos_sq)
    half_root = half_root * (1.5 - 0.5 * cos_sq * half_root * half_root)
    return cos_sq * half_root, 0.5 * (across * root) * half_root


def triangle():
    rows = lax.broadcasted_iota(jnp.int32, (LANES, LANES), 0)
    cols = lax.broadcasted_iota(jnp.int32, (LANES, LANES), 1)
    return rows, cols


def full_gram(packed):
    shared, block01, block20, block21, block22 = (
        packed[index * LANES : (index + 1) * LANES] for index in range(5)
    )
    diag11 = packed[5 * LANES : 5 * LANES + 1]
    rows, cols = triangle()
    flipped = shared.T
    block00 = jnp.where(rows <= cols, shared, flipped)
    block11 = jnp.where(rows > cols, shared, jnp.where(rows < cols, flipped, diag11))
    first = jnp.concatenate([block00, block01, block20.T], axis=1)
    second = jnp.concatenate([block01.T, block11, block21.T], axis=1)
    third = jnp.concatenate([block20, block21, block22], axis=1)
    return jnp.concatenate([first, second, third], axis=0)


def send_columns(lanes, base, slot, width):
    section = lanes // LANES
    lane = lanes % LANES
    rest = width - LANES
    main_start = base + jnp.where(slot == 0, 0, rest)
    rest_start = base + jnp.where(slot == 0, LANES, 0)
    high = (section // 2 + slot) % 2
    inside = lane - high * (LANES - rest)
    mixed = jnp.where((inside >= 0) & (inside < rest), rest_start + inside, -1)
    return jnp.where(section == 1, main_start + lane, mixed)


def block_sums(gram_sum):
    squares = gram_sum * gram_sum
    rows = lax.broadcasted_iota(jnp.int32, squares.shape, 0)
    cols = lax.broadcasted_iota(jnp.int32, squares.shape, 1)
    total = jnp.sum(squares, keepdims=True)
    diag_sq = jnp.sum(jnp.where(rows == cols, squares, 0.0), keepdims=True)
    row = lax.broadcasted_iota(jnp.int32, (SUM_ROWS, LANES), 0)
    pieces = jnp.zeros((SUM_ROWS, LANES), jnp.float32)
    for index, piece in enumerate(split_three(total - diag_sq) + split_three(diag_sq)):
        pieces = jnp.where(row == index, piece.astype(jnp.float32), pieces)
    return pieces.astype(jnp.bfloat16)


def pack_unit(values, turn, packed_ref, at):
    half = UNIT // 2
    top = dot32(values[:half], turn[:, : 2 * LANES])
    low = dot32(values[half:], turn[:, LANES:])
    packed_ref[at : at + half] = top[:, LANES:].astype(jnp.bfloat16)
    packed_ref[at + half : at + UNIT] = low[:, :LANES].astype(jnp.bfloat16)
    packed_ref[at + UNIT : at + PACK] = (top[:, :LANES] + low[:, LANES:]).astype(jnp.bfloat16)


def moves(plan_ref):
    count = plan_ref.shape[0] // 2
    position = lax.axis_index("blk")
    slow_dev = lax.rem(position + 2 * lax.rem(position, 2) - 1 + count, count)
    mine = plan_ref[2 * position], plan_ref[2 * position + 1]
    theirs = plan_ref[2 * slow_dev], plan_ref[2 * slow_dev + 1]
    first_slow = mine[0] // 2 == slow_dev
    slow_slot = lax.rem(jnp.where(first_slow, mine[0], mine[1]), 2)
    fast_slot = lax.rem(jnp.where(first_slow, mine[1], mine[0]), 2)
    in_slot = lax.rem(jnp.where(theirs[0] // 2 == position, theirs[0], theirs[1]), 2)
    return first_slow, slow_slot, fast_slot, in_slot


def jacobi_kernel(plan_ref, *refs):
    jacobi_body(plan_ref, refs[:-15], *refs[-15:])


def jacobi_body(
    plan_ref, gram_refs, matrix_ref, head_ref, first_ref, last_ref, fast_ref, sums_ref,
    gram_a, gram_b, basis_a, basis_b, cos_buf, sin_buf, held, packs, sems,
):
    matrix_copy = pltpu.make_async_copy(matrix_ref.at[pl.ds(RAW_ROWS, held.shape[0])], held, sems.at[0])
    size = matrix_ref.shape[1]
    half = size // 2
    groups = half // SUBS
    last = groups - 1
    edge = half // 2 - 1
    lane_row = lax.broadcasted_iota(jnp.int32, (1, LANES), 1)
    lane = lax.broadcasted_iota(jnp.int32, (SUBS, LANES), 1)
    sub = lax.broadcasted_iota(jnp.int32, (SUBS, LANES), 0)
    spot = lane - sub * (groups // 2)

    def on_diag(group):
        return spot == group // 2

    row_slot = slot_of_row(lax.broadcasted_iota(jnp.int32, (size, 1), 0), groups, half)
    take_rows = onehot(row_slot, lax.broadcasted_iota(jnp.int32, (size, size), 1))
    lane_slot = slot_of_lane(lax.broadcasted_iota(jnp.int32, (1, 4 * LANES), 1), half)
    take_cols = onehot(lax.broadcasted_iota(jnp.int32, (size, 4 * LANES), 0), lane_slot)
    arranged = jnp.zeros((size, 4 * LANES), jnp.float32)
    matrix_copy.start()
    packed = gram_refs[0][...]
    for other in gram_refs[1:]:
        packed = packed + other[...]
    gram_sum = full_gram(packed)
    sums_ref[...] = block_sums(gram_sum)
    for piece in split_three(gram_sum):
        moved = dot32(take_rows, piece).astype(jnp.bfloat16)
        arranged = arranged + dot32(moved, take_cols)
    gram_a[...] = arranged.reshape(2, groups, SUBS, 4 * LANES)
    basis_a[...] = take_rows.astype(jnp.float32).reshape(2, groups, SUBS, size)

    zero = jnp.zeros((SUBS, LANES), jnp.float32)
    heads, tails, couplings = [zero, zero], [zero, zero], [zero, zero]
    for group in range(groups):
        odd = group % 2
        mask = on_diag(group)
        lead_cols = slice(odd * LANES, (odd + 1) * LANES)
        tail_cols = slice((2 + odd) * LANES, (3 + odd) * LANES)
        heads[odd] += jnp.where(mask, gram_a[0, group, :, lead_cols], 0.0)
        tails[odd] += jnp.where(mask, gram_a[1, group, :, tail_cols], 0.0)
        couplings[odd] += jnp.where(mask, gram_a[0, group, :, tail_cols], 0.0)

    def flat(values):
        return jnp.sum(values, axis=0, keepdims=True)

    def shift_lanes(lead, tail):
        lead0, lead1 = lead[:, :LANES], lead[:, LANES:]
        tail0, tail1 = tail[:, :LANES], tail[:, LANES:]
        here = lane[: lead.shape[0]]
        new_lead1 = jnp.where(here == 0, tail0, lead0)
        new_lead0 = jnp.where(here == 0, lead0, pltpu.roll(lead1, 1, 1))
        new_tail1 = jnp.where(here == edge, lead1, pltpu.roll(tail0, LANES - 1, 1))
        return new_lead0, new_lead1, tail1, new_tail1

    def turn(gram_from, gram_to, basis_from, basis_to, carry):
        heads, tails, couplings = carry
        cosines, sines, new_heads, new_tails = [], [], [], []
        for odd in range(2):
            head, tail = heads[odd], tails[odd]
            coupling = flat(couplings[odd])
            cosine, sine_val = angles(head, tail, coupling)
            cosines.append(cosine)
            sines.append(sine_val)
            first = cosine * head + sine_val * coupling
            second = cosine * coupling + sine_val * tail
            new_heads.append(cosine * first + sine_val * second)
            first = cosine * coupling - sine_val * head
            second = cosine * tail - sine_val * coupling
            new_tails.append(cosine * second - sine_val * first)
        shifted_diag = shift_lanes(
            jnp.concatenate([jnp.broadcast_to(x, (SUBS, LANES)) for x in new_heads], axis=1),
            jnp.concatenate([jnp.broadcast_to(x, (SUBS, LANES)) for x in new_tails], axis=1),
        )
        shifted_diag = [x[:1] for x in shifted_diag]
        cos_lanes = [jnp.broadcast_to(x, (SUBS, LANES)) for x in cosines]
        sin_lanes = [jnp.broadcast_to(x, (SUBS, LANES)) for x in sines]
        cos_wide = jnp.concatenate(cos_lanes, axis=1)
        sin_wide = jnp.concatenate(sin_lanes, axis=1)

        for group in range(groups):
            mask = on_diag(group)
            odd = group % 2
            for buf, lanes in ((cos_buf, cos_lanes[odd]), (sin_buf, sin_lanes[odd])):
                picked = jnp.sum(jnp.where(mask, lanes, 0.0), axis=1, keepdims=True)
                buf[group] = jnp.broadcast_to(picked, (SUBS, LANES))

        def work(group):
            cos_row = jnp.concatenate([cos_buf[group]] * 2, axis=1)
            sin_row = jnp.concatenate([sin_buf[group]] * 2, axis=1)
            cos_base = jnp.concatenate([cos_buf[group]] * (size // LANES), axis=1)
            sin_base = jnp.concatenate([sin_buf[group]] * (size // LANES), axis=1)

            def turned(part):
                values = gram_from[part, group]
                lead, tail = values[:, : 2 * LANES], values[:, 2 * LANES :]
                return cos_wide * lead + sin_wide * tail, cos_wide * tail - sin_wide * lead

            top_lead, top_tail = turned(0)
            low_lead, low_tail = turned(1)
            top = shift_lanes(
                cos_row * top_lead + sin_row * low_lead, cos_row * top_tail + sin_row * low_tail
            )
            low = shift_lanes(
                cos_row * low_lead - sin_row * top_lead, cos_row * low_tail - sin_row * top_tail
            )
            lead = basis_from[0, group]
            tail = basis_from[1, group]
            base_top = cos_base * lead + sin_base * tail
            base_low = cos_base * tail - sin_base * lead
            return (
                list(top) + [base_top[:, i : i + LANES] for i in range(0, size, LANES)],
                list(low) + [base_low[:, i : i + LANES] for i in range(0, size, LANES)],
            )

        sums = [zero, zero]

        def store(part, group, values):
            for index, value in enumerate(values[:4]):
                gram_to[part, group, :, index * LANES : (index + 1) * LANES] = value
            for index, value in enumerate(values[4:]):
                basis_to[part, group, :, index * LANES : (index + 1) * LANES] = value
            if part == 0:
                odd = group % 2
                sums[odd] += jnp.where(on_diag(group), values[2 + odd], 0.0)

        first_top, first_low = work(0)
        last_top, last_low = work(last)
        store(0, 1, [jnp.where(sub == 0, y, x) for x, y in zip(first_top, first_low)])
        store(0, 0, [jnp.where(sub == 0, x, pltpu.roll(y, 1, 0)) for x, y in zip(first_top, last_top)])
        store(1, last, [
            jnp.where(sub == SUBS - 1, y, pltpu.roll(x, SUBS - 1, 0))
            for x, y in zip(first_low, last_top)
        ])
        store(1, last - 1, last_low)
        for group in range(1, last):
            top, low = work(group)
            store(0, group + 1, top)
            store(1, group - 1, low)
        return (
            (shifted_diag[0], shifted_diag[1]), (shifted_diag[2], shifted_diag[3]), tuple(sums)
        )

    start = (
        tuple(flat(x) for x in heads), tuple(flat(x) for x in tails), tuple(couplings)
    )

    def two_turns(_, carry):
        carry = turn(gram_a, gram_b, basis_a, basis_b, carry)
        return turn(gram_b, gram_a, basis_b, basis_a, carry)

    lax.fori_loop(0, ROUNDS // 2, two_turns, start)

    held_slot = jnp.where(row_slot == 0, 0, 1 + (row_slot + (size - 2 - ROUNDS % (size - 1))) % (size - 1))
    basis = basis_a[...].reshape(size, size).astype(jnp.bfloat16)
    lanes = lax.broadcasted_iota(jnp.int32, (1, size), 1)
    first_slow, slow_slot, fast_slot, _ = moves(plan_ref)
    slow_base = jnp.where(first_slow, 0, half)
    def turned(base, slot):
        place = onehot(held_slot, send_columns(lanes, base, slot, half))
        return dot32(basis, place, ((0,), (0,))).astype(jnp.bfloat16)

    fast_ref[...] = turned(half - slow_base, fast_slot)
    slow = turned(slow_base, slow_slot)
    head_rows = size + half
    packs[:size] = slow[:, LANES : 2 * LANES]
    packs[size:head_rows] = slow[:half, :LANES] + slow[half:, 2 * LANES :]
    matrix_copy.wait()
    copies = []

    def leave(start, count, ref):
        copies.append(
            pltpu.make_async_copy(packs.at[pl.ds(start, count)], ref, sems.at[1 + len(copies)])
        )
        copies[-1].start()

    leave(0, head_rows, head_ref.at[pl.ds(0, head_rows)])
    tail = head_ref.at[pl.ds(head_rows, SUM_ROWS)]
    copies.append(pltpu.make_async_copy(sums_ref, tail, sems.at[2]))
    copies[-1].start()
    first_count = first_ref.shape[0]
    for unit in range(held.shape[0] // UNIT):
        at = (1 + unit) * PACK
        pack_unit(held[unit * UNIT : (unit + 1) * UNIT], slow, packs, at)
        place = unit * PACK
        if place < first_count:
            leave(at, PACK, first_ref.at[pl.ds(place, PACK)])
        else:
            leave(at, PACK, last_ref.at[pl.ds(place - first_count, PACK)])
    for copy in copies:
        copy.wait()


def jacobi(plan, grams, matrix):
    rows, size = matrix.shape
    groups = size // 2 // SUBS
    moved = rows - RAW_ROWS
    blocks = 1 + moved // UNIT
    last = LAST_ROWS // UNIT * PACK
    return pl.pallas_call(
        jacobi_kernel,
        out_shape=(
            jax.ShapeDtypeStruct((size + size // 2 + SUM_ROWS, LANES), jnp.bfloat16),
            jax.ShapeDtypeStruct(((blocks - 1) * PACK - last, LANES), jnp.bfloat16),
            jax.ShapeDtypeStruct((last, LANES), jnp.bfloat16),
            jax.ShapeDtypeStruct((size, size), jnp.bfloat16),
            jax.ShapeDtypeStruct((SUM_ROWS, LANES), jnp.bfloat16),
        ),
        in_specs=[pl.BlockSpec(memory_space=pltpu.SMEM)]
        + [pl.BlockSpec(memory_space=pltpu.VMEM)] * len(grams)
        + [pl.BlockSpec(memory_space=pl.ANY)],
        out_specs=[pl.BlockSpec(memory_space=pl.ANY)] * 3
        + [pl.BlockSpec(memory_space=pltpu.VMEM)] * 2,
        scratch_shapes=[
            pltpu.VMEM((2, groups, SUBS, 4 * LANES), jnp.float32),
            pltpu.VMEM((2, groups, SUBS, 4 * LANES), jnp.float32),
            pltpu.VMEM((2, groups, SUBS, size), jnp.float32),
            pltpu.VMEM((2, groups, SUBS, size), jnp.float32),
            pltpu.VMEM((groups, SUBS, LANES), jnp.float32),
            pltpu.VMEM((groups, SUBS, LANES), jnp.float32),
            pltpu.VMEM((moved, size), jnp.bfloat16),
            pltpu.VMEM((blocks * PACK, LANES), jnp.bfloat16),
            pltpu.SemaphoreType.DMA((2 + blocks,)),
        ],
        compiler_params=pltpu.CompilerParams(vmem_limit_bytes=JACOBI_VMEM_LIMIT),
        cost_estimate=pl.CostEstimate(
            flops=size, bytes_accessed=size, transcendentals=0
        ),
        name="jacobi_turns",
    )(plan, *grams, matrix)


def gram_spans(rows):
    spans = []
    start = 0
    while start < rows:
        wanted = GRAM_PARTS[len(spans)] if len(spans) < len(GRAM_PARTS) else GRAM_TILE
        spans.append((start, min(wanted, rows - start)))
        start += spans[-1][1]
    return spans


def gram_kernel(matrix_ref, packed_ref, raw_ref, held, upper_ref, corner_ref, sems, raw_sem):
    rows = held.shape[0]
    copies = []
    spans = gram_spans(rows)
    for index, (start, count) in enumerate(spans):
        part = pl.ds(start, count)
        copies.append(pltpu.make_async_copy(matrix_ref.at[part], held.at[part], sems.at[index]))
    for copy in copies[:IN_FLIGHT]:
        copy.start()
    early = pl.ds(0, RAW_ROWS)
    leave = pltpu.make_async_copy(held.at[early], raw_ref, raw_sem)
    for index, copy in enumerate(copies):
        copy.wait()
        if index + IN_FLIGHT < len(copies):
            copies[index + IN_FLIGHT].start()
        start, count = spans[index]
        if start + count == RAW_ROWS:
            leave.start()
        values = held[start : start + count]
        right = values[:, 2 * LANES :]
        upper = dot32(values, values[:, : 2 * LANES], ((0,), (0,)))
        corner = dot32(right, right, ((0,), (0,)))
        if index == 0:
            upper_ref[...] = upper
            corner_ref[...] = corner
        else:
            upper_ref[...] += upper
            corner_ref[...] += corner
    rows_at, cols_at = triangle()
    block11 = upper_ref[LANES : 2 * LANES, LANES:]
    packed_ref[:LANES] = jnp.where(rows_at <= cols_at, upper_ref[:LANES, :LANES], block11)
    packed_ref[LANES : 2 * LANES] = upper_ref[:LANES, LANES:]
    packed_ref[2 * LANES : 3 * LANES] = upper_ref[2 * LANES :, :LANES]
    packed_ref[3 * LANES : 4 * LANES] = upper_ref[2 * LANES :, LANES:]
    packed_ref[4 * LANES : 5 * LANES] = corner_ref[...]
    diag11 = jnp.sum(jnp.where(rows_at == cols_at, block11, 0.0), axis=0, keepdims=True)
    packed_ref[5 * LANES :] = jnp.broadcast_to(diag11, (SUBS, LANES))
    leave.wait()


def gram_blocks(matrix):
    rows, size = matrix.shape
    return pl.pallas_call(
        gram_kernel,
        in_specs=[pl.BlockSpec(memory_space=pl.ANY)],
        out_specs=[pl.BlockSpec(memory_space=pltpu.VMEM), pl.BlockSpec(memory_space=pl.ANY)],
        out_shape=(
            jax.ShapeDtypeStruct((5 * LANES + SUBS, LANES), jnp.float32),
            jax.ShapeDtypeStruct((RAW_ROWS, size), jnp.bfloat16),
        ),
        scratch_shapes=[
            pltpu.VMEM((rows, size), jnp.bfloat16),
            pltpu.VMEM((size, 2 * LANES), jnp.float32),
            pltpu.VMEM((LANES, LANES), jnp.float32),
            pltpu.SemaphoreType.DMA((len(gram_spans(rows)),)),
            pltpu.SemaphoreType.DMA,
        ],
        compiler_params=pltpu.CompilerParams(vmem_limit_bytes=VMEM_LIMIT),
        cost_estimate=pl.CostEstimate(
            flops=2 * rows * size * size, bytes_accessed=2 * rows * size, transcendentals=0
        ),
        name="gram_blocks",
    )(matrix)


def place_main(slot, out_ref, rows, slow_main, near_main):
    @pl.when(slot == 0)
    def _():
        out_ref[rows, :LANES] = slow_main
        out_ref[rows, 2 * LANES :] = near_main

    @pl.when(slot != 0)
    def _():
        out_ref[rows, :LANES] = near_main
        out_ref[rows, 2 * LANES :] = slow_main


def slot_lanes(slot, rows):
    lane = lax.broadcasted_iota(jnp.int32, (rows, LANES), 1)
    return (lane // (LANES // 2)) == slot


def near_kernel(near_ref, turn_ref, packed_ref):
    for unit in range(near_ref.shape[0] // UNIT):
        values = near_ref[unit * UNIT : (unit + 1) * UNIT]
        pack_unit(values, turn_ref[...], packed_ref, unit * PACK)


def rotate_near(near, turn):
    rows, size = near.shape
    pack = WIDE_TILE // UNIT * PACK
    return pl.pallas_call(
        near_kernel,
        grid=(rows // WIDE_TILE,),
        in_specs=[
            pl.BlockSpec((WIDE_TILE, size), lambda i: (i, 0)),
            pl.BlockSpec((size, size), lambda i: (0, 0)),
        ],
        out_specs=pl.BlockSpec((pack, LANES), lambda i: (i, 0)),
        out_shape=jax.ShapeDtypeStruct((rows // UNIT * PACK, LANES), jnp.bfloat16),
        compiler_params=pltpu.CompilerParams(vmem_limit_bytes=FILL_VMEM_LIMIT),
        cost_estimate=pl.CostEstimate(flops=size, bytes_accessed=size, transcendentals=0),
        name="rotate_near",
    )(near, turn)


def fill_kernel(plan_ref, near_ref, slow_ref, *refs):
    out_ref = refs[-1]
    half = UNIT // 2
    slot = moves(plan_ref)[3]
    mask = slot_lanes(slot, half)
    middle = slice(LANES, 2 * LANES)
    for unit in range(out_ref.shape[0] // UNIT):
        start, at = unit * UNIT, unit * PACK
        rows = slice(start, start + UNIT)
        main, rest = slice(at, at + UNIT), slice(at + UNIT, at + PACK)
        place_main(slot, out_ref, rows, slow_ref[main], near_ref[main])
        slow = slow_ref[rest].astype(jnp.float32)
        near = near_ref[rest].astype(jnp.float32)
        out_ref[start : start + half, middle] = jnp.where(mask, slow, near).astype(jnp.bfloat16)
        low = pltpu.roll(jnp.where(mask, near, slow), LANES // 2, 1)
        out_ref[start + half : start + UNIT, middle] = low.astype(jnp.bfloat16)


def raw_kernel(plan_ref, near_ref, slow_ref, slow_turn_ref, out_ref):
    size = slow_ref.shape[1]
    half = UNIT // 2
    slot = moves(plan_ref)[3]
    mask = slot_lanes(slot, half)
    middle = slice(LANES, 2 * LANES)
    mixed = slow_turn_ref[size : size + size // 2].astype(jnp.float32)
    side = slot_lanes(slot, size // 2)
    mixed = jnp.concatenate(
        [jnp.where(side, mixed, 0.0), pltpu.roll(jnp.where(side, 0.0, mixed), LANES // 2, 1)], axis=0
    )
    slow_turn = jnp.concatenate([mixed.astype(jnp.bfloat16), slow_turn_ref[:size]], axis=1)
    for unit in range(out_ref.shape[0] // UNIT):
        start, at = unit * UNIT, unit * PACK
        rows = slice(start, start + UNIT)
        slow = dot32(slow_ref[rows], slow_turn)
        slow_main = slow[:, LANES:].astype(jnp.bfloat16)
        place_main(slot, out_ref, rows, slow_main, near_ref[at : at + UNIT])
        near = near_ref[at + UNIT : at + PACK].astype(jnp.float32)
        top = jnp.where(mask, slow[:half, :LANES], near)
        low = jnp.where(mask, slow[half:, :LANES], pltpu.roll(near, LANES // 2, 1))
        out_ref[start : start + half, middle] = top.astype(jnp.bfloat16)
        out_ref[start + half : start + UNIT, middle] = low.astype(jnp.bfloat16)


def fill_rows(kernel, plan, sources, specs, near_pack, result, shape, start, count, tile):
    first = start // tile
    operands = [plan, near_pack, *sources]
    in_specs = [
        pl.BlockSpec(memory_space=pltpu.SMEM),
        pl.BlockSpec((tile // UNIT * PACK, LANES), lambda i: (first + i, 0)),
        *specs,
    ]
    aliases = {}
    if result is not None:
        aliases = {len(operands): 0}
        operands.append(result)
        in_specs.append(pl.BlockSpec(memory_space=pl.ANY))
    return pl.pallas_call(
        kernel,
        grid=(count // tile,),
        in_specs=in_specs,
        out_specs=pl.BlockSpec((tile, shape[1]), lambda i: (first + i, 0)),
        out_shape=jax.ShapeDtypeStruct(shape, jnp.bfloat16),
        input_output_aliases=aliases,
        compiler_params=pltpu.CompilerParams(vmem_limit_bytes=FILL_VMEM_LIMIT),
        cost_estimate=pl.CostEstimate(
            flops=count * shape[1], bytes_accessed=4 * count * shape[1], transcendentals=0
        ),
        name="fill_rows",
    )(*operands)


def swapped_with(value, axis, partner):
    count = lax.axis_size(axis)
    return lax.ppermute(value, axis, [(source, partner(source, count)) for source in range(count)])


def slow_partner(source, count):
    return (source + 1) % count if source % 2 else (source + count - 1) % count


def fast_partner(source, count):
    return source ^ 1


def permuted(value, pairs):
    return lax.ppermute(value, "blk", pairs)


def joined(pieces):
    values = pieces.astype(jnp.float32)
    row = lax.broadcasted_iota(jnp.int32, (SUBS, LANES), 0)
    off = values[0:1] + values[1:2] + values[2:3]
    diag = values[3:4] + values[4:5] + values[5:6]
    return jnp.where(row == 0, off, diag)


def add_pairs(left, right):
    total = left[0] + right[0]
    moved = total - left[0]
    lost = (left[0] - (total - moved)) + (right[0] - moved)
    small = left[1] + right[1] + lost
    high = total + small
    return high, small - (high - total)


def cycle_sums(mine, theirs):
    count = lax.axis_size("blk")
    zero = jnp.zeros((SUBS, LANES), jnp.float32)
    sums = add_pairs((joined(mine), zero), (joined(theirs), zero))
    step = 1
    while step < count:
        if step != 2:
            pairs = [(place, place ^ step) for place in range(count)]
            moved = permuted(jnp.concatenate(sums, axis=0), pairs)
            sums = add_pairs(sums, (moved[:SUBS], moved[SUBS:]))
        step *= 2
    return sums[0]


def on_device(matrix, plan):
    rows, size = matrix.shape
    own, early = gram_blocks(matrix)
    matrix_after, own = lax.optimization_barrier((matrix, own))
    if lax.axis_size("rows") == 2:
        grams = [own, swapped_with(own, "rows", fast_partner)]
    else:
        grams = [lax.psum(own, "rows")]
    raw = swapped_with(early, "blk", slow_partner)
    near = swapped_with(matrix_after, "blk", fast_partner)
    head, first, last, near_turn, sums = jacobi(plan, grams, matrix)

    head = swapped_with(head, "blk", slow_partner)
    first = swapped_with(first, "blk", slow_partner)
    last = swapped_with(last, "blk", slow_partner)
    near_turn = swapped_with(near_turn, "blk", fast_partner)
    near_pack = rotate_near(near, near_turn)
    theirs = head[size + size // 2 :]
    theirs, near_pack, raw = lax.optimization_barrier((theirs, near_pack, raw))
    totals = cycle_sums(sums, theirs)
    off_ratio = jnp.sqrt(totals[0, 0] / totals[1, 0])

    shape = (rows, size)
    turn_spec = pl.BlockSpec(head.shape, lambda i: (0, 0))
    raw_spec = pl.BlockSpec((UNIT, size), lambda i: (i, 0))
    wide_spec = pl.BlockSpec((WIDE_TILE // UNIT * PACK, LANES), lambda i: (i, 0))
    last_spec = pl.BlockSpec((PACK, LANES), lambda i: (i, 0))
    middle = rows - RAW_ROWS - LAST_ROWS
    result = fill_rows(
        raw_kernel, plan, [raw, head], [raw_spec, turn_spec], near_pack, None, shape,
        0, RAW_ROWS, UNIT,
    )
    result = fill_rows(
        fill_kernel, plan, [first], [wide_spec], near_pack, result, shape,
        RAW_ROWS, middle, WIDE_TILE,
    )
    result, off_ratio = lax.optimization_barrier((result, off_ratio))
    result = fill_rows(
        fill_kernel, plan, [last], [last_spec], near_pack, result, shape,
        rows - LAST_ROWS, LAST_ROWS, UNIT,
    )
    return result, off_ratio


def solution(mesh):
    in_specs = (P("rows", "blk"), P())
    out_specs = (P("rows", "blk"), P())
    return jax.shard_map(
        on_device, mesh=mesh, in_specs=in_specs, out_specs=out_specs, check_vma=False
    )
```
